32 devices in a mesh: section: 2 (over y), dp: 16 (over z, x, core).
Axes of the slice: x: 2, y: 2, z: 4, core: 2. Of those that a mesh axis runs over, the one named last changes fastest.
Arguments:
- tokens_in: bfloat16 [16384, 512], P('dp'), may hold values from -6 to 6
- out_cot: bfloat16 [16384, 512], P('dp'), may hold values from -6 to 6
- term_cot: float32 [16384], P('dp'), may hold values from -6 to 6
- long_flag: int32 [32], P('dp'), may hold values from 0 to 1, as said below
- token_mask: int32 [16384], P('dp'), may hold values from 0 to 1, as said below
- w_qkv: bfloat16 [2, 512, 1536], P('section', 'dp'), may hold values from -0.25 to 0.25
- w_out: bfloat16 [2, 512, 512], P('section', 'dp'), may hold values from -2 to 2
- w_ff_in: bfloat16 [2, 512, 2048], P('section', 'dp'), may hold values from -0.25 to 0.25
- w_ff_out: bfloat16 [2, 2048, 512], P('section', 'dp'), may hold values from -0.125 to 0.125
- vectors: bfloat16 [2, 8, 512], P('section', None, 'dp'), may hold values from -1.4 to 1.4
- ff_bias: bfloat16 [2, 2048], P('section', 'dp'), may hold values from -1.5 to 1.5
- head_weight: bfloat16 [512], replicated, may hold values from -0.25 to 0.25
- head_bias: float32 [1], replicated, may hold values from -2 to 2
Outputs:
- activations: bfloat16 [2, 16384, 512], P('section', 'dp')
- term_weights: bfloat16 [16384], P('dp')
- input_grads: bfloat16 [2, 16384, 512], P('section', 'dp')
- grad_qkv: float32 [2, 512, 1536], P('section', 'dp')
- grad_out: float32 [2, 512, 512], P('section', 'dp')
- grad_ff_in: float32 [2, 512, 2048], P('section', 'dp')
- grad_ff_out: float32 [2, 2048, 512], P('section', 'dp')
- grad_vectors: float32 [2, 8, 512], P('section', None, 'dp')
- grad_ff_bias: float32 [2, 2048], P('section', 'dp')
- grad_head_weight: float32 [512], replicated
- grad_head_bias: float32 [1], replicated
The draws below stay inside these ranges and needn't reach their ends.
Inputs may be any that keep to these rules, and one draw needn't show every extreme that they name: long_flag is 0 or 1 for each micro-batch. `token_mask`: within each micro-batch, a long one (long_flag 1) holds one passage whose real tokens are a non-empty prefix of its 512 rows; otherwise each aligned run of 128 rows holds one passage whose real tokens are a non-empty prefix of the run.
All inputs are finite; a program needn't handle non-finite values.
Results may differ from the reference program's by a relative error of at most 0.024.
Values may be sent and summed in bfloat16 or wider, within the bound.
A program may use at most 320 MiB of HBM per device.

```python
import jax
import jax.numpy as jnp
from jax import lax

D = 512
FF = 2048
HEADS = 8
MB_LEN = 512
SLOT_LEN = 128
TOKENS = 16384
MICRO_ALL = 32


def passage_plan(key):
    key_flag, key_long, key_short = jax.random.split(key, 3)
    flags = jax.random.randint(key_flag, (MICRO_ALL,), 0, 2)
    long_len = jax.random.randint(key_long, (MICRO_ALL, 1), MB_LEN // 2, MB_LEN + 1)
    pieces = MB_LEN // SLOT_LEN
    short_len = jax.random.randint(key_short, (MICRO_ALL, pieces, 1), SLOT_LEN // 2, SLOT_LEN + 1)
    inner = jnp.arange(SLOT_LEN)[None, None, :]
    short_mask = (inner < short_len).reshape(MICRO_ALL, MB_LEN)
    long_mask = jnp.arange(MB_LEN)[None, :] < long_len
    mask = jnp.where(flags[:, None] == 1, long_mask, short_mask)
    return (flags.astype(jnp.int32), mask.astype(jnp.int32).reshape(-1))


def draw_long_flag(key, part):
    return passage_plan(key)[0]


def draw_token_mask(key, part):
    return passage_plan(key)[1]


def draw_vectors(key, part):
    key = jax.random.fold_in(key, 7)
    key_bias, key_gain = jax.random.split(key)
    biases = jnp.clip(jax.random.normal(key_bias, (2, 8, D), jnp.float32) * 0.3, -1.2, 1.2)
    gains = jax.random.uniform(key_gain, (2, 8, D), jnp.float32, 0.6, 1.4)
    rows = jnp.arange(8)
    is_gain = (rows == 3) | (rows == 6)
    return jnp.where(is_gain[None, :, None], gains, biases).astype(jnp.bfloat16)


def level_of(stream_key, shape, cuts, least, top_value):
    def one(dim, parts):
        draws = jax.random.uniform(jax.random.fold_in(jax.random.fold_in(stream_key, 6), dim), (parts,), jnp.float32, least / len(cuts), top_value / len(cuts))
        return jnp.repeat(jnp.exp(draws), shape[dim] // parts).reshape((-1,) + (1,) * (len(shape) - dim - 1))

    factor_of = one(*cuts[0])
    for cut in cuts[1:]:
        factor_of = factor_of * one(*cut)
    return factor_of


def noise(rng, dims, deviation, most, cuts=(), held_as=jnp.bfloat16):
    level = level_of(rng, dims, cuts, -0.22, 0.18) if cuts else 1.0
    result = jax.random.normal(rng, dims, jnp.float32) * deviation * level
    return jnp.minimum(jnp.maximum(result, -most), most).astype(held_as)


def setup_inputs(seed: int = 0) -> dict:
    key_list = jax.random.split(jax.random.key(seed), 14)
    return {
        "tokens_in": noise(key_list[0], (TOKENS, D), 1.0, 6.0, ((0, 16),)),
        "out_cot": noise(key_list[1], (TOKENS, D), 1.0, 6.0, ((0, 16),)),
        "term_cot": noise(key_list[2], (TOKENS,), 1.0, 6.0, ((0, 16),), jnp.float32),
        "long_flag": draw_long_flag(jax.random.fold_in(key_list[13], 71), 0),
        "token_mask": draw_token_mask(jax.random.fold_in(key_list[13], 71), 0),
        "w_qkv": noise(key_list[5], (2, D, 3 * D), D ** -0.5, 0.25, ((0, 2), (1, 16))),
        "w_out": noise(key_list[6], (2, D, D), (D // 64) ** -0.5, 2.0, ((0, 2), (1, 16))),
        "w_ff_in": noise(key_list[7], (2, D, FF), D ** -0.5, 0.25, ((0, 2), (1, 16))),
        "w_ff_out": noise(key_list[8], (2, FF, D), FF ** -0.5, 0.125, ((0, 2), (1, 16))),
        "vectors": draw_vectors(jax.random.fold_in(key_list[13], 71), 0),
        "ff_bias": noise(key_list[10], (2, FF), 0.3, 1.5, ((0, 2), (1, 16))),
        "head_weight": noise(key_list[11], (D,), D ** -0.5, 0.25),
        "head_bias": noise(key_list[12], (1,), 0.5, 2.0, (), jnp.float32),
    }


norm_eps = 1e-12

@jax.custom_vjp
def low(v):
    return lax.optimization_barrier(v.astype(jnp.bfloat16)).astype(jnp.float32)

@jax.custom_vjp
def low_back(v):
    return v

def low_keep(v):
    return (low(v), None)

def low_pass(kept, grad):
    return (grad,)

def back_keep(v):
    return (v, None)

def back_low(kept, grad):
    return (low(grad),)
low.defvjp(low_keep, low_pass)
low_back.defvjp(back_keep, back_low)

def both_ways(values):
    return low_back(low(values))

def layer_norm(values, gain, shift):
    center = values - lax.optimization_barrier(jnp.mean(values, -1, keepdims=True))
    spread = lax.optimization_barrier(jnp.mean(center * center, -1, keepdims=True))
    return center * lax.rsqrt(spread + norm_eps) * gain + shift

def soft_plus(values):
    return jnp.log1p(jnp.exp(-jnp.abs(values))) + jnp.maximum(values, 0.0)

def layer(entry, w_qkv, w_out, w_in, w_back, vec, bias_ff, valid, flag):
    best = lax.Precision.HIGHEST
    width = entry.shape[1]
    qkv = jnp.dot(entry, w_qkv, precision=best)
    query = both_ways(qkv[:, :width] + vec[0]).reshape(MB_LEN, HEADS, -1)
    keys = both_ways(qkv[:, width:2 * width]).reshape(MB_LEN, HEADS, -1)
    values = both_ways(qkv[:, 2 * width:] + vec[1]).reshape(MB_LEN, HEADS, -1)
    raw = low_back(jnp.einsum('lhe,mhe->hlm', query, keys, precision=best) * 0.125)
    position = jnp.arange(MB_LEN)
    segment = jnp.where(flag == 1, 0, position // SLOT_LEN)
    allowed = (segment[:, None] == segment[None, :]) & (valid[None, :] > 0)
    scores = jnp.where(allowed[None], raw, -1000000000.0)
    expo = jnp.exp(scores - lax.optimization_barrier(jnp.max(scores, -1, keepdims=True)))
    probs = low(expo / lax.optimization_barrier(jnp.sum(expo, -1, keepdims=True)))
    context = both_ways(jnp.einsum('hlm,mhe->lhe', probs, values, precision=best).reshape(MB_LEN, width))
    first = entry + low_back(jnp.dot(context, w_out, precision=best) + vec[2])
    normed = layer_norm(first, vec[3], vec[4])
    inner = low_back(jnp.dot(low(normed), w_in, precision=best) + bias_ff)
    branch = jnp.dot(low(jax.nn.gelu(inner, approximate=False)), w_back, precision=best)
    second = normed + low_back(branch + vec[5])
    return layer_norm(second, vec[6], vec[7])

def reference(tokens_in, out_cot, term_cot, long_flag, token_mask, w_qkv, w_out, w_ff_in, w_ff_out, vectors, ff_bias, head_weight, head_bias):
    single = jnp.float32
    count = long_flag.shape[0]
    width = tokens_in.shape[1]
    inputs = tokens_in.astype(single).reshape(count, MB_LEN, width)
    valid = token_mask.astype(single).reshape(count, MB_LEN)
    params = tuple((item.astype(single) for item in (w_qkv, w_out, w_ff_in, w_ff_out, vectors, ff_bias, head_weight, head_bias)))
    offset = jnp.zeros_like(inputs)

    def forward(inputs, offset, wq, wo, wi, wf, vec, bias, hw, hb):

        def single_batch(item):
            entry, delta, mask, flag = item
            lower = layer(entry, wq[0], wo[0], wi[0], wf[0], vec[0], bias[0], mask, flag)
            passed = low_back(low(lower) + delta)
            upper = layer(passed, wq[1], wo[1], wi[1], wf[1], vec[1], bias[1], mask, flag)
            top = low(upper)
            terms = soft_plus(jnp.dot(top, hw, precision=lax.Precision.HIGHEST) + hb[0])
            return (low(lower), top, terms)
        return lax.map(jax.checkpoint(single_batch), (inputs, offset, valid, long_flag))
    outs, pull = jax.vjp(forward, inputs, offset, *params)
    lower, upper, terms = outs
    cots = (jnp.zeros_like(lower), out_cot.astype(single).reshape(count, MB_LEN, width) * valid[..., None], term_cot.astype(single).reshape(count, MB_LEN) * valid)
    grads = pull(cots)
    g_in, g_off, g_wq, g_wo, g_wi, g_wf, g_vec, g_bias, g_hw, g_hb = grads
    acts = jnp.stack([lower, upper]).reshape(2, -1, width).astype(jnp.bfloat16)
    in_grads = jnp.stack([g_in, g_off]).reshape(2, -1, width).astype(jnp.bfloat16)
    return (acts, terms.reshape(-1).astype(jnp.bfloat16), in_grads, g_wq, g_wo, g_wi, g_wf, g_vec, g_bias, g_hw, g_hb)
```

```python
import functools
import types

import jax
import jax.numpy as jnp
from jax import lax
from jax.experimental import pallas as pl
from jax.experimental.pallas import tpu as pltpu
from jax.sharding import PartitionSpec as P

RUN = 128
HEADS = 8
EPS = 1e-12
F32, BF16 = jnp.float32, jnp.bfloat16
VMEM_BYTES = 64 * 2**20


def dot(a, b):
    return lax.dot_general(a, b, (((1,), (0,)), ((), ())), preferred_element_type=F32)


def dot_nt(a, b):
    return lax.dot_general(a, b, (((1,), (1,)), ((), ())), preferred_element_type=F32)


def dot_tn(a, b):
    return lax.dot_general(a, b, (((0,), (0,)), ((), ())), preferred_element_type=F32)


def rows8(v):
    return jnp.sum(v.reshape(-1, 8, v.shape[1]), axis=0)


def gelu_both(u):
    e = jnp.exp(u * u * -0.5)
    d = jnp.abs(u) * (0.3275911 * 0.7071067811865476) + 1.0
    t = pl.reciprocal(d, approx=True)
    t = t * (2.0 - d * t)
    q = t * 0.5307027145 - 0.7265760135
    q = q * t + 0.7107068705
    q = q * t - 0.142248368
    q = q * t + 0.127414796
    q = q * t * e
    cdf = jnp.where(u >= 0.0, 1.0 - q, q)
    return u * cdf, cdf + u * (e * 0.3989422804014327)


def layer_norm_rows(y):
    c = y - jnp.mean(y, -1, keepdims=True)
    r = lax.rsqrt(jnp.mean(c * c, -1, keepdims=True) + EPS)
    return c * r, r


def layer_norm_back(g, gain, xh, r):
    gx = g * gain
    a = jnp.mean(gx, -1, keepdims=True)
    b = jnp.mean(gx * xh, -1, keepdims=True)
    return (gx - a - xh * b) * r


MESH = pl.DeviceIdType.MESH
PARTS = 12
GATHER = ((0, 2), (2, 2), (4, 2), (6, 2), (8, 2), (10, 2))
GATHER_LATE = (4, 5)
GATHER_ORDER = (0, 1, 4, 5, 2, 3)
REDUCE = ((0, 3), (3, 1), (4, 2), (6, 2), (8, 2), (10, 2))
REDUCE_LATE = {1: (4, 5), 0: ()}


class Exchange:
    def __init__(self, o, grid, rp):
        self.o, self.rp = o, rp
        self.Z, self.X, self.C = grid
        self.s = lax.axis_index("section")
        d = lax.axis_index("dp")
        self.c = lax.rem(d, 2)
        self.x = lax.rem(d // 2, 2)
        self.z = d // 4
        self.late = sorted({k for ks in REDUCE_LATE.values() for k in ks})
        self.late_rows = {}
        at = 0
        for k in self.late:
            self.late_rows[k] = at
            at += REDUCE[k][1] * rp
        self.small = len(GATHER)

    def dev(self, s=None, z=None, x=None, c=None):
        s = self.s if s is None else s
        z = self.z if z is None else z
        x = self.x if x is None else x
        c = self.c if c is None else c
        return (s, (z * 2 + x) * 2 + c)

    def peers(self):
        out = [self.dev(z=lax.rem(self.z + j, self.Z)) for j in range(1, self.Z)]
        return out + [self.dev(x=1 - self.x), self.dev(c=1 - self.c), self.dev(s=1 - self.s)]

    def barrier(self):
        b = pltpu.get_barrier_semaphore()
        ps = self.peers()
        for p in ps:
            pl.semaphore_signal(b, inc=1, device_id=p, device_id_type=MESH)
        pl.semaphore_wait(b, len(ps))

    def copy(self, src, dst, send, recv, dev):
        return pltpu.make_async_remote_copy(
            src_ref=src, dst_ref=dst, send_sem=send, recv_sem=recv, device_id=dev, device_id_type=MESH)

    def gbuf(self, l, k):
        if k == self.small:
            return self.o.wsm.at[l], slice(None)
        p, n = GATHER[k]
        return self.o.wall.at[l], pl.ds(p * self.rp, n * self.rp)

    def g_copy(self, kind, l, k, j=0):
        o = self.o
        w, rows = self.gbuf(l, k)
        z, x, c = self.z, self.x, self.c
        if kind == "z":
            own = w.at[z, x, c, rows]
            return self.copy(own, own, o.gs.at[l, k, j], o.gr.at[l, k, j], self.dev(z=lax.rem(z + j + 1, self.Z)))
        if kind == "x":
            own = w.at[:, x, c, rows]
            return self.copy(own, own, o.gs.at[l, k, 3], o.gr.at[l, k, 3], self.dev(x=1 - x))
        if kind == "y":
            own = w.at[:, :, c, rows] if k in GATHER_LATE else w.at[z, x, c, rows]
            return self.copy(own, own, o.gs.at[l, k, 4], o.gr.at[l, k, 4], self.dev(s=1 - self.s))
        own = w.at[:, :, c, rows]
        return self.copy(own, own, o.gs.at[l, k, 5], o.gr.at[l, k, 5], self.dev(c=1 - c))

    def g_begin(self, l):
        for k in (self.small,) + GATHER_ORDER:
            if k not in GATHER_LATE:
                self.g_copy("y", l, k).start()
        for k in (self.small,) + GATHER_ORDER:
            for j in range(self.Z - 1):
                self.g_copy("z", l, k, j).start()

    def g_relay(self, l, k):
        if k not in GATHER_LATE:
            @pl.when(self.s != l)
            def _():
                self.g_copy("y", l, k).wait_recv()
                for j in range(self.Z - 1):
                    self.g_copy("z", l, k, j).start()

    def both(self, l, k, late, f):
        if k in late:
            pl.when(self.s == l)(f)
        else:
            f()

    def g_x(self, l, k):
        def go():
            for j in range(self.Z - 1):
                self.g_copy("z", l, k, j).wait_recv()
            self.g_copy("x", l, k).start()

        self.both(l, k, GATHER_LATE, go)

    def g_core(self, l, k):
        def go():
            self.g_copy("x", l, k).wait_recv()
            if k in GATHER_LATE:
                self.g_copy("y", l, k).start()

        self.both(l, k, GATHER_LATE, go)
        if k in GATHER_LATE:
            @pl.when(self.s != l)
            def _():
                self.g_copy("y", l, k).wait_recv()
        self.g_copy("c", l, k).start()

    def g_done(self, l, k):
        self.g_copy("c", l, k).wait_recv()

    def g_drain(self, l):
        for k in range(self.small + 1):
            def own():
                for j in range(self.Z - 1):
                    self.g_copy("z", l, k, j).wait_send()
                self.g_copy("x", l, k).wait_send()

            self.both(l, k, GATHER_LATE, own)
            @pl.when(self.s == l)
            def _():
                self.g_copy("y", l, k).wait_send()
            self.g_copy("c", l, k).wait_send()

    def r_small(self, k):
        return k == len(REDUCE)

    def rows(self, k):
        p, n = REDUCE[k]
        return pl.ds(p * self.rp, n * self.rp)

    def is_late(self, l, k):
        return k in REDUCE_LATE[l]

    def r_bufs(self, l, k):
        o = self.o
        if self.r_small(k):
            return o.gsm.at[l], slice(None), o.r1s.at[l], o.rxs.at[l], o.rzs.at[l], o.rys
        g = o.g1 if l == 1 else o.wall.at[1]
        return g, self.rows(k), o.r1, o.rx.at[l], o.rz.at[l], o.rf

    def r_copy(self, kind, l, k, j=0):
        o = self.o
        g, rows, r1, rx, rz, rf = self.r_bufs(l, k)
        z, x, c = self.z, self.x, self.c
        ss, rr = o.rs_.at[l, k], o.rr_.at[l, k]
        if kind == "c":
            return self.copy(g.at[:, :, 1 - c, rows], r1.at[:, :, rows], ss.at[0], rr.at[0], self.dev(c=1 - c))
        if kind == "x":
            return self.copy(g.at[:, 1 - x, c, rows], rx.at[:, rows], ss.at[1], rr.at[1], self.dev(x=1 - x))
        if kind == "z":
            to = lax.rem(z + j + 1, self.Z)
            return self.copy(g.at[to, x, c, rows], rz.at[z, rows], ss.at[2 + j], rr.at[2 + j], self.dev(z=to))
        if self.is_late(l, k):
            dst = o.ry.at[:, :, pl.ds(self.late_rows[k], REDUCE[k][1] * self.rp)]
            return self.copy(g.at[:, :, c, rows], dst, ss.at[5], rr.at[5], self.dev(s=1 - self.s))
        return self.copy(g.at[z, x, c, rows], rf.at[rows], ss.at[5], rr.at[5], self.dev(s=1 - self.s))

    def r_c(self, l, k):
        if l == 0 and not self.r_small(k):
            pl.semaphore_wait(self.o.credit.at[k], 1)
        self.r_copy("c", l, k).start()

    def add(self, dst, src, lead):
        def one(i, _):
            if lead == 2:
                a, b = i // 2, lax.rem(i, 2)
                d, t = dst(a, b), src(a, b)
            else:
                d, t = dst(i), src(i)
            d[...] = (d[...].astype(F32) + t[...].astype(F32)).astype(d.dtype)
            return 0

        lax.fori_loop(0, self.Z * (self.X if lead == 2 else 1), one, 0)

    def r_1(self, l, k):
        g, rows, r1, rx, rz, rf = self.r_bufs(l, k)
        c = self.c
        self.r_copy("c", l, k).wait_recv()
        self.add(lambda a, b: g.at[a, b, c, rows], lambda a, b: r1.at[a, b, rows], 2)
        if l == 1 and not self.r_small(k):
            pl.semaphore_signal(self.o.credit.at[k], inc=1, device_id=self.dev(c=1 - c), device_id_type=MESH)
        if self.is_late(l, k):
            pl.when(self.s != l)(lambda: self.r_copy("y", l, k).start())
        else:
            self.r_copy("x", l, k).start()

    def r_y(self, l, k):
        if self.is_late(l, k):
            g, rows, r1, rx, rz, rf = self.r_bufs(l, k)
            c = self.c

            @pl.when(self.s == l)
            def _():
                self.r_copy("y", l, k).wait_recv()
                got = pl.ds(self.late_rows[k], REDUCE[k][1] * self.rp)
                self.add(lambda a, b: g.at[a, b, c, rows], lambda a, b: self.o.ry.at[a, b, got], 2)
                self.r_copy("x", l, k).start()

    def r_2(self, l, k):
        g, rows, r1, rx, rz, rf = self.r_bufs(l, k)
        x, c = self.x, self.c

        def go():
            self.r_copy("x", l, k).wait_recv()
            self.add(lambda a: g.at[a, x, c, rows], lambda a: rx.at[a, rows], 1)
            for j in range(self.Z - 1):
                self.r_copy("z", l, k, j).start()

        self.both(l, k, REDUCE_LATE[l], go)

    def r_3(self, l, k):
        g, rows, r1, rx, rz, rf = self.r_bufs(l, k)
        z, x, c = self.z, self.x, self.c

        def go():
            for j in range(self.Z - 1):
                self.r_copy("z", l, k, j).wait_recv()
            rz[z, rows] = g[z, x, c, rows]
            total = rz[0, rows].astype(F32)
            for i in range(1, self.Z):
                total = total + rz[i, rows].astype(F32)
            if self.is_late(l, k):
                self.result(k, total)
            else:
                g[z, x, c, rows] = total.astype(g.dtype)
                pl.when(self.s != l)(lambda: self.r_copy("y", l, k).start())

        self.both(l, k, REDUCE_LATE[l], go)

    def r_4(self, l, k):
        if not self.is_late(l, k):
            g, rows, r1, rx, rz, rf = self.r_bufs(l, k)

            @pl.when(self.s == l)
            def _():
                self.r_copy("y", l, k).wait_recv()
                self.result(k, g[self.z, self.x, self.c, rows].astype(F32) + rf[rows].astype(F32))

    def result(self, k, v):
        o, rp = self.o, self.rp
        if self.r_small(k):
            o.d_small[...] = v
            return
        p0, n = REDUCE[k]
        w = v.shape[1]
        for i in range(n):
            p, t = p0 + i, v[i * rp : (i + 1) * rp]
            if p < 3:
                o.d_wq[0, :, p * w : (p + 1) * w] = t
            elif p == 3:
                o.d_wo[0] = t
            elif p < 8:
                o.d_wi[0, :, (p - 4) * w : (p - 3) * w] = t
            else:
                o.d_wf[0, (p - 8) * rp : (p - 7) * rp, :] = t

    def r_drain(self, l):
        for k in range(len(REDUCE) + 1):
            self.r_copy("c", l, k).wait_send()

            def xz():
                self.r_copy("x", l, k).wait_send()
                for j in range(self.Z - 1):
                    self.r_copy("z", l, k, j).wait_send()

            self.both(l, k, REDUCE_LATE[l], xz)
            pl.when(self.s != l)(lambda: self.r_copy("y", l, k).wait_send())


def kernel(names, grid, *refs):
    o = types.SimpleNamespace(**dict(zip(names, refs)))
    fused = grid is not None
    W = o.h_s.shape[2]
    FF = o.f_s.shape[1]
    Z, X, C, total = o.wall.shape[1:5]
    rp = total // PARTS
    flag, hb, hw, wall, g1 = o.flag, o.hb, o.hw, o.wall, o.g1
    q_s, k_s, v_s, p_s, c_s, xh1, r1, n1 = o.q_s, o.k_s, o.v_s, o.p_s, o.c_s, o.xh1, o.r1n, o.n1
    f_s, gp, xh2, r2, y_s, h_s, oc = o.f_s, o.gp, o.xh2, o.r2n, o.y_s, o.h_s, o.oc
    gin1, mrow, g_s, go, gt, ds_s, gqkv, xt, cols = o.gin1, o.mrow, o.g_s, o.go, o.gt, o.ds_s, o.gqkv, o.xt, o.cols
    vec, bff, dvec, dbff, sems = o.vec, o.bff, o.dvec, o.dbff, o.sems
    tc, mask = o.aux[0:1, :], o.aux[1:2, :]

    if fused:
        ex = Exchange(o, grid, rp)
        s, z, x, c = ex.s, ex.z, ex.x, ex.c
        R = h_s.shape[1]
        cin = [pltpu.make_async_copy(o.x_in.at[pl.ds(pl.multiple_of(s * R, R), R)], h_s.at[0], sems.at[0]),
               pltpu.make_async_copy(o.oc_in.at[pl.ds(pl.multiple_of(s * R, R), R)], oc, sems.at[1])]
        for t in cin:
            t.start()
        for i in range(3):
            wall[s, z, x, c, i * rp : (i + 1) * rp, :] = o.wq_in[0, :, i * W : (i + 1) * W]
        wall[s, z, x, c, 3 * rp : 4 * rp, :] = o.wo_in[0]
        for i in range(4):
            wall[s, z, x, c, (4 + i) * rp : (5 + i) * rp, :] = o.wi_in[0, :, i * W : (i + 1) * W]
        wall[s, z, x, c, 8 * rp :, :] = o.wf_in[0]
        nv, nb = o.vec_in.shape[2], o.bff_in.shape[1]
        o.wsm[s, z, x, c] = jnp.zeros(o.wsm.shape[4:], F32)
        o.wsm[s, z, x, c, 0:8, 0:nv] = o.vec_in[0].astype(F32)
        o.wsm[s, z, x, c, 8:9, 0:nb] = o.bff_in[...].astype(F32)
        ex.barrier()
        K = len(GATHER)
        for l in range(2):
            pl.when(s == l)(functools.partial(ex.g_begin, l))
        for k in (K,) + GATHER_ORDER:
            ex.g_relay(0, k)
            ex.g_relay(1, k)
    else:
        cin = [pltpu.make_async_copy(o.x_in, h_s.at[0], sems.at[0]),
               pltpu.make_async_copy(o.oc_in, oc, sems.at[1]),
               pltpu.make_async_copy(o.w_in, wall, sems.at[2])]
        for t in cin:
            t.start()
        vec[...] = o.vec_in[...]
        bff[...] = o.bff_in[...]

    for t in cin:
        t.wait()

    lane = lax.broadcasted_iota(jnp.int32, (W, 128), 1)
    sides4 = ((lane < 64).astype(F32).astype(BF16), (lane >= 64).astype(F32).astype(BF16))
    sides = tuple(t[:RUN] for t in sides4)

    valid = mask > 0.0
    key_run = lax.broadcasted_iota(jnp.int32, (1, W), 1) // RUN
    for r in range(4):
        ok = valid & ((key_run == r) | (flag[0] == 1))
        mrow[r : r + 1, :] = jnp.where(ok, 0.0, -1e9)

    def small_weights(l):
        for i in range(Z * X * C):
            b = o.wsm.at[l, i // (X * C), (i // C) % X, i % C]
            vec[l, :, i * nv : (i + 1) * nv] = b[0:8, 0:nv]
            bff[l, 0:1, i * nb : (i + 1) * nb] = b[8:9, 0:nb]

    def part(l, p, cs=slice(None)):
        a = wall[l, :, :, :, pl.ds(pl.multiple_of(p * rp, rp), rp), cs]
        return a.reshape(W, a.shape[-1])

    def part_rows(l, p, r0, n):
        if C == 1:
            return wall[l, 0, 0, 0, pl.ds(pl.multiple_of(p * rp + r0, n), n), :]
        k = n // (X * C * rp)
        return wall[l, pl.ds(r0 // (X * C * rp), k), :, :, pl.ds(pl.multiple_of(p * rp, rp), rp), :].reshape(n, W)

    def back_w(l, cs):
        a = wall[l, :, :, :, 8 * rp :, cs]
        return a.reshape(FF, a.shape[-1])

    def back_rows(l, j, n):
        if C == 1:
            return wall[l, 0, 0, 0, pl.ds(pl.multiple_of(8 * rp + j * n, n), n), :]
        return wall[l, j // X, lax.rem(j, X), :, 8 * rp :, :].reshape(n, W)

    def g_ref(l):
        return g1 if l == 1 else wall.at[1]

    def put_part(l, p, cs, val):
        rows = pl.ds(pl.multiple_of(p * rp, rp), rp)
        g_ref(l)[:, :, :, rows, cs] = val.reshape(Z, X, C, rp, -1).astype(BF16)

    def put_back(l, j, val):
        n = val.shape[0]
        if C == 1:
            g_ref(l)[0, 0, 0, pl.ds(pl.multiple_of(8 * rp + j * n, n), n), :] = val.astype(BF16)
        else:
            g_ref(l)[j // X, lax.rem(j, X), :, 8 * rp :, :] = val.reshape(C, 4 * rp, W).astype(BF16)

    def vrow(l, i):
        return vec[l, i : i + 1, :]

    def keep(src, dst, i):
        return pltpu.make_async_copy(src, dst, sems.at[i])

    def qkv(l):
        h = h_s.at[l]

        def step(j, _):
            cs = pl.ds(pl.multiple_of(j * 256, 256), 256)
            hv = h[...]
            rq = dot(hv, part(l, 0, cs)) + vec[l, 0:1, cs]
            q_s[l, :, cs] = (rq.astype(BF16).astype(F32) * 0.125).astype(BF16)
            k_s[l, :, cs] = dot(hv, part(l, 1, cs)).astype(BF16)
            v_s[l, :, cs] = (dot(hv, part(l, 2, cs)) + vec[l, 1:2, cs]).astype(BF16)
            return 0

        lax.fori_loop(0, 2, step, 0)

    def attend(l, each=None):
        def pair(p, _):
            cs = pl.ds(pl.multiple_of(p * 128, 128), 128)
            k2 = k_s[l, :, cs]
            v2 = v_s[l, :, cs]
            vh = [v2 * t for t in sides4]
            for r in range(4):
                rs = slice(r * RUN, (r + 1) * RUN)
                q2 = q_s[l, rs, cs]
                acc = None
                for t in range(2):
                    raw = dot_nt(q2 * sides[t], k2) + mrow[r : r + 1, :]
                    e = jnp.exp(raw - jnp.max(raw, -1, keepdims=True))
                    pr = (e * (1.0 / jnp.sum(e, -1, keepdims=True))).astype(BF16)
                    p_s[2 * p + t, rs, :] = pr
                    d = dot(pr, vh[t])
                    acc = d if acc is None else acc + d
                c_s[l, rs, cs] = acc.astype(BF16)
            if each is not None:
                each(p)
            return 0

        lax.fori_loop(0, 4, pair, 0)
        if l == 0:
            keep(p_s, o.keep_p, 3).start()

    def project(l):
        def step(j, _):
            rs = pl.ds(pl.multiple_of(j * 256, 256), 256)
            y = h_s[l, rs, :].astype(F32) + dot(c_s[l, rs, :], part(l, 3)) + vrow(l, 2)
            xh, r = layer_norm_rows(y)
            xh1[l, rs, :] = xh
            r1[l, rs, :] = r
            n1[l, rs, :] = (xh * vrow(l, 3) + vrow(l, 4)).astype(BF16)
            return 0

        lax.fori_loop(0, 2, step, 0)

    def ff_in(l, j0, j1):
        def step(j, _):
            cs = pl.ds(pl.multiple_of(j * 256, 256), 256)
            sub = pl.ds(pl.multiple_of(lax.rem(j, 2) * 256, 256), 256)
            u = dot(n1[l], part(l, 4 + j // 2, sub)) + bff[l, 0:1, cs]
            f, d = gelu_both(u)
            f_s[:, cs] = f.astype(BF16)
            gp[:, cs] = d.astype(BF16)
            return 0

        lax.fori_loop(j0, j1, step, 0)

    def ff_out(l):
        def step(j, _):
            cs = pl.ds(pl.multiple_of(j * 256, 256), 256)
            y_s[:, cs] = dot(f_s[...], back_w(l, cs))
            return 0

        lax.fori_loop(0, 2, step, 0)
        if l == 0:
            keep(f_s, o.keep_f, 4).start()
            keep(gp, o.keep_g, 5).start()

        def top(j, _):
            rs = pl.ds(pl.multiple_of(j * RUN, RUN), RUN)
            y = xh1[l, rs, :] * vrow(l, 3) + vrow(l, 4) + y_s[rs, :] + vrow(l, 5)
            xh, r = layer_norm_rows(y)
            xh2[l, rs, :] = xh
            r2[l, rs, :] = r
            h_s[l + 1, rs, :] = (xh * vrow(l, 6) + vrow(l, 7)).astype(BF16)
            return 0

        lax.fori_loop(0, 4, top, 0)

    spilled = ((p_s, o.keep_p, 3), (f_s, o.keep_f, 4), (gp, o.keep_g, 5))

    if fused:
        K = len(GATHER)
        for l in range(2):
            for k in (K,) + GATHER_ORDER:
                ex.g_x(l, k)
                ex.g_core(l, k)
        for l in range(2):
            for k in range(K + 1):
                ex.g_done(l, k)
            ex.g_drain(l)
            small_weights(l)
        for l in range(2):
            qkv(l)
            if l == 1:
                keep(*spilled[0]).wait()
            attend(l)
            project(l)
            if l == 1:
                keep(*spilled[1]).wait()
                keep(*spilled[2]).wait()
            ff_in(l, 0, FF // 256)
            ff_out(l)
    else:
        for l in range(2):
            qkv(l)
            if l == 1:
                keep(*spilled[0]).wait()
            attend(l)
            project(l)
            if l == 1:
                keep(*spilled[1]).wait()
                keep(*spilled[2]).wait()
            ff_in(l, 0, FF // 256)
            ff_out(l)

    act1 = h_s.at[2]
    hw16 = jnp.broadcast_to(hw[...], (16, W))
    zr = dot_nt(hw16, act1[...])[0:1] + hb[0]
    ez = jnp.exp(-jnp.abs(zr))
    terms = jnp.log1p(ez) + jnp.maximum(zr, 0.0)
    sig = jnp.where(zr >= 0.0, 1.0, ez) / (1.0 + ez)
    gz = tc * mask * sig
    dhb = jnp.sum(gz, -1, keepdims=True)
    sub8 = lax.broadcasted_iota(jnp.int32, (8, W), 0)
    cols[...] = jnp.where(sub8 == 0, gz, jnp.where(sub8 == 1, mask, 0.0)).T
    if fused:
        o.term[s] = terms
        send_act = ex.copy(h_s.at[2 - s], o.act_out.at[pl.ds(pl.multiple_of(s * R, R), R)], o.os.at[0], o.orr.at[0],
                           ex.dev(s=1 - s))
        send_term = ex.copy(o.term.at[s], o.term.at[s], o.os.at[1], o.orr.at[1], ex.dev(s=1 - s))
        own_act = pltpu.make_async_copy(h_s.at[1 + s], o.act_out.at[pl.ds(pl.multiple_of(s * R, R), R)], sems.at[0])
        send_act.start()
        send_term.start()
        own_act.start()
    else:
        o.term[...] = terms

    def top_back(l):
        zero = jnp.zeros((8, W), F32)

        def step(j, carry):
            sg, ss, sb, sh = carry
            rs = pl.ds(pl.multiple_of(j * RUN, RUN), RUN)
            if l == 1:
                gzc = cols[rs, 0:1]
                g = oc[rs, :].astype(F32) * cols[rs, 1:2] + gzc * hw[...].astype(F32)
                sh = sh + rows8(gzc * act1[rs, :].astype(F32))
            else:
                g = gin1[rs, :].astype(F32)
            xh = xh2[l, rs, :]
            sg = sg + rows8(g * xh)
            ss = ss + rows8(g)
            gy = layer_norm_back(g, vrow(l, 6), xh, r2[l, rs, :])
            g_s[rs, :] = gy
            gl = gy.astype(BF16)
            go[rs, :] = gl
            sb = sb + rows8(gl.astype(F32))
            return sg, ss, sb, sh

        sg, ss, sb, sh = lax.fori_loop(0, 4, step, (zero,) * 4)
        dvec[l, 6:7, :] = jnp.sum(sg, 0, keepdims=True)
        dvec[l, 7:8, :] = jnp.sum(ss, 0, keepdims=True)
        dvec[l, 5:6, :] = jnp.sum(sb, 0, keepdims=True)
        if l == 1:
            o.dhw[...] = jnp.sum(sh, 0, keepdims=True)
            if not fused:
                o.dhb[...] = dhb
            xt[...] = n1[l].T
        else:
            xt[...] = n1[l].T

    def ff_out_grad(l):
        def step(j, _):
            cs = pl.ds(pl.multiple_of(j * 256, 256), 256)
            put_back(l, j, dot_tn(f_s[:, cs], go[...]))
            return 0

        lax.fori_loop(0, FF // 256, step, 0)

    def ff_back(l, j0, j1):
        def step(j, _):
            cs = pl.ds(pl.multiple_of(j * 256, 256), 256)
            gf = dot_nt(go[...], back_rows(l, j, 256)) * gp[:, cs].astype(F32)
            gul = gf.astype(BF16)
            f_s[:, cs] = gul
            dbff[l, 0:1, cs] = jnp.sum(rows8(gul.astype(F32)), 0, keepdims=True)
            sub = pl.ds(pl.multiple_of(lax.rem(j, 2) * 256, 256), 256)
            put_part(l, 4 + j // 2, sub, dot(xt[...], gul))
            return 0

        lax.fori_loop(j0, j1, step, 0)

    def mid(l):
        def step(j, _):
            cs = pl.ds(pl.multiple_of(j * 256, 256), 256)
            acc = None
            for p in range(4):
                d = dot_nt(f_s[:, p * W : (p + 1) * W], part_rows(l, 4 + p, j * 256, 256))
                acc = d if acc is None else acc + d
            y_s[:, cs] = acc
            return 0

        lax.fori_loop(0, 2, step, 0)
        if l == 1:
            keep(o.keep_f, f_s, 4).start()
            keep(o.keep_g, gp, 5).start()

        zero = jnp.zeros((8, W), F32)

        def back(j, carry):
            sg, ss, sb = carry
            rs = pl.ds(pl.multiple_of(j * RUN, RUN), RUN)
            g = g_s[rs, :] + y_s[rs, :]
            xh = xh1[l, rs, :]
            sg = sg + rows8(g * xh)
            ss = ss + rows8(g)
            gy = layer_norm_back(g, vrow(l, 3), xh, r1[l, rs, :])
            g_s[rs, :] = gy
            gl = gy.astype(BF16)
            go[rs, :] = gl
            sb = sb + rows8(gl.astype(F32))
            return sg, ss, sb

        sg, ss, sb = lax.fori_loop(0, 4, back, (zero,) * 3)
        dvec[l, 3:4, :] = jnp.sum(sg, 0, keepdims=True)
        dvec[l, 4:5, :] = jnp.sum(ss, 0, keepdims=True)
        dvec[l, 2:3, :] = jnp.sum(sb, 0, keepdims=True)

    def project_back(l):
        put_part(l, 3, slice(None), dot_tn(c_s[l], go[...]))
        gc = dot_nt(go[...], part(l, 3)).astype(BF16)
        go[...] = gc
        gt[...] = gc.T

    def attend_back(l, each=None):
        def pair(p, _):
            c0 = pl.multiple_of(p * 128, 128)
            cs = pl.ds(c0, 128)
            k2 = k_s[l, :, cs]
            v2 = v_s[l, :, cs]
            qt = q_s[l, :, cs].T
            gct = gt[cs, :]
            kh = [k2 * t for t in sides4]
            dq = [None] * 4
            dvt, dkt = [], []
            for t in range(2):
                for r in range(4):
                    rs = slice(r * RUN, (r + 1) * RUN)
                    pr = p_s[2 * p + t, rs, :].astype(F32)
                    w = pr * dot_nt(go[rs, cs] * sides[t], v2)
                    dsl = (w - pr * jnp.sum(w, -1, keepdims=True)).astype(BF16)
                    ds_s[t, rs, :] = dsl
                    dd = dot(dsl, kh[t])
                    dq[r] = dd if dq[r] is None else dq[r] + dd
                hs = slice(64 * t, 64 * t + 64)
                dvt.append(dot(gct[hs], p_s[2 * p + t]))
                dkt.append(dot(qt[hs], ds_s[t]))
            dql = (jnp.concatenate(dq, 0) * 0.125).astype(BF16)
            dvl = jnp.concatenate(dvt, 0).T.astype(BF16)
            dkl = jnp.concatenate(dkt, 0).T.astype(BF16)
            gqkv[:, cs] = dql
            gqkv[:, pl.ds(pl.multiple_of(c0 + W, 128), 128)] = dkl
            gqkv[:, pl.ds(pl.multiple_of(c0 + 2 * W, 128), 128)] = dvl
            dvec[l, 0:1, cs] = jnp.sum(rows8(dql.astype(F32)), 0, keepdims=True)
            dvec[l, 1:2, cs] = jnp.sum(rows8(dvl.astype(F32)), 0, keepdims=True)
            if each is not None:
                each(p)
            return 0

        lax.fori_loop(0, 4, pair, 0)
        if l == 1:
            keep(o.keep_p, p_s, 3).start()
        xt[...] = h_s[l].T

    def qkv_grad(l):
        for p in range(3):
            put_part(l, p, slice(None), dot(xt[...], gqkv[:, p * W : (p + 1) * W]))

    def qkv_back(l):
        gdst = gin1 if l == 1 else oc

        def step(j, _):
            cs = pl.ds(pl.multiple_of(j * 256, 256), 256)
            acc = g_s[:, cs]
            for p in range(3):
                acc = acc + dot_nt(gqkv[:, p * W : (p + 1) * W], part_rows(l, p, j * 256, 256))
            gdst[:, cs] = acc.astype(BF16)
            return 0

        lax.fori_loop(0, 2, step, 0)

    def small_grads(l):
        for i in range(Z * X * C):
            b = o.gsm.at[l, i // (X * C), (i // C) % X, i % C]
            b[...] = jnp.zeros(b.shape, F32)
            b[0:8, 0:nv] = dvec[l, :, i * nv : (i + 1) * nv]
            b[8:9, 0:nb] = dbff[l, 0:1, i * nb : (i + 1) * nb]
            for t in range(W // 128):
                b[9 + t : 10 + t, :] = o.dhw[0:1, t * 128 : (t + 1) * 128]
            b[9 + W // 128 : 10 + W // 128, 0:1] = dhb

    if fused:
        KR = len(REDUCE)
        for l in (1, 0):
            if l == 0:
                for src, dst, i in spilled:
                    keep(dst, src, i).wait()
            top_back(l)
            ff_out_grad(l)
            ff_back(l, 0, FF // 256)
            mid(l)
            project_back(l)
            attend_back(l)
            qkv_back(l)
            qkv_grad(l)
            small_grads(l)
            for k in range(KR + 1):
                ex.r_c(l, k)
            for k in range(KR + 1):
                ex.r_1(l, k)
            for k in range(KR + 1):
                ex.r_y(l, k)
            for k in range(KR + 1):
                ex.r_2(l, k)
            for k in range(KR + 1):
                ex.r_3(l, k)
            for k in range(KR + 1):
                ex.r_4(l, k)
        own_rows = pl.ds(pl.multiple_of(s * R, R), R)
        send_g = [ex.copy(g, o.gin_out.at[own_rows], o.os.at[2], o.orr.at[2], ex.dev(s=1 - s)) for g in (oc, gin1)]
        own_g = [pltpu.make_async_copy(g, o.gin_out.at[own_rows], sems.at[1]) for g in (oc, gin1)]
        for i in range(2):
            pl.when(s != i)(send_g[i].start)
            pl.when(s == i)(own_g[i].start)
        for l in (1, 0):
            ex.r_drain(l)
        send_act.wait()
        send_term.wait()
        own_act.wait()
        send_g[0].wait()
        own_g[0].wait()
    else:
        for l in (1, 0):
            if l == 0:
                for src, dst, i in spilled:
                    keep(dst, src, i).wait()
            top_back(l)
            ff_out_grad(l)
            ff_back(l, 0, FF // 256)
            mid(l)
            project_back(l)
            attend_back(l)
            qkv_back(l)
            qkv_grad(l)
        outs = [pltpu.make_async_copy(g1, o.g_out.at[1], sems.at[0]),
                pltpu.make_async_copy(wall.at[1], o.g_out.at[0], sems.at[1]),
                pltpu.make_async_copy(h_s.at[pl.ds(1, 2)], o.act_out, sems.at[2]),
                pltpu.make_async_copy(oc, o.gin_out.at[0], sems.at[3]),
                pltpu.make_async_copy(gin1, o.gin_out.at[1], sems.at[4])]
        for t in outs:
            t.start()
        for t in outs:
            t.wait()


def make_call(rows, width, inner, n_vec, n_bias, grid, gather=None):
    f32 = lambda *t: jax.ShapeDtypeStruct(t, F32)
    b16 = lambda *t: jax.ShapeDtypeStruct(t, BF16)
    v = lambda dt, *t: pltpu.VMEM(t, dt)
    Z, X, C = grid or (1, 1, 1)
    rp = width // (Z * X * C)
    total = PARTS * rp
    vm = pl.BlockSpec(memory_space=pltpu.VMEM)
    sm = pl.BlockSpec(memory_space=pltpu.SMEM)
    hbm = pl.BlockSpec(memory_space=pl.ANY)
    ins = {"flag": sm, "hb": sm, "x_in": hbm, "oc_in": hbm, "aux": vm, "hw": vm}
    if grid:
        ins |= {"wq_in": vm, "wo_in": vm, "wi_in": vm, "wf_in": vm, "vec_in": vm, "bff_in": vm}
        outs = {
            "act_out": (b16(2 * rows, width), hbm), "gin_out": (b16(2 * rows, width), hbm),
            "term": (f32(2, 1, rows), vm),
            "d_wq": (f32(1, rp, 3 * width), vm), "d_wo": (f32(1, rp, width), vm), "d_wi": (f32(1, rp, inner), vm),
            "d_wf": (f32(1, 4 * rp, width), vm), "d_small": (f32(16, 128), vm),
        }
    else:
        ins |= {"w_in": hbm, "vec_in": vm, "bff_in": vm}
        outs = {
            "act_out": (b16(2, rows, width), hbm), "gin_out": (b16(2, rows, width), hbm), "term": (f32(1, rows), vm),
            "g_out": (b16(2, 1, 1, 1, total, width), hbm), "dvec": (f32(2, 8, width), vm),
            "dbff": (f32(2, 1, inner), vm), "dhw": (f32(1, width), vm), "dhb": (f32(1, 1), vm),
        }
    outs |= {"keep_p": (b16(HEADS, rows, rows), hbm), "keep_f": (b16(rows, inner), hbm),
             "keep_g": (b16(rows, inner), hbm)}
    scratch = {
        "wall": v(BF16, 2, Z, X, C, total, width), "g1": v(BF16, Z, X, C, total, width),
        "q_s": v(BF16, 2, rows, width), "k_s": v(BF16, 2, rows, width), "v_s": v(BF16, 2, rows, width),
        "p_s": v(BF16, HEADS, rows, rows), "c_s": v(BF16, 2, rows, width),
        "xh1": v(F32, 2, rows, width), "r1n": v(F32, 2, rows, 1), "n1": v(BF16, 2, rows, width),
        "f_s": v(BF16, rows, inner), "gp": v(BF16, rows, inner),
        "xh2": v(F32, 2, rows, width), "r2n": v(F32, 2, rows, 1), "y_s": v(F32, rows, width),
        "h_s": v(BF16, 3, rows, width), "oc": v(BF16, rows, width), "gin1": v(BF16, rows, width),
        "mrow": v(F32, 8, rows), "g_s": v(F32, rows, width), "go": v(BF16, rows, width), "gt": v(BF16, rows, width),
        "ds_s": v(BF16, 2, rows, rows), "gqkv": v(BF16, rows, 3 * width), "xt": v(BF16, width, rows),
        "cols": v(F32, rows, 8), "vec": v(F32, 2, 8, width), "bff": v(F32, 2, 1, inner),
        "sems": pltpu.SemaphoreType.DMA((6,)),
    }
    if grid:
        late = sum(REDUCE[k][1] for k in {k for ks in REDUCE_LATE.values() for k in ks}) * rp
        kg, kr = len(GATHER) + 1, len(REDUCE) + 1
        dma = pltpu.SemaphoreType.DMA
        scratch |= {
            "dvec": v(F32, 2, 8, width), "dbff": v(F32, 2, 1, inner), "dhw": v(F32, 1, width),
            "wsm": v(F32, 2, Z, X, C, 16, 128), "gsm": v(F32, 2, Z, X, C, 16, 128),
            "r1s": v(F32, 2, Z, X, 16, 128), "rxs": v(F32, 2, Z, 16, 128), "rzs": v(F32, 2, Z, 16, 128),
            "rys": v(F32, 16, 128),
            "r1": v(BF16, Z, X, total, width), "ry": v(BF16, Z, X, late, width),
            "rx": v(BF16, 2, Z, total, width), "rz": v(BF16, 2, Z, total, width), "rf": v(BF16, total, width),
            "gs": dma((2, kg, 6)), "gr": dma((2, kg, 6)), "rs_": dma((2, kr, 6)), "rr_": dma((2, kr, 6)),
            "os": dma((3,)), "orr": dma((3,)), "credit": pltpu.SemaphoreType.REGULAR((kr,)),
        }
    names = list(ins) + list(outs) + list(scratch)
    params = dict(vmem_limit_bytes=VMEM_BYTES)
    if grid:
        params |= dict(collective_id=0, has_side_effects=True)
    call = pl.pallas_call(
        functools.partial(kernel, names, grid),
        out_shape=tuple(t[0] for t in outs.values()),
        in_specs=list(ins.values()),
        out_specs=tuple(t[1] for t in outs.values()),
        scratch_shapes=list(scratch.values()),
        compiler_params=pltpu.CompilerParams(**params),
    )
    return call, list(outs)


def pick_own(section, micro, rows, a):
    return lax.dynamic_index_in_dim(a.reshape((micro, rows) + a.shape[1:]), section, 0, keepdims=False)


def fused_local(grid, tokens_in, out_cot, term_cot, long_flag, token_mask, w_qkv, w_out, w_ff_in, w_ff_out, vectors,
                ff_bias, head_weight, head_bias):
    section = lax.axis_index("section")
    width = tokens_in.shape[1]
    micro = long_flag.shape[0]
    rows = tokens_in.shape[0] // micro
    own = functools.partial(pick_own, section, micro, rows)
    aux = jnp.stack([own(term_cot), own(token_mask).astype(F32)])
    flag = lax.dynamic_slice_in_dim(long_flag, section, 1)
    call, names = make_call(rows, width, w_ff_in.shape[2], vectors.shape[2], ff_bias.shape[1], grid)
    res = dict(zip(names, call(flag, head_bias, tokens_in, out_cot, aux, head_weight[None], w_qkv, w_out, w_ff_in,
                               w_ff_out, vectors, ff_bias)))
    small = res["d_small"]
    heads = width // 128
    return (
        res["act_out"][None], res["term"].reshape(-1).astype(BF16), res["gin_out"][None],
        res["d_wq"], res["d_wo"], res["d_wi"], res["d_wf"],
        small[None, 0:8, 0 : vectors.shape[2]], small[8:9, 0 : ff_bias.shape[1]],
        small[9 : 9 + heads].reshape(width), small[9 + heads, 0:1],
    )


def plain_local(tokens_in, out_cot, term_cot, long_flag, token_mask, w_qkv, w_out, w_ff_in, w_ff_out, vectors, ff_bias,
                head_weight, head_bias):
    section = lax.axis_index("section")
    width = tokens_in.shape[1]
    micro = long_flag.shape[0]
    rows = tokens_in.shape[0] // micro
    inner = w_ff_in.shape[2]
    own = functools.partial(pick_own, section, micro, rows)
    everyone = lambda a, ax: lax.all_gather(lax.all_gather(a, "dp", axis=ax, tiled=True), "section", axis=0, tiled=True)
    wq, wo, wi, wf = (everyone(a, 1) for a in (w_qkv, w_out, w_ff_in, w_ff_out))
    vec = everyone(vectors, 2).astype(F32)
    bff = everyone(ff_bias, 1).astype(F32)[:, None]
    cut = lambda a: a.reshape(2, width, -1, width).transpose(0, 2, 1, 3).reshape(2, -1, width)
    wall = jnp.concatenate([cut(wq), wo, cut(wi), wf], 1)[:, None, None, None]
    aux = jnp.stack([own(term_cot), own(token_mask).astype(F32)])
    flag = lax.dynamic_slice_in_dim(long_flag, section, 1)
    call, names = make_call(rows, width, inner, width, inner, None)
    res = dict(zip(names, call(flag, head_bias, own(tokens_in), own(out_cot), aux, head_weight[None], wall, vec, bff)))
    swap = lambda a: lax.all_gather(a, "section", axis=1, tiled=True)[section][None]
    terms = lax.all_gather(res["term"][0], "section", axis=0, tiled=True).astype(BF16)

    def scatter(a, ax):
        a = lax.psum_scatter(a.astype(F32), "section", scatter_dimension=0, tiled=True)
        return lax.psum_scatter(a, "dp", scatter_dimension=ax, tiled=True)

    g = res["g_out"][:, 0, 0, 0]
    glue = lambda a, n: a.reshape(2, n, width, width).transpose(0, 2, 1, 3).reshape(2, width, n * width)
    dhw, dhb = lax.psum((res["dhw"][0], res["dhb"][0]), ("section", "dp"))
    return (
        swap(res["act_out"]), terms, swap(res["gin_out"]),
        scatter(glue(g[:, : 3 * width], 3), 1), scatter(g[:, 3 * width : 4 * width], 1),
        scatter(glue(g[:, 4 * width : 8 * width], 4), 1), scatter(g[:, 8 * width :], 1),
        scatter(res["dvec"], 2), scatter(res["dbff"][:, 0], 1), dhw, dhb,
    )


def solution(mesh):
    dp = mesh.shape["dp"]
    if dp == 16:
        local = functools.partial(fused_local, (4, 2, 2))
    else:
        local = plain_local
    shard = P("section", "dp", None)
    in_specs = (P("dp", None), P("dp", None), P("dp"), P("dp"), P("dp"), shard, shard, shard, shard,
                P("section", None, "dp"), P("section", "dp"), P(), P())
    out_specs = (shard, P("dp"), shard, shard, shard, shard, shard, P("section", None, "dp"), P("section", "dp"),
                 P(), P())
    return jax.shard_map(local, mesh=mesh, in_specs=in_specs, out_specs=out_specs, check_vma=False)
```

```python
import functools
import types

import jax
import jax.numpy as jnp
from jax import lax
from jax.experimental import pallas as pl
from jax.experimental.pallas import tpu as pltpu
from jax.sharding import PartitionSpec as P

RUN = 128
HEADS = 8
EPS = 1e-12
F32, BF16 = jnp.float32, jnp.bfloat16
VMEM_BYTES = 64 * 2**20


def dot(a, b):
    return lax.dot_general(a, b, (((1,), (0,)), ((), ())), preferred_element_type=F32)


def dot_nt(a, b):
    return lax.dot_general(a, b, (((1,), (1,)), ((), ())), preferred_element_type=F32)


def dot_tn(a, b):
    return lax.dot_general(a, b, (((0,), (0,)), ((), ())), preferred_element_type=F32)


def rows8(v):
    return jnp.sum(v.reshape(-1, 8, v.shape[1]), axis=0)


def gelu_both(u):
    e = jnp.exp(u * u * -0.5)
    d = jnp.abs(u) * (0.3275911 * 0.7071067811865476) + 1.0
    t = pl.reciprocal(d, approx=True)
    t = t * (2.0 - d * t)
    q = t * 0.5307027145 - 0.7265760135
    q = q * t + 0.7107068705
    q = q * t - 0.142248368
    q = q * t + 0.127414796
    q = q * t * e
    cdf = jnp.where(u >= 0.0, 1.0 - q, q)
    return u * cdf, cdf + u * (e * 0.3989422804014327)


def layer_norm_rows(y):
    c = y - jnp.mean(y, -1, keepdims=True)
    r = lax.rsqrt(jnp.mean(c * c, -1, keepdims=True) + EPS)
    return c * r, r


def layer_norm_back(g, gain, xh, r):
    gx = g * gain
    a = jnp.mean(gx, -1, keepdims=True)
    b = jnp.mean(gx * xh, -1, keepdims=True)
    return (gx - a - xh * b) * r


MESH = pl.DeviceIdType.MESH
PARTS = 12
GATHER = ((0, 1), (1, 1), (2, 1), (3, 1), (4, 1), (5, 1), (6, 1), (7, 1), (8, 1), (9, 1), (10, 1), (11, 1))
GATHER_ROUTE = (("own", "own", "other", "own", "own", "both", "own", "both", "other", "other", "other", "both"), ("both", "own", "other", "both", "own", "both", "own", "both", "other", "own", "other", "other"))
REDUCE = ((0, 1), (1, 1), (2, 1), (3, 1), (4, 1), (5, 1), (6, 1), (7, 1), (8, 1), (9, 1), (10, 1), (11, 1))
REDUCE_ROUTE = (("both", "both", "both", "both", "other", "both", "both", "both", "other", "both", "own", "own"), ("own", "other", "both", "other", "other", "other", "both", "other", "own", "own", "other", "other"))


def late_place(l, k):
    takes = lambda a, b: a if REDUCE_ROUTE[a][b] == "own" else 1 - a
    at = 0
    for a in range(2):
        for b, (_, n) in enumerate(REDUCE):
            if (a, b) == (l, k):
                return at, n
            if REDUCE_ROUTE[a][b] != "both" and takes(a, b) == takes(l, k):
                at += n
    return at, 0


def late_parts():
    ends = [sum(late_place(l, k)) for l in range(2) for k in range(len(REDUCE)) if REDUCE_ROUTE[l][k] != "both"]
    return max(ends, default=1)


def layer_steps(l):
    return (
        (("restore", 0),) if l else ()) + (
        ("qkv", l), ("attend", l, 0, 4), ("project", l)) + (
        (("restore", 1), ("restore", 2)) if l else ()) + (
        ("ff_in", l, 0, 8), ("ff_out", l))


def layer_back_steps(l):
    return (
        () if l else (("reload", 0), ("reload", 1), ("reload", 2))) + (
        ("top_back", l), ("ff_out_grad", l), ("ff_back", l, 0, 8), ("mid", l), ("project_back", l),
        ("attend_back", l, 0, 4), ("qkv_back", l), ("qkv_grad", l))


PLAIN_STEPS = layer_steps(0) + layer_steps(1) + (("head",),) + layer_back_steps(1) + layer_back_steps(0)


FUSED_STEPS = (
    ("exchange", (
        ("gy", 0, 12), ("gy", 0, 8), ("gy", 0, 7), ("gy", 0, 2), ("gy", 0, 5), ("gz", 0, 12), ("gz", 0, 0),
        ("gy", 0, 9), ("gy", 0, 10), ("gz", 1, 12), ("gy", 0, 11), ("gx", 0, 12), ("gz", 0, 1), ("gc", 0, 12),
        ("gx", 0, 0), ("gz", 0, 3), ("gd", 0, 12),
    ), (
        ("gy", 1, 12), ("gy", 1, 2), ("gy", 1, 11), ("gy", 1, 5), ("gy", 1, 3), ("gz", 1, 12), ("gz", 1, 1),
        ("gy", 1, 10), ("gy", 1, 0), ("gz", 0, 12), ("gy", 1, 8), ("gx", 1, 12), ("gz", 0, 7), ("gy", 1, 7),
        ("gc", 1, 12), ("gx", 1, 1), ("gz", 0, 2), ("gd", 1, 12), ("gx", 0, 12), ("gz", 0, 10), ("gx", 0, 7),
        ("gc", 1, 1), ("gc", 0, 12), ("gd", 1, 1), ("gd", 0, 12),
    )),
    ("small_weights", 0),
    ("exchange", (
        ("gx", 1, 12), ("gz", 0, 7), ("gx", 0, 1), ("gc", 0, 0), ("gc", 1, 12), ("gd", 0, 0), ("gd", 1, 12),
        ("gz", 0, 6), ("gx", 0, 3), ("gc", 0, 1), ("gz", 0, 5), ("gd", 0, 1), ("gx", 0, 7), ("gc", 0, 3),
        ("gc", 1, 1), ("gz", 1, 0), ("gd", 0, 3), ("gx", 0, 6), ("gd", 1, 1), ("gc", 0, 7), ("gz", 0, 4),
        ("gd", 0, 7), ("gx", 0, 5), ("gc", 0, 6), ("gc", 0, 2), ("gz", 1, 2), ("gd", 0, 6), ("gx", 1, 0),
        ("gc", 0, 5), ("gd", 0, 2),
    ), (
        ("gz", 0, 5), ("gx", 0, 2), ("gc", 0, 7), ("gz", 0, 8), ("gd", 0, 7), ("gx", 0, 10), ("gc", 0, 2),
        ("gc", 0, 0), ("gz", 0, 9), ("gx", 0, 5), ("gd", 0, 2), ("gd", 0, 0), ("gc", 0, 10), ("gz", 1, 4),
        ("gx", 0, 8), ("gd", 0, 10), ("gc", 0, 5), ("gc", 0, 1), ("gz", 1, 6), ("gx", 0, 9), ("gd", 0, 5),
        ("gd", 0, 1),
    )),
    ("qkv", 0),
    ("exchange", (
        ("gz", 1, 11), ("gd", 0, 5), ("gx", 0, 4),
    ), (
        ("gc", 0, 8),
    )),
    ("attend", 0, 0, 1),
    ("exchange", (
        ("gc", 1, 0),
    ), (
        ("gx", 1, 4), ("gc", 0, 9), ("gz", 1, 5), ("gc", 0, 3), ("gd", 0, 8),
    )),
    ("attend", 0, 1, 2),
    ("exchange", (
        ("gx", 1, 2), ("gc", 0, 4), ("gc", 0, 10), ("gz", 0, 11), ("gd", 1, 0),
    ), (
        ("gx", 1, 6), ("gz", 1, 3), ("gd", 0, 3), ("gd", 0, 9),
    )),
    ("attend", 0, 2, 3),
    ("exchange", (
        ("gx", 1, 11), ("gz", 1, 10), ("gd", 0, 4), ("gd", 0, 10),
    ), (
        ("gx", 1, 5), ("gc", 1, 4), ("gz", 0, 11),
    )),
    ("attend", 0, 3, 4),
    ("exchange", (
        ("gx", 0, 11), ("gc", 0, 8), ("gc", 1, 2), ("gz", 1, 5),
    ), (
        ("gx", 1, 3), ("gc", 0, 6), ("gc", 1, 6), ("gz", 1, 0), ("gd", 1, 4),
    )),
    ("project", 0),
    ("exchange", (
        ("gx", 1, 10), ("gc", 1, 11), ("gz", 1, 7), ("gd", 0, 8), ("gd", 1, 2),
    ), (
        ("gc", 1, 5), ("gx", 0, 11), ("gz", 1, 9), ("gd", 0, 6), ("gd", 1, 6), ("gd", 1, 5), ("gc", 0, 4),
        ("gc", 1, 3), ("gz", 1, 7), ("gx", 1, 0), ("gd", 0, 4),
    )),
    ("ff_in", 0, 0, 2),
    ("exchange", (
        ("gc", 0, 9), ("gd", 1, 11),
    ), (
        ("gd", 1, 3),
    )),
    ("ff_in", 0, 2, 4),
    ("exchange", (
        ("gx", 1, 5), ("gc", 0, 11), ("gz", 1, 3), ("gd", 0, 9),
    ), (
        ("gx", 1, 9), ("gc", 0, 11),
    )),
    ("ff_in", 0, 4, 6),
    ("exchange", (
        ("gx", 1, 7), ("gc", 1, 10), ("gz", 1, 8), ("gd", 0, 11),
    ), (
        ("gc", 1, 2), ("gd", 0, 11), ("gc", 1, 0),
    )),
    ("ff_in", 0, 6, 8),
    ("exchange", (
        ("gc", 1, 4), ("gd", 1, 10),
    ), (
        ("gx", 1, 7), ("gd", 1, 2),
    )),
    ("ff_out", 0),
    ("exchange", (
        ("gx", 1, 3), ("gc", 1, 5), ("gd", 1, 4),
    ), (
        ("gc", 1, 9), ("gd", 1, 0),
    )),
    ("small_weights", 1),
    ("restore", 0),
    ("qkv", 1),
    ("exchange", (
        ("gx", 1, 8), ("gc", 1, 7), ("gd", 1, 5),
    ), (
        ("gc", 1, 11), ("gc", 1, 7), ("gd", 1, 9),
    )),
    ("attend", 1, 0, 1),
    ("exchange", (
        ("gc", 1, 6), ("gc", 1, 3), ("gd", 1, 7),
    ), (
        ("gd", 1, 11), ("gd", 1, 7),
    )),
    ("attend", 1, 1, 2),
    ("exchange", (
        ("gd", 1, 6), ("gd", 1, 3),
    ), (
    )),
    ("attend", 1, 2, 3),
    ("exchange", (
        ("gc", 1, 8), ("gc", 1, 9),
    ), (
        ("gc", 1, 10),
    )),
    ("attend", 1, 3, 4),
    ("exchange", (
        ("gd", 1, 9), ("gd", 1, 8),
    ), (
        ("gd", 1, 10),
    )),
    ("project", 1),
    ("restore", 1),
    ("restore", 2),
    ("ff_in", 1, 0, 2),
    ("ff_in", 1, 2, 4),
    ("exchange", (
    ), (
        ("gc", 1, 8),
    )),
    ("ff_in", 1, 4, 6),
    ("ff_in", 1, 6, 8),
    ("exchange", (
    ), (
        ("gd", 1, 8),
    )),
    ("ff_out", 1),
    ("head",),
    ("send_acts",),
    ("top_back", 1),
    ("ff_out_grad", 1),
    ("exchange", (
        ("rc", 1, 9), ("rc", 1, 11), ("rc", 1, 10), ("rc", 1, 8),
    ), (
        ("rc", 1, 9), ("rc", 1, 11), ("rc", 1, 10), ("rc", 1, 8),
    )),
    ("ff_back", 1, 0, 2),
    ("exchange", (
        ("r1", 1, 9), ("r1", 1, 11), ("r1", 1, 10), ("r1", 1, 8), ("rc", 1, 4),
    ), (
        ("r1", 1, 9), ("r1", 1, 11), ("r1", 1, 10), ("r1", 1, 8), ("rc", 1, 4),
    )),
    ("ff_back", 1, 2, 4),
    ("exchange", (
        ("r1", 1, 4), ("rc", 1, 5),
    ), (
        ("r1", 1, 4), ("rc", 1, 5),
    )),
    ("ff_back", 1, 4, 6),
    ("exchange", (
        ("r1", 1, 5), ("rc", 1, 6),
    ), (
        ("r1", 1, 5), ("rc", 1, 6),
    )),
    ("ff_back", 1, 6, 8),
    ("exchange", (
        ("r1", 1, 6), ("rc", 1, 7),
    ), (
        ("r1", 1, 6), ("rc", 1, 7),
    )),
    ("mid", 1),
    ("exchange", (
        ("r1", 1, 7),
    ), (
        ("r1", 1, 7),
    )),
    ("project_back", 1),
    ("exchange", (
        ("rc", 1, 3),
    ), (
        ("rc", 1, 3),
    )),
    ("attend_back", 1, 0, 1),
    ("exchange", (
        ("r2", 1, 6), ("r1", 1, 3), ("ry", 1, 11),
    ), (
        ("r2", 1, 6), ("ry", 1, 9), ("r1", 1, 3),
    )),
    ("attend_back", 1, 1, 2),
    ("attend_back", 1, 2, 3),
    ("exchange", (
        ("r3", 1, 6), ("r2", 1, 11),
    ), (
        ("r3", 1, 6), ("r2", 1, 9), ("ry", 1, 8),
    )),
    ("attend_back", 1, 3, 4),
    ("exchange", (
        ("ry", 1, 10),
    ), (
        ("r4", 1, 6),
    )),
    ("qkv_grad", 1),
    ("exchange", (
        ("rc", 1, 1), ("rc", 1, 2), ("rc", 1, 0), ("r3", 1, 11),
    ), (
        ("rc", 1, 1), ("rc", 1, 2), ("r3", 1, 9), ("rc", 1, 0), ("r2", 1, 8),
    )),
    ("qkv_back", 1),
    ("exchange", (
        ("r1", 1, 1), ("r1", 1, 2), ("r2", 1, 10), ("ry", 1, 4), ("r1", 1, 0),
    ), (
        ("r4", 1, 11), ("r1", 1, 1), ("r1", 1, 2), ("r1", 1, 0),
    )),
    ("send_grad", 1),
    ("small_grads", 1),
    ("exchange", (
        ("rc", 1, 12),
    ), (
        ("rc", 1, 12),
    )),
    ("reload", 1),
    ("reload", 2),
    ("exchange", (
        ("ge", 0), ("ge", 1),
    ), (
        ("ge", 0), ("ge", 1),
    )),
    ("top_back", 0),
    ("exchange", (
        ("r1", 1, 12),
    ), (
        ("r3", 1, 8), ("r1", 1, 12),
    )),
    ("ff_out_grad", 0),
    ("exchange", (
        ("r3", 1, 10), ("r2", 1, 2), ("ry", 1, 5), ("rc", 0, 8), ("rc", 0, 10), ("rc", 0, 11), ("rc", 0, 9),
    ), (
        ("r2", 1, 2), ("r2", 1, 12), ("rc", 0, 8), ("rc", 0, 10), ("rc", 0, 11), ("rc", 0, 9),
    )),
    ("ff_back", 0, 0, 2),
    ("exchange", (
        ("r2", 1, 4), ("r2", 1, 12), ("r1", 0, 8), ("r1", 0, 10), ("r1", 0, 11), ("r1", 0, 9), ("rc", 0, 4),
        ("r3", 1, 2),
    ), (
        ("ry", 1, 0), ("r1", 0, 8), ("r1", 0, 10), ("r1", 0, 11), ("r1", 0, 9), ("rc", 0, 4),
    )),
    ("ff_back", 0, 2, 4),
    ("exchange", (
        ("r2", 1, 5), ("ry", 1, 7), ("r1", 0, 4), ("rc", 0, 5), ("r3", 1, 4),
    ), (
        ("r3", 1, 2), ("r3", 1, 12), ("r1", 0, 4), ("rc", 0, 5),
    )),
    ("ff_back", 0, 4, 6),
    ("exchange", (
        ("r3", 1, 12), ("r2", 0, 9), ("r1", 0, 5), ("rc", 0, 6),
    ), (
        ("r2", 1, 0), ("r1", 0, 5), ("rc", 0, 6),
    )),
    ("ff_back", 0, 6, 8),
    ("exchange", (
        ("r3", 1, 5), ("r2", 1, 7), ("ry", 1, 3), ("r1", 0, 6), ("rc", 0, 7),
    ), (
        ("r2", 0, 9), ("r1", 0, 6), ("rc", 0, 7),
    )),
    ("mid", 0),
    ("exchange", (
        ("r3", 0, 9), ("r2", 0, 5), ("r1", 0, 7),
    ), (
        ("r4", 1, 10), ("r3", 1, 0), ("r2", 0, 5), ("r1", 0, 7),
    )),
    ("project_back", 0),
    ("exchange", (
        ("r3", 1, 7), ("rc", 0, 3), ("r2", 1, 3), ("ry", 1, 1),
    ), (
        ("r3", 0, 9), ("rc", 0, 3), ("r2", 0, 6),
    )),
    ("reload", 0),
    ("attend_back", 0, 0, 1),
    ("exchange", (
        ("r3", 0, 5), ("r2", 0, 6), ("r1", 0, 3),
    ), (
        ("r1", 0, 3), ("r3", 0, 5), ("r2", 0, 7),
    )),
    ("attend_back", 0, 1, 2),
    ("exchange", (
        ("r3", 1, 3), ("r2", 0, 7), ("ry", 0, 10),
    ), (
        ("r4", 1, 2), ("ry", 0, 8), ("r3", 0, 6),
    )),
    ("attend_back", 0, 2, 3),
    ("exchange", (
        ("r3", 0, 6), ("r2", 1, 1),
    ), (
        ("r2", 0, 3),
    )),
    ("attend_back", 0, 3, 4),
    ("exchange", (
    ), (
        ("r3", 0, 7), ("r2", 0, 8), ("ry", 0, 4), ("r4", 1, 4), ("r4", 1, 12),
    )),
    ("qkv_grad", 0),
    ("exchange", (
        ("r3", 0, 7), ("r4", 0, 9), ("r2", 0, 3), ("ry", 0, 11), ("rc", 0, 0), ("r4", 0, 5), ("rc", 0, 2),
        ("rc", 0, 1),
    ), (
        ("r4", 1, 5), ("r4", 1, 7), ("r3", 0, 3), ("rc", 0, 0), ("r4", 1, 3), ("rc", 0, 2), ("rc", 0, 1),
    )),
    ("qkv_back", 0),
    ("exchange", (
        ("r4", 0, 7), ("r4", 0, 6), ("r3", 1, 1), ("r2", 0, 10), ("r1", 0, 0), ("r1", 0, 2), ("r1", 0, 1),
    ), (
        ("r2", 0, 4), ("r3", 0, 8), ("r1", 0, 0), ("r1", 0, 2), ("r1", 0, 1),
    )),
    ("send_grad", 0),
    ("small_grads", 0),
    ("exchange", (
        ("r4", 0, 8), ("r3", 0, 3), ("r4", 0, 3), ("r2", 0, 11), ("rc", 0, 12), ("r1", 0, 12), ("r3", 0, 10),
        ("r2", 0, 0), ("r3", 0, 11), ("r2", 0, 2), ("r3", 0, 0), ("r2", 0, 1), ("r2", 0, 12), ("r3", 0, 2),
        ("r4", 0, 4), ("r4", 0, 0), ("r4", 0, 2), ("r3", 0, 1), ("r4", 0, 1), ("r3", 0, 12), ("r4", 0, 12),
    ), (
        ("rc", 0, 12), ("r4", 1, 1), ("r1", 0, 12), ("r3", 0, 4), ("r2", 0, 0), ("r2", 0, 2), ("r3", 0, 0),
        ("r2", 0, 1), ("r2", 0, 12), ("r3", 0, 2), ("r3", 0, 1), ("r3", 0, 12),
    )),
    ("exchange", (
        ("re", 1), ("re", 0),
    ), (
        ("re", 1), ("re", 0),
    )),
)


class Exchange:
    def __init__(self, o, grid, rp):
        self.o, self.rp = o, rp
        self.Z, self.X, self.C = grid
        self.s = lax.axis_index("section")
        d = lax.axis_index("dp")
        self.c = lax.rem(d, 2)
        self.x = lax.rem(d // 2, 2)
        self.z = d // 4

    def dev(self, s=None, z=None, x=None, c=None):
        s = self.s if s is None else s
        z = self.z if z is None else z
        x = self.x if x is None else x
        c = self.c if c is None else c
        return (s, (z * 2 + x) * 2 + c)

    def along_z(self, j):
        return lax.rem(self.z + j + 1, self.Z)

    def barrier(self):
        b = pltpu.get_barrier_semaphore()
        peers = [self.dev(z=self.along_z(j)) for j in range(self.Z - 1)]
        peers += [self.dev(x=1 - self.x), self.dev(c=1 - self.c), self.dev(s=1 - self.s)]
        for p in peers:
            pl.semaphore_signal(b, inc=1, device_id=p, device_id_type=MESH)
        pl.semaphore_wait(b, len(peers))

    def copy(self, src, dst, send, recv, dev):
        return pltpu.make_async_remote_copy(
            src_ref=src, dst_ref=dst, send_sem=send, recv_sem=recv, device_id=dev, device_id_type=MESH)

    def g_route(self, l, k):
        return "both" if k == len(GATHER) else GATHER_ROUTE[l][k]

    def g_works(self, s, l, k):
        return self.g_route(l, k) in ("both", "own" if s == l else "other")

    def g_copy(self, kind, s, l, k, j=0):
        o = self.o
        z, x, c = self.z, self.x, self.c
        if k == len(GATHER):
            w, mine, rows = o.wsm.at[l], o.own_small, slice(None)
        else:
            p, n = GATHER[k]
            w, mine, rows = o.wall.at[l], o.own, slice(p * self.rp, (p + n) * self.rp)
        ss, rr = o.gs.at[l, k], o.gr.at[l, k]
        if kind == "z":
            a = w.at[z, x, c, rows]
            return self.copy(a, a, ss.at[j], rr.at[j], self.dev(z=self.along_z(j)))
        if kind == "x":
            a = w.at[:, x, c, rows]
            return self.copy(a, a, ss.at[3], rr.at[3], self.dev(x=1 - x))
        if kind == "shard":
            return self.copy(mine.at[rows], w.at[z, x, c, rows], ss.at[4], rr.at[4], self.dev(s=1 - s))
        a = w.at[:, :, c, rows]
        if kind == "plane":
            return self.copy(a, a, ss.at[4], rr.at[4], self.dev(s=1 - s))
        return self.copy(a, a, ss.at[5], rr.at[5], self.dev(c=1 - c))

    def gy(self, s, l, k):
        self.g_copy("shard", s, l, k).start()

    def gz(self, s, l, k):
        if s != l:
            self.g_copy("shard", s, l, k).wait_recv()
        for j in range(self.Z - 1):
            self.g_copy("z", s, l, k, j).start()

    def gx(self, s, l, k):
        for j in range(self.Z - 1):
            self.g_copy("z", s, l, k, j).wait_recv()
        self.g_copy("x", s, l, k).start()

    def gc(self, s, l, k):
        if self.g_works(s, l, k):
            self.g_copy("x", s, l, k).wait_recv()
            if self.g_route(l, k) != "both":
                self.g_copy("plane", s, l, k).start()
        else:
            self.g_copy("plane", s, l, k).wait_recv()
        self.g_copy("c", s, l, k).start()

    def gd(self, s, l, k):
        self.g_copy("c", s, l, k).wait_recv()

    def ge(self, s, l):
        for k in range(len(GATHER) + 1):
            route = self.g_route(l, k)
            if s == l and route != "own":
                self.g_copy("shard", s, l, k).wait_send()
            if self.g_works(s, l, k):
                for j in range(self.Z - 1):
                    self.g_copy("z", s, l, k, j).wait_send()
                self.g_copy("x", s, l, k).wait_send()
                if route != "both":
                    self.g_copy("plane", s, l, k).wait_send()
            self.g_copy("c", s, l, k).wait_send()

    def r_small(self, k):
        return k == len(REDUCE)

    def r_route(self, l, k):
        return "both" if self.r_small(k) else REDUCE_ROUTE[l][k]

    def r_works(self, s, l, k):
        return self.r_route(l, k) in ("both", "own" if s == l else "other")

    def r_bufs(self, l, k):
        o = self.o
        if self.r_small(k):
            return o.gsm.at[l], slice(None), o.r1s.at[l], o.rxs.at[l], o.rzs.at[l], o.rys
        p, n = REDUCE[k]
        g = o.g1 if l == 1 else o.wall.at[1]
        return g, slice(p * self.rp, (p + n) * self.rp), o.r1, o.rx.at[l], o.rz.at[l], o.rf

    def r_late(self, l, k):
        at, n = late_place(l, k)
        return slice(at * self.rp, (at + n) * self.rp)

    def r_copy(self, kind, s, l, k, j=0):
        o = self.o
        g, rows, r1, rx, rz, rf = self.r_bufs(l, k)
        z, x, c = self.z, self.x, self.c
        ss, rr = o.ss.at[l, k], o.sr.at[l, k]
        if kind == "c":
            return self.copy(g.at[:, :, 1 - c, rows], r1.at[:, :, rows], ss.at[0], rr.at[0], self.dev(c=1 - c))
        if kind == "x":
            return self.copy(g.at[:, 1 - x, c, rows], rx.at[:, rows], ss.at[1], rr.at[1], self.dev(x=1 - x))
        if kind == "z":
            to = self.along_z(j)
            return self.copy(g.at[to, x, c, rows], rz.at[z, rows], ss.at[2 + j], rr.at[2 + j], self.dev(z=to))
        if kind == "plane":
            return self.copy(g.at[:, :, c, rows], o.ry.at[:, :, self.r_late(l, k)], ss.at[5], rr.at[5],
                             self.dev(s=1 - s))
        return self.copy(g.at[z, x, c, rows], rf.at[rows], ss.at[5], rr.at[5], self.dev(s=1 - s))

    def add(self, n, dst, src):
        def one(i, _):
            d = dst(i)
            d[...] = d[...] + src(i)[...]
            return 0

        lax.fori_loop(0, n, one, 0)

    def rc(self, s, l, k):
        if l == 0 and not self.r_small(k):
            pl.semaphore_wait(self.o.credit.at[k], 1)
        self.r_copy("c", s, l, k).start()

    def r1(self, s, l, k):
        g, rows, r1, rx, rz, rf = self.r_bufs(l, k)
        c, X = self.c, self.X
        self.r_copy("c", s, l, k).wait_recv()
        self.add(self.Z * X, lambda i: g.at[i // X, lax.rem(i, X), c, rows], lambda i: r1.at[i // X, lax.rem(i, X), rows])
        if l == 1 and not self.r_small(k):
            pl.semaphore_signal(self.o.credit.at[k], inc=1, device_id=self.dev(c=1 - c), device_id_type=MESH)
        route = self.r_route(l, k)
        if route == "both":
            self.r_copy("x", s, l, k).start()
        elif not self.r_works(s, l, k):
            self.r_copy("plane", s, l, k).start()

    def ry(self, s, l, k):
        g, rows, r1, rx, rz, rf = self.r_bufs(l, k)
        c, X, late = self.c, self.X, self.r_late(l, k)
        self.r_copy("plane", s, l, k).wait_recv()
        self.add(self.Z * X, lambda i: g.at[i // X, lax.rem(i, X), c, rows],
                 lambda i: self.o.ry.at[i // X, lax.rem(i, X), late])
        self.r_copy("x", s, l, k).start()

    def r2(self, s, l, k):
        g, rows, r1, rx, rz, rf = self.r_bufs(l, k)
        x, c = self.x, self.c
        self.r_copy("x", s, l, k).wait_recv()
        self.add(self.Z, lambda i: g.at[i, x, c, rows], lambda i: rx.at[i, rows])
        for j in range(self.Z - 1):
            self.r_copy("z", s, l, k, j).start()

    def r3(self, s, l, k):
        g, rows, r1, rx, rz, rf = self.r_bufs(l, k)
        z, x, c = self.z, self.x, self.c
        for j in range(self.Z - 1):
            self.r_copy("z", s, l, k, j).wait_recv()
        rz[z, rows] = g[z, x, c, rows]
        total = rz[0, rows].astype(F32)
        for i in range(1, self.Z):
            total = total + rz[i, rows].astype(F32)
        if s == l and self.r_route(l, k) == "own":
            self.result(k, total)
        else:
            g[z, x, c, rows] = total.astype(g.dtype)
            if s != l:
                self.r_copy("shard", s, l, k).start()

    def r4(self, s, l, k):
        g, rows, r1, rx, rz, rf = self.r_bufs(l, k)
        self.r_copy("shard", s, l, k).wait_recv()
        total = rf[rows].astype(F32)
        if self.r_route(l, k) == "both":
            total = g[self.z, self.x, self.c, rows].astype(F32) + total
        self.result(k, total)

    def result(self, k, v):
        o, rp = self.o, self.rp
        if self.r_small(k):
            o.d_small[...] = v
            return
        p0, n = REDUCE[k]
        w = v.shape[1]
        for i in range(n):
            p, t = p0 + i, v[i * rp : (i + 1) * rp]
            if p < 3:
                o.d_wq[0, :, p * w : (p + 1) * w] = t
            elif p == 3:
                o.d_wo[0] = t
            elif p < 8:
                o.d_wi[0, :, (p - 4) * w : (p - 3) * w] = t
            else:
                o.d_wf[0, (p - 8) * rp : (p - 7) * rp, :] = t

    def re(self, s, l):
        for k in range(len(REDUCE) + 1):
            route, works = self.r_route(l, k), self.r_works(s, l, k)
            self.r_copy("c", s, l, k).wait_send()
            if works:
                self.r_copy("x", s, l, k).wait_send()
                for j in range(self.Z - 1):
                    self.r_copy("z", s, l, k, j).wait_send()
                if s != l:
                    self.r_copy("shard", s, l, k).wait_send()
            else:
                self.r_copy("plane", s, l, k).wait_send()


def kernel(names, grid, *refs):
    o = types.SimpleNamespace(**dict(zip(names, refs)))
    fused = grid is not None
    W = o.h_s.shape[2]
    FF = o.f_s.shape[1]
    Z, X, C, total = o.wall.shape[1:5]
    rp = total // PARTS
    flag, hb, hw, wall, g1 = o.flag, o.hb, o.hw, o.wall, o.g1
    q_s, k_s, v_s, p_s, c_s, xh1, r1, n1 = o.q_s, o.k_s, o.v_s, o.p_s, o.c_s, o.xh1, o.r1n, o.n1
    f_s, gp, xh2, r2, y_s, h_s, oc = o.f_s, o.gp, o.xh2, o.r2n, o.y_s, o.h_s, o.oc
    gin1, mrow, g_s, go, gt, ds_s, gqkv, xt, cols = o.gin1, o.mrow, o.g_s, o.go, o.gt, o.ds_s, o.gqkv, o.xt, o.cols
    vec, bff, dvec, dbff, sems = o.vec, o.bff, o.dvec, o.dbff, o.sems
    tc, mask = o.aux[0:1, :], o.aux[1:2, :]

    if fused:
        ex = Exchange(o, grid, rp)
        s, z, x, c = ex.s, ex.z, ex.x, ex.c
        R = h_s.shape[1]
        cin = [pltpu.make_async_copy(o.x_in.at[pl.ds(pl.multiple_of(s * R, R), R)], h_s.at[0], sems.at[0]),
               pltpu.make_async_copy(o.oc_in.at[pl.ds(pl.multiple_of(s * R, R), R)], oc, sems.at[1])]
        for t in cin:
            t.start()
        for i in range(3):
            o.own[i * rp : (i + 1) * rp, :] = o.wq_in[0, :, i * W : (i + 1) * W]
        o.own[3 * rp : 4 * rp, :] = o.wo_in[0]
        for i in range(4):
            o.own[(4 + i) * rp : (5 + i) * rp, :] = o.wi_in[0, :, i * W : (i + 1) * W]
        o.own[8 * rp :, :] = o.wf_in[0]
        wall[s, z, x, c] = o.own[...]
        nv, nb = o.vec_in.shape[2], o.bff_in.shape[1]
        o.own_small[...] = jnp.zeros(o.own_small.shape, F32)
        o.own_small[0:8, 0:nv] = o.vec_in[0].astype(F32)
        o.own_small[8:9, 0:nb] = o.bff_in[...].astype(F32)
        o.wsm[s, z, x, c] = o.own_small[...]
        ex.barrier()
    else:
        cin = [pltpu.make_async_copy(o.x_in, h_s.at[0], sems.at[0]),
               pltpu.make_async_copy(o.oc_in, oc, sems.at[1]),
               pltpu.make_async_copy(o.w_in, wall, sems.at[2])]
        for t in cin:
            t.start()
        vec[...] = o.vec_in[...]
        bff[...] = o.bff_in[...]

    for t in cin:
        t.wait()

    lane = lax.broadcasted_iota(jnp.int32, (W, 128), 1)
    sides4 = ((lane < 64).astype(F32).astype(BF16), (lane >= 64).astype(F32).astype(BF16))
    sides = tuple(t[:RUN] for t in sides4)

    valid = mask > 0.0
    key_run = lax.broadcasted_iota(jnp.int32, (1, W), 1) // RUN
    for r in range(4):
        ok = valid & ((key_run == r) | (flag[0] == 1))
        mrow[r : r + 1, :] = jnp.where(ok, 0.0, -1e9)

    def small_weights(l):
        for i in range(Z * X * C):
            b = o.wsm.at[l, i // (X * C), (i // C) % X, i % C]
            vec[l, :, i * nv : (i + 1) * nv] = b[0:8, 0:nv]
            bff[l, 0:1, i * nb : (i + 1) * nb] = b[8:9, 0:nb]

    def part(l, p, cs=slice(None)):
        a = wall[l, :, :, :, pl.ds(pl.multiple_of(p * rp, rp), rp), cs]
        return a.reshape(W, a.shape[-1])

    def part_rows(l, p, r0, n):
        if C == 1:
            return wall[l, 0, 0, 0, pl.ds(pl.multiple_of(p * rp + r0, n), n), :]
        k = n // (X * C * rp)
        return wall[l, pl.ds(r0 // (X * C * rp), k), :, :, pl.ds(pl.multiple_of(p * rp, rp), rp), :].reshape(n, W)

    def back_w(l, cs):
        a = wall[l, :, :, :, 8 * rp :, cs]
        return a.reshape(FF, a.shape[-1])

    def back_rows(l, j, n):
        if C == 1:
            return wall[l, 0, 0, 0, pl.ds(pl.multiple_of(8 * rp + j * n, n), n), :]
        return wall[l, j // X, lax.rem(j, X), :, 8 * rp :, :].reshape(n, W)

    def g_ref(l):
        return g1 if l == 1 else wall.at[1]

    def put_part(l, p, cs, val):
        rows = pl.ds(pl.multiple_of(p * rp, rp), rp)
        g_ref(l)[:, :, :, rows, cs] = val.reshape(Z, X, C, rp, -1).astype(BF16)

    def put_back(l, j, val):
        n = val.shape[0]
        if C == 1:
            g_ref(l)[0, 0, 0, pl.ds(pl.multiple_of(8 * rp + j * n, n), n), :] = val.astype(BF16)
        else:
            g_ref(l)[j // X, lax.rem(j, X), :, 8 * rp :, :] = val.reshape(C, 4 * rp, W).astype(BF16)

    def vrow(l, i):
        return vec[l, i : i + 1, :]

    def keep(src, dst, i):
        return pltpu.make_async_copy(src, dst, sems.at[i])

    def qkv(l):
        h = h_s.at[l]

        def step(j, _):
            cs = pl.ds(pl.multiple_of(j * 256, 256), 256)
            hv = h[...]
            rq = dot(hv, part(l, 0, cs)) + vec[l, 0:1, cs]
            q_s[l, :, cs] = (rq.astype(BF16).astype(F32) * 0.125).astype(BF16)
            k_s[l, :, cs] = dot(hv, part(l, 1, cs)).astype(BF16)
            v_s[l, :, cs] = (dot(hv, part(l, 2, cs)) + vec[l, 1:2, cs]).astype(BF16)
            return 0

        lax.fori_loop(0, 2, step, 0)

    def attend(l, p0, p1):
        def pair(p, _):
            cs = pl.ds(pl.multiple_of(p * 128, 128), 128)
            k2 = k_s[l, :, cs]
            v2 = v_s[l, :, cs]
            vh = [v2 * t for t in sides4]
            for r in range(4):
                rs = slice(r * RUN, (r + 1) * RUN)
                q2 = q_s[l, rs, cs]
                acc = None
                for t in range(2):
                    raw = dot_nt(q2 * sides[t], k2) + mrow[r : r + 1, :]
                    e = jnp.exp(raw - jnp.max(raw, -1, keepdims=True))
                    pr = (e * (1.0 / jnp.sum(e, -1, keepdims=True))).astype(BF16)
                    p_s[2 * p + t, rs, :] = pr
                    d = dot(pr, vh[t])
                    acc = d if acc is None else acc + d
                c_s[l, rs, cs] = acc.astype(BF16)
            return 0

        lax.fori_loop(p0, p1, pair, 0)
        if l == 0 and p1 == 4:
            keep(p_s, o.keep_p, 3).start()

    def project(l):
        def step(j, _):
            rs = pl.ds(pl.multiple_of(j * 256, 256), 256)
            y = h_s[l, rs, :].astype(F32) + dot(c_s[l, rs, :], part(l, 3)) + vrow(l, 2)
            xh, r = layer_norm_rows(y)
            xh1[l, rs, :] = xh
            r1[l, rs, :] = r
            n1[l, rs, :] = (xh * vrow(l, 3) + vrow(l, 4)).astype(BF16)
            return 0

        lax.fori_loop(0, 2, step, 0)

    def ff_in(l, j0, j1):
        def step(j, _):
            cs = pl.ds(pl.multiple_of(j * 256, 256), 256)
            sub = pl.ds(pl.multiple_of(lax.rem(j, 2) * 256, 256), 256)
            u = dot(n1[l], part(l, 4 + j // 2, sub)) + bff[l, 0:1, cs]
            f, d = gelu_both(u)
            f_s[:, cs] = f.astype(BF16)
            gp[:, cs] = d.astype(BF16)
            return 0

        lax.fori_loop(j0, j1, step, 0)

    def ff_out(l):
        def step(j, _):
            cs = pl.ds(pl.multiple_of(j * 256, 256), 256)
            y_s[:, cs] = dot(f_s[...], back_w(l, cs))
            return 0

        lax.fori_loop(0, 2, step, 0)
        if l == 0:
            keep(f_s, o.keep_f, 4).start()
            keep(gp, o.keep_g, 5).start()

        def top(j, _):
            rs = pl.ds(pl.multiple_of(j * RUN, RUN), RUN)
            y = xh1[l, rs, :] * vrow(l, 3) + vrow(l, 4) + y_s[rs, :] + vrow(l, 5)
            xh, r = layer_norm_rows(y)
            xh2[l, rs, :] = xh
            r2[l, rs, :] = r
            h_s[l + 1, rs, :] = (xh * vrow(l, 6) + vrow(l, 7)).astype(BF16)
            return 0

        lax.fori_loop(0, 4, top, 0)

    spilled = ((p_s, o.keep_p, 3), (f_s, o.keep_f, 4), (gp, o.keep_g, 5))

    def restore(i):
        src, dst, at = spilled[i]
        keep(src, dst, at).wait()

    def reload(i):
        src, dst, at = spilled[i]
        keep(dst, src, at).wait()

    act1 = h_s.at[2]

    def head():
        hw16 = jnp.broadcast_to(hw[...], (16, W))
        zr = dot_nt(hw16, act1[...])[0:1] + hb[0]
        ez = jnp.exp(-jnp.abs(zr))
        terms = jnp.log1p(ez) + jnp.maximum(zr, 0.0)
        sig = jnp.where(zr >= 0.0, 1.0, ez) / (1.0 + ez)
        gz = tc * mask * sig
        o.dhb[...] = jnp.sum(gz, -1, keepdims=True)
        sub8 = lax.broadcasted_iota(jnp.int32, (8, W), 0)
        cols[...] = jnp.where(sub8 == 0, gz, jnp.where(sub8 == 1, mask, 0.0)).T
        if fused:
            o.term[s] = terms
        else:
            o.term[...] = terms

    if fused:
        own_rows = pl.ds(pl.multiple_of(s * R, R), R)
        across = ex.dev(s=1 - s)
        send_act = ex.copy(h_s.at[2 - s], o.act_out.at[own_rows], o.os.at[0], o.orr.at[0], across)
        send_term = ex.copy(o.term.at[s], o.term.at[s], o.os.at[1], o.orr.at[1], across)
        own_act = pltpu.make_async_copy(h_s.at[1 + s], o.act_out.at[own_rows], sems.at[0])
        send_g = [ex.copy(g, o.gin_out.at[own_rows], o.os.at[2], o.orr.at[2], across) for g in (oc, gin1)]
        own_g = [pltpu.make_async_copy(g, o.gin_out.at[own_rows], sems.at[1]) for g in (oc, gin1)]

    def send_acts():
        send_act.start()
        send_term.start()
        own_act.start()

    def send_grad(i):
        pl.when(s != i)(send_g[i].start)
        pl.when(s == i)(own_g[i].start)

    def top_back(l):
        zero = jnp.zeros((8, W), F32)

        def step(j, carry):
            sg, ss, sb, sh = carry
            rs = pl.ds(pl.multiple_of(j * RUN, RUN), RUN)
            if l == 1:
                gzc = cols[rs, 0:1]
                g = oc[rs, :].astype(F32) * cols[rs, 1:2] + gzc * hw[...].astype(F32)
                sh = sh + rows8(gzc * act1[rs, :].astype(F32))
            else:
                g = gin1[rs, :].astype(F32)
            xh = xh2[l, rs, :]
            sg = sg + rows8(g * xh)
            ss = ss + rows8(g)
            gy = layer_norm_back(g, vrow(l, 6), xh, r2[l, rs, :])
            g_s[rs, :] = gy
            gl = gy.astype(BF16)
            go[rs, :] = gl
            sb = sb + rows8(gl.astype(F32))
            return sg, ss, sb, sh

        sg, ss, sb, sh = lax.fori_loop(0, 4, step, (zero,) * 4)
        dvec[l, 6:7, :] = jnp.sum(sg, 0, keepdims=True)
        dvec[l, 7:8, :] = jnp.sum(ss, 0, keepdims=True)
        dvec[l, 5:6, :] = jnp.sum(sb, 0, keepdims=True)
        if l == 1:
            o.dhw[...] = jnp.sum(sh, 0, keepdims=True)
            xt[...] = n1[l].T
        else:
            xt[...] = n1[l].T

    def ff_out_grad(l):
        def step(j, _):
            cs = pl.ds(pl.multiple_of(j * 256, 256), 256)
            put_back(l, j, dot_tn(f_s[:, cs], go[...]))
            return 0

        lax.fori_loop(0, FF // 256, step, 0)

    def ff_back(l, j0, j1):
        def step(j, _):
            cs = pl.ds(pl.multiple_of(j * 256, 256), 256)
            gf = dot_nt(go[...], back_rows(l, j, 256)) * gp[:, cs].astype(F32)
            gul = gf.astype(BF16)
            f_s[:, cs] = gul
            dbff[l, 0:1, cs] = jnp.sum(rows8(gul.astype(F32)), 0, keepdims=True)
            sub = pl.ds(pl.multiple_of(lax.rem(j, 2) * 256, 256), 256)
            put_part(l, 4 + j // 2, sub, dot(xt[...], gul))
            return 0

        lax.fori_loop(j0, j1, step, 0)

    def mid(l):
        def step(j, _):
            cs = pl.ds(pl.multiple_of(j * 256, 256), 256)
            acc = None
            for p in range(4):
                d = dot_nt(f_s[:, p * W : (p + 1) * W], part_rows(l, 4 + p, j * 256, 256))
                acc = d if acc is None else acc + d
            y_s[:, cs] = acc
            return 0

        lax.fori_loop(0, 2, step, 0)
        if l == 1:
            keep(o.keep_f, f_s, 4).start()
            keep(o.keep_g, gp, 5).start()

        zero = jnp.zeros((8, W), F32)

        def back(j, carry):
            sg, ss, sb = carry
            rs = pl.ds(pl.multiple_of(j * RUN, RUN), RUN)
            g = g_s[rs, :] + y_s[rs, :]
            xh = xh1[l, rs, :]
            sg = sg + rows8(g * xh)
            ss = ss + rows8(g)
            gy = layer_norm_back(g, vrow(l, 3), xh, r1[l, rs, :])
            g_s[rs, :] = gy
            gl = gy.astype(BF16)
            go[rs, :] = gl
            sb = sb + rows8(gl.astype(F32))
            return sg, ss, sb

        sg, ss, sb = lax.fori_loop(0, 4, back, (zero,) * 3)
        dvec[l, 3:4, :] = jnp.sum(sg, 0, keepdims=True)
        dvec[l, 4:5, :] = jnp.sum(ss, 0, keepdims=True)
        dvec[l, 2:3, :] = jnp.sum(sb, 0, keepdims=True)

    def project_back(l):
        put_part(l, 3, slice(None), dot_tn(c_s[l], go[...]))
        gc = dot_nt(go[...], part(l, 3)).astype(BF16)
        go[...] = gc
        gt[...] = gc.T

    def attend_back(l, p0, p1):
        def pair(p, _):
            c0 = pl.multiple_of(p * 128, 128)
            cs = pl.ds(c0, 128)
            k2 = k_s[l, :, cs]
            v2 = v_s[l, :, cs]
            qt = q_s[l, :, cs].T
            gct = gt[cs, :]
            kh = [k2 * t for t in sides4]
            dq = [None] * 4
            dvt, dkt = [], []
            for t in range(2):
                for r in range(4):
                    rs = slice(r * RUN, (r + 1) * RUN)
                    pr = p_s[2 * p + t, rs, :].astype(F32)
                    w = pr * dot_nt(go[rs, cs] * sides[t], v2)
                    dsl = (w - pr * jnp.sum(w, -1, keepdims=True)).astype(BF16)
                    ds_s[t, rs, :] = dsl
                    dd = dot(dsl, kh[t])
                    dq[r] = dd if dq[r] is None else dq[r] + dd
                hs = slice(64 * t, 64 * t + 64)
                dvt.append(dot(gct[hs], p_s[2 * p + t]))
                dkt.append(dot(qt[hs], ds_s[t]))
            dql = (jnp.concatenate(dq, 0) * 0.125).astype(BF16)
            dvl = jnp.concatenate(dvt, 0).T.astype(BF16)
            dkl = jnp.concatenate(dkt, 0).T.astype(BF16)
            gqkv[:, cs] = dql
            gqkv[:, pl.ds(pl.multiple_of(c0 + W, 128), 128)] = dkl
            gqkv[:, pl.ds(pl.multiple_of(c0 + 2 * W, 128), 128)] = dvl
            dvec[l, 0:1, cs] = jnp.sum(rows8(dql.astype(F32)), 0, keepdims=True)
            dvec[l, 1:2, cs] = jnp.sum(rows8(dvl.astype(F32)), 0, keepdims=True)
            return 0

        lax.fori_loop(p0, p1, pair, 0)
        if p1 == 4:
            if l == 1:
                keep(o.keep_p, p_s, 3).start()
            xt[...] = h_s[l].T

    def qkv_grad(l):
        for p in range(3):
            put_part(l, p, slice(None), dot(xt[...], gqkv[:, p * W : (p + 1) * W]))

    def qkv_back(l):
        gdst = gin1 if l == 1 else oc

        def step(j, _):
            cs = pl.ds(pl.multiple_of(j * 256, 256), 256)
            acc = g_s[:, cs]
            for p in range(3):
                acc = acc + dot_nt(gqkv[:, p * W : (p + 1) * W], part_rows(l, p, j * 256, 256))
            gdst[:, cs] = acc.astype(BF16)
            return 0

        lax.fori_loop(0, 2, step, 0)

    def small_grads(l):
        for i in range(Z * X * C):
            b = o.gsm.at[l, i // (X * C), (i // C) % X, i % C]
            b[...] = jnp.zeros(b.shape, F32)
            b[0:8, 0:nv] = dvec[l, :, i * nv : (i + 1) * nv]
            b[8:9, 0:nb] = dbff[l, 0:1, i * nb : (i + 1) * nb]
            for t in range(W // 128):
                b[9 + t : 10 + t, :] = o.dhw[0:1, t * 128 : (t + 1) * 128]
            b[9 + W // 128 : 10 + W // 128, 0:1] = o.dhb[...]

    steps = {
        "qkv": qkv, "attend": attend, "project": project, "ff_in": ff_in, "ff_out": ff_out, "restore": restore,
        "head": head, "top_back": top_back, "ff_out_grad": ff_out_grad, "ff_back": ff_back, "mid": mid,
        "project_back": project_back, "attend_back": attend_back, "qkv_grad": qkv_grad, "qkv_back": qkv_back,
        "reload": reload,
    }
    def exchange(*lists):
        for sec, todo in enumerate(lists):
            if todo:
                @pl.when(s == sec)
                def _():
                    for what, *which in todo:
                        getattr(ex, what)(sec, *which)

    if fused:
        steps |= {"exchange": exchange, "small_weights": small_weights, "small_grads": small_grads,
                  "send_acts": send_acts, "send_grad": send_grad}
    for name, *args in FUSED_STEPS if fused else PLAIN_STEPS:
        steps[name](*args)

    if fused:
        send_act.wait()
        send_term.wait()
        own_act.wait()
        send_g[0].wait()
        own_g[0].wait()
    else:
        outs = [pltpu.make_async_copy(g1, o.g_out.at[1], sems.at[0]),
                pltpu.make_async_copy(wall.at[1], o.g_out.at[0], sems.at[1]),
                pltpu.make_async_copy(h_s.at[pl.ds(1, 2)], o.act_out, sems.at[2]),
                pltpu.make_async_copy(oc, o.gin_out.at[0], sems.at[3]),
                pltpu.make_async_copy(gin1, o.gin_out.at[1], sems.at[4])]
        for t in outs:
            t.start()
        for t in outs:
            t.wait()


def make_call(rows, width, inner, n_vec, n_bias, grid, gather=None):
    f32 = lambda *t: jax.ShapeDtypeStruct(t, F32)
    b16 = lambda *t: jax.ShapeDtypeStruct(t, BF16)
    v = lambda dt, *t: pltpu.VMEM(t, dt)
    Z, X, C = grid or (1, 1, 1)
    rp = width // (Z * X * C)
    total = PARTS * rp
    vm = pl.BlockSpec(memory_space=pltpu.VMEM)
    sm = pl.BlockSpec(memory_space=pltpu.SMEM)
    hbm = pl.BlockSpec(memory_space=pl.ANY)
    ins = {"flag": sm, "hb": sm, "x_in": hbm, "oc_in": hbm, "aux": vm, "hw": vm}
    if grid:
        ins |= {"wq_in": vm, "wo_in": vm, "wi_in": vm, "wf_in": vm, "vec_in": vm, "bff_in": vm}
        outs = {
            "act_out": (b16(2 * rows, width), hbm), "gin_out": (b16(2 * rows, width), hbm),
            "term": (f32(2, 1, rows), vm),
            "d_wq": (f32(1, rp, 3 * width), vm), "d_wo": (f32(1, rp, width), vm), "d_wi": (f32(1, rp, inner), vm),
            "d_wf": (f32(1, 4 * rp, width), vm), "d_small": (f32(16, 128), vm),
        }
    else:
        ins |= {"w_in": hbm, "vec_in": vm, "bff_in": vm}
        outs = {
            "act_out": (b16(2, rows, width), hbm), "gin_out": (b16(2, rows, width), hbm), "term": (f32(1, rows), vm),
            "g_out": (b16(2, 1, 1, 1, total, width), hbm), "dvec": (f32(2, 8, width), vm),
            "dbff": (f32(2, 1, inner), vm), "dhw": (f32(1, width), vm), "dhb": (f32(1, 1), vm),
        }
    outs |= {"keep_p": (b16(HEADS, rows, rows), hbm), "keep_f": (b16(rows, inner), hbm),
             "keep_g": (b16(rows, inner), hbm)}
    scratch = {
        "wall": v(BF16, 2, Z, X, C, total, width), "g1": v(BF16, Z, X, C, total, width),
        "q_s": v(BF16, 2, rows, width), "k_s": v(BF16, 2, rows, width), "v_s": v(BF16, 2, rows, width),
        "p_s": v(BF16, HEADS, rows, rows), "c_s": v(BF16, 2, rows, width),
        "xh1": v(F32, 2, rows, width), "r1n": v(F32, 2, rows, 1), "n1": v(BF16, 2, rows, width),
        "f_s": v(BF16, rows, inner), "gp": v(BF16, rows, inner),
        "xh2": v(F32, 2, rows, width), "r2n": v(F32, 2, rows, 1), "y_s": v(F32, rows, width),
        "h_s": v(BF16, 3, rows, width), "oc": v(BF16, rows, width), "gin1": v(BF16, rows, width),
        "mrow": v(F32, 8, rows), "g_s": v(F32, rows, width), "go": v(BF16, rows, width), "gt": v(BF16, rows, width),
        "ds_s": v(BF16, 2, rows, rows), "gqkv": v(BF16, rows, 3 * width), "xt": v(BF16, width, rows),
        "cols": v(F32, rows, 8), "vec": v(F32, 2, 8, width), "bff": v(F32, 2, 1, inner),
        "sems": pltpu.SemaphoreType.DMA((6,)),
    }
    if grid:
        late = late_parts() * rp
        kg, kr = len(GATHER) + 1, len(REDUCE) + 1
        dma = pltpu.SemaphoreType.DMA
        scratch |= {
            "dvec": v(F32, 2, 8, width), "dbff": v(F32, 2, 1, inner), "dhw": v(F32, 1, width), "dhb": v(F32, 1, 1),
            "wsm": v(F32, 2, Z, X, C, 16, 128), "gsm": v(F32, 2, Z, X, C, 16, 128),
            "r1s": v(F32, 2, Z, X, 16, 128), "rxs": v(F32, 2, Z, 16, 128), "rzs": v(F32, 2, Z, 16, 128),
            "rys": v(F32, 16, 128),
            "r1": v(BF16, Z, X, total, width), "ry": v(BF16, Z, X, late, width),
            "rx": v(BF16, 2, Z, total, width), "rz": v(BF16, 2, Z, total, width), "rf": v(BF16, total, width),
            "own": v(BF16, total, width), "own_small": v(F32, 16, 128),
            "gs": dma((2, kg, 6)), "gr": dma((2, kg, 6)), "ss": dma((2, kr, 6)), "sr": dma((2, kr, 6)),
            "os": dma((3,)), "orr": dma((3,)), "credit": pltpu.SemaphoreType.REGULAR((kr,)),
        }
    names = list(ins) + list(outs) + list(scratch)
    params = dict(vmem_limit_bytes=VMEM_BYTES)
    if grid:
        params |= dict(collective_id=0, has_side_effects=True)
    call = pl.pallas_call(
        functools.partial(kernel, names, grid),
        out_shape=tuple(t[0] for t in outs.values()),
        in_specs=list(ins.values()),
        out_specs=tuple(t[1] for t in outs.values()),
        scratch_shapes=list(scratch.values()),
        compiler_params=pltpu.CompilerParams(**params),
    )
    return call, list(outs)


def pick_own(section, micro, rows, a):
    return lax.dynamic_index_in_dim(a.reshape((micro, rows) + a.shape[1:]), section, 0, keepdims=False)


def fused_local(grid, tokens_in, out_cot, term_cot, long_flag, token_mask, w_qkv, w_out, w_ff_in, w_ff_out, vectors,
                ff_bias, head_weight, head_bias):
    section = lax.axis_index("section")
    width = tokens_in.shape[1]
    micro = long_flag.shape[0]
    rows = tokens_in.shape[0] // micro
    own = functools.partial(pick_own, section, micro, rows)
    aux = jnp.stack([own(term_cot), own(token_mask).astype(F32)])
    flag = lax.dynamic_slice_in_dim(long_flag, section, 1)
    call, names = make_call(rows, width, w_ff_in.shape[2], vectors.shape[2], ff_bias.shape[1], grid)
    res = dict(zip(names, call(flag, head_bias, tokens_in, out_cot, aux, head_weight[None], w_qkv, w_out, w_ff_in,
                               w_ff_out, vectors, ff_bias)))
    small = res["d_small"]
    heads = width // 128
    return (
        res["act_out"][None], res["term"].reshape(-1).astype(BF16), res["gin_out"][None],
        res["d_wq"], res["d_wo"], res["d_wi"], res["d_wf"],
        small[None, 0:8, 0 : vectors.shape[2]], small[8:9, 0 : ff_bias.shape[1]],
        small[9 : 9 + heads].reshape(width), small[9 + heads, 0:1],
    )


def plain_local(tokens_in, out_cot, term_cot, long_flag, token_mask, w_qkv, w_out, w_ff_in, w_ff_out, vectors, ff_bias,
                head_weight, head_bias):
    section = lax.axis_index("section")
    width = tokens_in.shape[1]
    micro = long_flag.shape[0]
    rows = tokens_in.shape[0] // micro
    inner = w_ff_in.shape[2]
    own = functools.partial(pick_own, section, micro, rows)
    everyone = lambda a, ax: lax.all_gather(lax.all_gather(a, "dp", axis=ax, tiled=True), "section", axis=0, tiled=True)
    wq, wo, wi, wf = (everyone(a, 1) for a in (w_qkv, w_out, w_ff_in, w_ff_out))
    vec = everyone(vectors, 2).astype(F32)
    bff = everyone(ff_bias, 1).astype(F32)[:, None]
    cut = lambda a: a.reshape(2, width, -1, width).transpose(0, 2, 1, 3).reshape(2, -1, width)
    wall = jnp.concatenate([cut(wq), wo, cut(wi), wf], 1)[:, None, None, None]
    aux = jnp.stack([own(term_cot), own(token_mask).astype(F32)])
    flag = lax.dynamic_slice_in_dim(long_flag, section, 1)
    call, names = make_call(rows, width, inner, width, inner, None)
    res = dict(zip(names, call(flag, head_bias, own(tokens_in), own(out_cot), aux, head_weight[None], wall, vec, bff)))
    swap = lambda a: lax.all_gather(a, "section", axis=1, tiled=True)[section][None]
    terms = lax.all_gather(res["term"][0], "section", axis=0, tiled=True).astype(BF16)

    def scatter(a, ax):
        a = lax.psum_scatter(a.astype(F32), "section", scatter_dimension=0, tiled=True)
        return lax.psum_scatter(a, "dp", scatter_dimension=ax, tiled=True)

    g = res["g_out"][:, 0, 0, 0]
    glue = lambda a, n: a.reshape(2, n, width, width).transpose(0, 2, 1, 3).reshape(2, width, n * width)
    dhw, dhb = lax.psum((res["dhw"][0], res["dhb"][0]), ("section", "dp"))
    return (
        swap(res["act_out"]), terms, swap(res["gin_out"]),
        scatter(glue(g[:, : 3 * width], 3), 1), scatter(g[:, 3 * width : 4 * width], 1),
        scatter(glue(g[:, 4 * width : 8 * width], 4), 1), scatter(g[:, 8 * width :], 1),
        scatter(res["dvec"], 2), scatter(res["dbff"][:, 0], 1), dhw, dhb,
    )


def solution(mesh):
    dp = mesh.shape["dp"]
    if dp == 16:
        local = functools.partial(fused_local, (4, 2, 2))
    else:
        local = plain_local
    shard = P("section", "dp", None)
    in_specs = (P("dp", None), P("dp", None), P("dp"), P("dp"), P("dp"), shard, shard, shard, shard,
                P("section", None, "dp"), P("section", "dp"), P(), P())
    out_specs = (shard, P("dp"), shard, shard, shard, shard, shard, P("section", None, "dp"), P("section", "dp"),
                 P(), P())
    return jax.shard_map(local, mesh=mesh, in_specs=in_specs, out_specs=out_specs, check_vma=False)
```

```python
import functools
import types

import jax
import jax.numpy as jnp
from jax import lax
from jax.experimental import pallas as pl
from jax.experimental.pallas import tpu as pltpu
from jax.sharding import PartitionSpec as P

RUN = 128
HEADS = 8
EPS = 1e-12
F32, BF16 = jnp.float32, jnp.bfloat16
VMEM_BYTES = 64 * 2**20
GELU_ROWS = 64
ATTEND_ROWS = 256
SOFTMAX_ROWS = 64


def dot(a, b):
    return lax.dot_general(a, b, (((1,), (0,)), ((), ())), preferred_element_type=F32)


def dot_nt(a, b):
    return lax.dot_general(a, b, (((1,), (1,)), ((), ())), preferred_element_type=F32)


def dot_tn(a, b):
    return lax.dot_general(a, b, (((0,), (0,)), ((), ())), preferred_element_type=F32)


def rows8(v):
    return jnp.sum(v.reshape(-1, 8, v.shape[1]), axis=0)


def tiled(i, n):
    return i if isinstance(i, int) else pl.multiple_of(i, n)


def loop(start, stop, step):
    for j in range(start, stop):
        step(j, 0)


def gelu_both(u):
    w = jnp.abs(u)
    e = jnp.exp2(u * u * -0.7213475204444817)
    d = w * (0.3275911 * 0.7071067811865476) + 1.0
    t = pl.reciprocal(d, approx=True)
    t = t * (2.0 - d * t)
    q = t * 0.5307027145 - 0.7265760135
    q = q * t + 0.7107068705
    q = q * t - 0.142248368
    q = q * t + 0.127414796
    q = q * t * e
    n = q - w * (e * 0.3989422804014327)
    return jnp.maximum(u, 0.0) - w * q, jnp.where(u >= 0.0, 1.0 - n, n)


def layer_norm_rows(y):
    c = y - jnp.mean(y, -1, keepdims=True)
    r = lax.rsqrt(jnp.mean(c * c, -1, keepdims=True) + EPS)
    return c * r, r


def layer_norm_back(g, gain, xh, r):
    gx = g * gain
    a = jnp.mean(gx, -1, keepdims=True)
    b = jnp.mean(gx * xh, -1, keepdims=True)
    return (gx - a - xh * b) * r


MESH = pl.DeviceIdType.MESH
(QKV, ATTEND, PROJECT, FF_IN, FF_OUT, RESTORE, HEAD, TOP_BACK, FF_OUT_GRAD, FF_BACK, MID, PROJECT_BACK, ATTEND_BACK,
 QKV_GRAD, QKV_BACK, RELOAD, EXCHANGE, SMALL_WEIGHTS, SMALL_GRADS, SEND_ACTS, SEND_GRAD) = range(21)
GY, GZ, GX, GC, GD, GE, RC, R1, RY, R2, R3, R4, RE = range(13)
BOTH, OWN, OTHER = range(3)
ALONG_Z, ALONG_X, SHARD, PLANE, TO_CORE = range(5)
PARTS = 12
GATHER = ((0, 1), (1, 1), (2, 1), (3, 1), (4, 1), (5, 1), (6, 1), (7, 1), (8, 1), (9, 1), (10, 1), (11, 1))
GATHER_ROUTE = ((OTHER, OWN, OWN, BOTH, OTHER, BOTH, BOTH, OTHER, OTHER, OWN, OWN, BOTH), (OTHER, BOTH, OTHER, OWN, OTHER, BOTH, OWN, OWN, BOTH, BOTH, BOTH, OWN))
REDUCE = ((0, 1), (1, 1), (2, 1), (3, 1), (4, 1), (5, 1), (6, 1), (7, 1), (8, 1), (9, 1), (10, 1), (11, 1))
REDUCE_ROUTE = ((BOTH, BOTH, BOTH, OWN, OWN, OWN, BOTH, BOTH, OTHER, BOTH, BOTH, OTHER), (OWN, OTHER, OWN, BOTH, BOTH, BOTH, BOTH, OTHER, OTHER, BOTH, OWN, BOTH))


def late_place(l, k):
    takes = lambda a, b: a if REDUCE_ROUTE[a][b] == OWN else 1 - a
    at = 0
    for a in range(2):
        for b, (_, n) in enumerate(REDUCE):
            if (a, b) == (l, k):
                return at, n
            if REDUCE_ROUTE[a][b] != BOTH and takes(a, b) == takes(l, k):
                at += n
    return at, 0


def late_parts():
    ends = [sum(late_place(l, k)) for l in range(2) for k in range(len(REDUCE)) if REDUCE_ROUTE[l][k] != BOTH]
    return max(ends, default=1)


def layer_steps(l):
    return (
        ((RESTORE, 0),) if l else ()) + (
        (QKV, l), (ATTEND, l, 0, 4), (PROJECT, l)) + (
        ((RESTORE, 1), (RESTORE, 2)) if l else ()) + (
        (FF_IN, l, 0, 8), (FF_OUT, l))


def layer_back_steps(l):
    return (
        () if l else ((RELOAD, 0), (RELOAD, 1), (RELOAD, 2))) + (
        (TOP_BACK, l), (FF_OUT_GRAD, l), (FF_BACK, l, 0, 8), (MID, l), (PROJECT_BACK, l),
        (ATTEND_BACK, l, 0, 4), (QKV_BACK, l), (QKV_GRAD, l))


PLAIN_STEPS = layer_steps(0) + layer_steps(1) + ((HEAD,),) + layer_back_steps(1) + layer_back_steps(0)


FUSED_STEPS = (
    (EXCHANGE, (
        (GY, 0, 12), (GY, 0, 0), (GY, 0, 6), (GY, 0, 5), (GZ, 0, 12), (GZ, 0, 2), (GY, 0, 3), (GY, 0, 11),
        (GY, 0, 4), (GZ, 1, 12), (GX, 0, 12), (GY, 0, 7), (GZ, 0, 1), (GY, 0, 8), (GC, 0, 12), (GX, 0, 2),
        (GD, 0, 12),
    ), (
        (GY, 1, 12), (GY, 1, 0), (GY, 1, 4), (GY, 1, 2), (GZ, 1, 12), (GZ, 1, 3), (GY, 1, 1), (GY, 1, 9), (GY, 1, 8),
        (GZ, 0, 12), (GX, 1, 12), (GY, 1, 5), (GZ, 0, 0), (GY, 1, 10), (GC, 1, 12), (GX, 1, 3), (GD, 1, 12),
        (GZ, 0, 5), (GX, 0, 12), (GZ, 0, 4), (GX, 0, 0), (GC, 1, 3), (GC, 0, 12), (GD, 1, 3), (GD, 0, 12),
    )),
    (SMALL_WEIGHTS, 0),
    (EXCHANGE, (
        (GZ, 1, 2), (GX, 1, 12), (GZ, 0, 6), (GX, 0, 1), (GC, 0, 2), (GC, 1, 12), (GD, 0, 2), (GD, 1, 12),
        (GZ, 0, 10), (GX, 1, 2), (GC, 0, 1), (GZ, 0, 9), (GD, 0, 1), (GX, 0, 6), (GC, 1, 2), (GC, 1, 3), (GZ, 0, 5),
        (GD, 1, 2), (GX, 0, 10), (GD, 1, 3), (GC, 0, 6), (GZ, 1, 0), (GD, 0, 6), (GX, 0, 9), (GC, 0, 10), (GC, 0, 0),
        (GZ, 0, 3), (GD, 0, 10), (GX, 0, 5), (GD, 0, 0),
    ), (
        (GZ, 0, 11), (GX, 0, 5), (GC, 0, 0), (GZ, 0, 7), (GD, 0, 0), (GX, 0, 4), (GC, 0, 5), (GC, 0, 2), (GZ, 0, 6),
        (GD, 0, 5), (GX, 0, 11), (GD, 0, 2), (GC, 0, 4), (GZ, 0, 8), (GD, 0, 4), (GX, 0, 7), (GC, 0, 11), (GC, 0, 1),
        (GZ, 0, 3), (GD, 0, 11), (GX, 0, 6), (GD, 0, 1),
    )),
    (QKV, 0),
    (EXCHANGE, (
        (GC, 0, 9),
    ), (
        (GC, 0, 7),
    )),
    (ATTEND, 0, 0, 1),
    (EXCHANGE, (
        (GZ, 0, 11), (GX, 1, 0),
    ), (
        (GZ, 1, 7), (GX, 0, 8),
    )),
    (ATTEND, 0, 1, 2),
    (EXCHANGE, (
        (GC, 0, 5), (GD, 0, 9),
    ), (
        (GC, 0, 6), (GD, 0, 7),
    )),
    (ATTEND, 0, 2, 3),
    (EXCHANGE, (
        (GX, 0, 3), (GC, 0, 4), (GZ, 1, 4), (GD, 0, 5),
    ), (
        (GX, 0, 3), (GC, 1, 2), (GZ, 1, 6), (GD, 0, 6),
    )),
    (ATTEND, 0, 3, 4),
    (EXCHANGE, (
        (GC, 1, 0), (GD, 0, 4), (GZ, 1, 1), (GX, 0, 11), (GD, 1, 0), (GC, 0, 3), (GC, 0, 7), (GZ, 1, 9), (GX, 1, 4),
        (GD, 0, 3),
    ), (
        (GC, 0, 8), (GD, 1, 2), (GZ, 1, 11), (GX, 1, 7), (GD, 0, 8), (GC, 0, 3), (GC, 0, 10), (GZ, 1, 1), (GX, 1, 6),
        (GD, 0, 3),
    )),
    (PROJECT, 0),
    (EXCHANGE, (
        (GD, 0, 7),
    ), (
        (GD, 0, 10),
    )),
    (FF_IN, 0, 0, 2),
    (EXCHANGE, (
        (GC, 0, 11),
    ), (
        (GC, 1, 7),
    )),
    (FF_IN, 0, 2, 4),
    (EXCHANGE, (
        (GX, 1, 1), (GZ, 1, 8),
    ), (
        (GX, 1, 11), (GZ, 1, 9),
    )),
    (FF_IN, 0, 4, 6),
    (EXCHANGE, (
        (GC, 1, 4), (GD, 0, 11),
    ), (
        (GC, 1, 6), (GD, 1, 7),
    )),
    (FF_IN, 0, 6, 8),
    (EXCHANGE, (
        (GC, 0, 8), (GZ, 1, 5), (GX, 1, 9), (GD, 1, 4), (GD, 0, 8), (GC, 1, 1),
    ), (
        (GC, 0, 9), (GZ, 1, 8), (GX, 1, 1), (GD, 1, 6), (GD, 0, 9), (GC, 1, 11),
    )),
    (FF_OUT, 0),
    (EXCHANGE, (
        (GX, 1, 8), (GZ, 1, 10), (GD, 1, 1),
    ), (
        (GX, 1, 9), (GZ, 1, 5), (GD, 1, 11),
    )),
    (SMALL_WEIGHTS, 1),
    (RESTORE, 0),
    (EXCHANGE, (
    ), (
        (GC, 1, 1), (GC, 1, 0), (GZ, 1, 10), (GX, 1, 8), (GD, 1, 1), (GD, 1, 0),
    )),
    (QKV, 1),
    (EXCHANGE, (
        (GC, 1, 7), (GC, 1, 9),
    ), (
        (GC, 1, 9),
    )),
    (ATTEND, 1, 0, 1),
    (EXCHANGE, (
        (GX, 1, 5),
    ), (
        (GX, 1, 5),
    )),
    (ATTEND, 1, 1, 2),
    (EXCHANGE, (
        (GC, 1, 8), (GD, 1, 7), (GD, 1, 9),
    ), (
        (GC, 1, 8), (GC, 1, 4), (GD, 1, 9),
    )),
    (ATTEND, 1, 2, 3),
    (EXCHANGE, (
        (GX, 1, 10),
    ), (
        (GX, 1, 10),
    )),
    (ATTEND, 1, 3, 4),
    (EXCHANGE, (
        (GC, 1, 6), (GC, 1, 5), (GD, 1, 8),
    ), (
        (GC, 1, 5), (GD, 1, 4), (GD, 1, 8),
    )),
    (PROJECT, 1),
    (RESTORE, 1),
    (RESTORE, 2),
    (FF_IN, 1, 0, 2),
    (EXCHANGE, (
        (GD, 1, 6), (GD, 1, 5),
    ), (
        (GD, 1, 5),
    )),
    (FF_IN, 1, 2, 4),
    (EXCHANGE, (
        (GC, 1, 10),
    ), (
        (GC, 1, 10),
    )),
    (FF_IN, 1, 4, 6),
    (FF_IN, 1, 6, 8),
    (EXCHANGE, (
        (GD, 1, 10), (GC, 1, 11), (GD, 1, 11),
    ), (
        (GD, 1, 10),
    )),
    (FF_OUT, 1),
    (HEAD,),
    (SEND_ACTS,),
    (TOP_BACK, 1),
    (FF_OUT_GRAD, 1),
    (EXCHANGE, (
        (RC, 1, 11), (RC, 1, 9), (RC, 1, 8), (RC, 1, 10),
    ), (
        (RC, 1, 11), (RC, 1, 9), (RC, 1, 8), (RC, 1, 10),
    )),
    (FF_BACK, 1, 0, 2),
    (EXCHANGE, (
        (RC, 1, 4),
    ), (
        (RC, 1, 4),
    )),
    (FF_BACK, 1, 2, 4),
    (EXCHANGE, (
        (RC, 1, 5), (R1, 1, 11),
    ), (
        (RC, 1, 5), (R1, 1, 11),
    )),
    (FF_BACK, 1, 4, 6),
    (EXCHANGE, (
        (R1, 1, 9), (R1, 1, 8), (RC, 1, 6),
    ), (
        (R1, 1, 9), (R1, 1, 8), (RC, 1, 6),
    )),
    (FF_BACK, 1, 6, 8),
    (EXCHANGE, (
        (R1, 1, 4), (R1, 1, 10), (R1, 1, 5), (RC, 1, 7),
    ), (
        (R1, 1, 4), (R1, 1, 10), (R1, 1, 5), (RC, 1, 7),
    )),
    (MID, 1),
    (EXCHANGE, (
        (R1, 1, 6), (R2, 1, 11), (R1, 1, 7),
    ), (
        (R1, 1, 6), (R2, 1, 11), (R1, 1, 7),
    )),
    (PROJECT_BACK, 1),
    (EXCHANGE, (
        (RC, 1, 3),
    ), (
        (RC, 1, 3),
    )),
    (ATTEND_BACK, 1, 0, 1),
    (ATTEND_BACK, 1, 1, 2),
    (EXCHANGE, (
        (R2, 1, 9), (R3, 1, 11), (R1, 1, 3),
    ), (
        (R2, 1, 9), (R3, 1, 11), (R1, 1, 3),
    )),
    (ATTEND_BACK, 1, 2, 3),
    (ATTEND_BACK, 1, 3, 4),
    (EXCHANGE, (
        (R2, 1, 4),
    ), (
        (R2, 1, 4),
    )),
    (QKV_GRAD, 1),
    (EXCHANGE, (
        (RC, 1, 0), (RC, 1, 1), (RC, 1, 2),
    ), (
        (RC, 1, 0), (RC, 1, 1), (RC, 1, 2),
    )),
    (QKV_BACK, 1),
    (EXCHANGE, (
        (R3, 1, 9), (R2, 1, 5),
    ), (
        (R3, 1, 9), (R2, 1, 5),
    )),
    (SEND_GRAD, 1),
    (SMALL_GRADS, 1),
    (EXCHANGE, (
        (RC, 1, 12), (R1, 1, 0),
    ), (
        (RC, 1, 12), (R1, 1, 0),
    )),
    (RELOAD, 1),
    (RELOAD, 2),
    (EXCHANGE, (
    ), (
        (RY, 1, 10), (R1, 1, 1),
    )),
    (EXCHANGE, (
        (GE, 0), (GE, 1),
    ), (
        (GE, 0), (GE, 1),
    )),
    (TOP_BACK, 0),
    (EXCHANGE, (
        (R1, 1, 1), (R1, 1, 2), (R3, 1, 4), (R1, 1, 12), (RY, 1, 8), (R2, 1, 6),
    ), (
        (R4, 1, 11), (R4, 1, 9), (R3, 1, 4), (R1, 1, 2), (R2, 1, 6), (R1, 1, 12),
    )),
    (FF_OUT_GRAD, 0),
    (EXCHANGE, (
        (RC, 0, 10), (RC, 0, 8), (RC, 0, 9), (RC, 0, 11),
    ), (
        (RC, 0, 10), (RC, 0, 8), (RC, 0, 9), (RC, 0, 11),
    )),
    (FF_BACK, 0, 0, 2),
    (EXCHANGE, (
        (RC, 0, 4),
    ), (
        (RC, 0, 4),
    )),
    (FF_BACK, 0, 2, 4),
    (EXCHANGE, (
        (R3, 1, 5), (R2, 1, 3), (R1, 0, 10), (RC, 0, 5),
    ), (
        (R3, 1, 5), (R2, 1, 3), (R1, 0, 10), (RC, 0, 5),
    )),
    (FF_BACK, 0, 4, 6),
    (EXCHANGE, (
        (R2, 1, 12), (R1, 0, 8), (R1, 0, 9), (R1, 0, 11), (RC, 0, 6),
    ), (
        (R1, 0, 8), (R1, 0, 9), (R1, 0, 11), (RC, 0, 6),
    )),
    (FF_BACK, 0, 6, 8),
    (EXCHANGE, (
        (R1, 0, 5), (R1, 0, 4), (R3, 1, 6), (RY, 1, 7), (RC, 0, 7),
    ), (
        (R1, 0, 5), (R3, 1, 6), (R1, 0, 4), (RC, 0, 7), (R2, 1, 10),
    )),
    (MID, 0),
    (EXCHANGE, (
        (R2, 1, 8), (R1, 0, 7), (R1, 0, 6),
    ), (
        (R2, 1, 12), (R1, 0, 7), (R1, 0, 6),
    )),
    (PROJECT_BACK, 0),
    (EXCHANGE, (
        (R3, 1, 3), (R3, 1, 12), (R2, 0, 10), (RC, 0, 3),
    ), (
        (R3, 1, 3), (RC, 0, 3), (R2, 0, 10),
    )),
    (RELOAD, 0),
    (ATTEND_BACK, 0, 0, 1),
    (ATTEND_BACK, 0, 1, 2),
    (EXCHANGE, (
        (R3, 1, 8), (R2, 0, 9), (RY, 1, 1), (R1, 0, 3),
    ), (
        (R3, 1, 10), (R3, 1, 12), (R2, 0, 9), (R1, 0, 3),
    )),
    (ATTEND_BACK, 0, 2, 3),
    (ATTEND_BACK, 0, 3, 4),
    (EXCHANGE, (
        (R3, 0, 10), (R2, 1, 7),
    ), (
        (R3, 0, 10), (R2, 0, 7),
    )),
    (QKV_GRAD, 0),
    (EXCHANGE, (
        (RC, 0, 1), (RC, 0, 2), (RC, 0, 0),
    ), (
        (RC, 0, 1), (RC, 0, 2), (RC, 0, 0),
    )),
    (QKV_BACK, 0),
    (EXCHANGE, (
        (RY, 0, 5),
    ), (
        (RY, 1, 0),
    )),
    (SEND_GRAD, 0),
    (SMALL_GRADS, 0),
    (EXCHANGE, (
        (R3, 0, 9), (R1, 0, 1), (R2, 0, 7), (RC, 0, 12), (R1, 0, 2), (R1, 0, 0), (R1, 0, 12), (R3, 1, 7), (R2, 0, 6),
        (RY, 0, 4), (R3, 0, 7), (R2, 1, 1), (R3, 0, 6), (R2, 0, 5), (RY, 0, 3), (R3, 1, 1), (R4, 0, 10), (R2, 0, 1),
        (R3, 0, 5), (R2, 0, 2), (R3, 0, 1), (R2, 0, 0), (R2, 0, 12), (R3, 0, 2), (R2, 0, 4), (R3, 0, 0), (R3, 0, 12),
        (R4, 0, 9), (R2, 0, 3), (R4, 0, 7), (R4, 0, 6), (R4, 0, 1), (R3, 0, 4), (R4, 0, 2), (R4, 0, 0), (R4, 0, 12),
        (R4, 0, 8), (R4, 0, 11), (R3, 0, 3),
    ), (
        (RC, 0, 12), (R3, 0, 9), (R1, 0, 1), (R2, 0, 6), (R1, 0, 2), (R1, 0, 0), (R1, 0, 12), (R3, 0, 7), (R2, 1, 0),
        (RY, 1, 2), (R3, 0, 6), (R4, 1, 4), (R4, 1, 5), (R2, 0, 1), (R3, 1, 0), (R2, 0, 2), (R3, 0, 1), (RY, 0, 8),
        (R2, 0, 0), (R2, 0, 12), (R3, 0, 2), (R2, 1, 2), (R3, 0, 0), (R3, 0, 12), (RY, 0, 11), (R4, 1, 6),
        (R2, 0, 8), (R4, 1, 3), (R4, 1, 12), (R4, 1, 8), (R3, 1, 2), (R4, 1, 7), (R4, 1, 1), (R2, 0, 11), (R3, 0, 8),
        (R3, 0, 11),
    )),
    (EXCHANGE, (
        (RE, 1), (RE, 0),
    ), (
        (RE, 1), (RE, 0),
    )),
)


class Exchange:
    def __init__(self, o, grid, rp):
        self.o, self.rp = o, rp
        self.Z, self.X, self.C = grid
        self.s = lax.axis_index("section")
        d = lax.axis_index("dp")
        self.c = lax.rem(d, 2)
        self.x = lax.rem(d // 2, 2)
        self.z = d // 4

    def dev(self, s=None, z=None, x=None, c=None):
        s = self.s if s is None else s
        z = self.z if z is None else z
        x = self.x if x is None else x
        c = self.c if c is None else c
        return (s, (z * 2 + x) * 2 + c)

    def along_z(self, j):
        return lax.rem(self.z + j + 1, self.Z)

    def barrier(self):
        b = pltpu.get_barrier_semaphore()
        peers = [self.dev(z=self.along_z(j)) for j in range(self.Z - 1)]
        peers += [self.dev(x=1 - self.x), self.dev(c=1 - self.c), self.dev(s=1 - self.s)]
        for p in peers:
            pl.semaphore_signal(b, inc=1, device_id=p, device_id_type=MESH)
        pl.semaphore_wait(b, len(peers))

    def copy(self, src, dst, send, recv, dev):
        return pltpu.make_async_remote_copy(
            src_ref=src, dst_ref=dst, send_sem=send, recv_sem=recv, device_id=dev, device_id_type=MESH)

    def g_route(self, l, k):
        return BOTH if k == len(GATHER) else GATHER_ROUTE[l][k]

    def g_works(self, s, l, k):
        return self.g_route(l, k) in (BOTH, OWN if s == l else OTHER)

    def g_copy(self, kind, s, l, k, j=0):
        o = self.o
        z, x, c = self.z, self.x, self.c
        if k == len(GATHER):
            w, mine, rows = o.wsm.at[l], o.own_small, slice(None)
        else:
            p, n = GATHER[k]
            w, mine, rows = o.wall.at[l], o.own, slice(p * self.rp, (p + n) * self.rp)
        ss, rr = o.gs.at[l, k], o.gr.at[l, k]
        if kind == ALONG_Z:
            a = w.at[z, x, c, rows]
            return self.copy(a, a, ss.at[j], rr.at[j], self.dev(z=self.along_z(j)))
        if kind == ALONG_X:
            a = w.at[:, x, c, rows]
            return self.copy(a, a, ss.at[3], rr.at[3], self.dev(x=1 - x))
        if kind == SHARD:
            return self.copy(mine.at[rows], w.at[z, x, c, rows], ss.at[4], rr.at[4], self.dev(s=1 - s))
        a = w.at[:, :, c, rows]
        if kind == PLANE:
            return self.copy(a, a, ss.at[4], rr.at[4], self.dev(s=1 - s))
        return self.copy(a, a, ss.at[5], rr.at[5], self.dev(c=1 - c))

    def gy(self, s, l, k):
        self.g_copy(SHARD, s, l, k).start()

    def gz(self, s, l, k):
        if s != l:
            self.g_copy(SHARD, s, l, k).wait_recv()
        for j in range(self.Z - 1):
            self.g_copy(ALONG_Z, s, l, k, j).start()

    def gx(self, s, l, k):
        for j in range(self.Z - 1):
            self.g_copy(ALONG_Z, s, l, k, j).wait_recv()
        self.g_copy(ALONG_X, s, l, k).start()

    def gc(self, s, l, k):
        if self.g_works(s, l, k):
            self.g_copy(ALONG_X, s, l, k).wait_recv()
            if self.g_route(l, k) != BOTH:
                self.g_copy(PLANE, s, l, k).start()
        else:
            self.g_copy(PLANE, s, l, k).wait_recv()
        self.g_copy(TO_CORE, s, l, k).start()

    def gd(self, s, l, k):
        self.g_copy(TO_CORE, s, l, k).wait_recv()

    def ge(self, s, l):
        for k in range(len(GATHER) + 1):
            route = self.g_route(l, k)
            if s == l and route != OWN:
                self.g_copy(SHARD, s, l, k).wait_send()
            if self.g_works(s, l, k):
                for j in range(self.Z - 1):
                    self.g_copy(ALONG_Z, s, l, k, j).wait_send()
                self.g_copy(ALONG_X, s, l, k).wait_send()
                if route != BOTH:
                    self.g_copy(PLANE, s, l, k).wait_send()
            self.g_copy(TO_CORE, s, l, k).wait_send()

    def r_small(self, k):
        return k == len(REDUCE)

    def r_route(self, l, k):
        return BOTH if self.r_small(k) else REDUCE_ROUTE[l][k]

    def r_works(self, s, l, k):
        return self.r_route(l, k) in (BOTH, OWN if s == l else OTHER)

    def r_bufs(self, l, k):
        o = self.o
        if self.r_small(k):
            return o.gsm.at[l], slice(None), o.r1s.at[l], o.rxs.at[l], o.rzs.at[l], o.rys
        p, n = REDUCE[k]
        g = o.g1 if l == 1 else o.wall.at[1]
        return g, slice(p * self.rp, (p + n) * self.rp), o.r1, o.rx.at[l], o.rz.at[l], o.rf

    def r_late(self, l, k):
        at, n = late_place(l, k)
        return slice(at * self.rp, (at + n) * self.rp)

    def r_copy(self, kind, s, l, k, j=0):
        o = self.o
        g, rows, r1, rx, rz, rf = self.r_bufs(l, k)
        z, x, c = self.z, self.x, self.c
        ss, rr = o.ss.at[l, k], o.sr.at[l, k]
        if kind == TO_CORE:
            return self.copy(g.at[:, :, 1 - c, rows], r1.at[:, :, rows], ss.at[0], rr.at[0], self.dev(c=1 - c))
        if kind == ALONG_X:
            return self.copy(g.at[:, 1 - x, c, rows], rx.at[:, rows], ss.at[1], rr.at[1], self.dev(x=1 - x))
        if kind == ALONG_Z:
            to = self.along_z(j)
            return self.copy(g.at[to, x, c, rows], rz.at[z, rows], ss.at[2 + j], rr.at[2 + j], self.dev(z=to))
        if kind == PLANE:
            return self.copy(g.at[:, :, c, rows], o.ry.at[:, :, self.r_late(l, k)], ss.at[5], rr.at[5],
                             self.dev(s=1 - s))
        return self.copy(g.at[z, x, c, rows], rf.at[rows], ss.at[5], rr.at[5], self.dev(s=1 - s))

    def add(self, n, dst, src):
        def one(i, _):
            d = dst(i)
            d[...] = d[...] + src(i)[...]
            return 0

        lax.fori_loop(0, n, one, 0)

    def rc(self, s, l, k):
        if l == 0 and not self.r_small(k):
            pl.semaphore_wait(self.o.credit.at[k], 1)
        self.r_copy(TO_CORE, s, l, k).start()

    def r1(self, s, l, k):
        g, rows, r1, rx, rz, rf = self.r_bufs(l, k)
        c, X = self.c, self.X
        self.r_copy(TO_CORE, s, l, k).wait_recv()
        self.add(self.Z * X, lambda i: g.at[i // X, lax.rem(i, X), c, rows], lambda i: r1.at[i // X, lax.rem(i, X), rows])
        if l == 1 and not self.r_small(k):
            pl.semaphore_signal(self.o.credit.at[k], inc=1, device_id=self.dev(c=1 - c), device_id_type=MESH)
        route = self.r_route(l, k)
        if route == BOTH:
            self.r_copy(ALONG_X, s, l, k).start()
        elif not self.r_works(s, l, k):
            self.r_copy(PLANE, s, l, k).start()

    def ry(self, s, l, k):
        g, rows, r1, rx, rz, rf = self.r_bufs(l, k)
        c, X, late = self.c, self.X, self.r_late(l, k)
        self.r_copy(PLANE, s, l, k).wait_recv()
        self.add(self.Z * X, lambda i: g.at[i // X, lax.rem(i, X), c, rows],
                 lambda i: self.o.ry.at[i // X, lax.rem(i, X), late])
        self.r_copy(ALONG_X, s, l, k).start()

    def r2(self, s, l, k):
        g, rows, r1, rx, rz, rf = self.r_bufs(l, k)
        x, c = self.x, self.c
        self.r_copy(ALONG_X, s, l, k).wait_recv()
        self.add(self.Z, lambda i: g.at[i, x, c, rows], lambda i: rx.at[i, rows])
        for j in range(self.Z - 1):
            self.r_copy(ALONG_Z, s, l, k, j).start()

    def r3(self, s, l, k):
        g, rows, r1, rx, rz, rf = self.r_bufs(l, k)
        z, x, c = self.z, self.x, self.c
        for j in range(self.Z - 1):
            self.r_copy(ALONG_Z, s, l, k, j).wait_recv()
        rz[z, rows] = g[z, x, c, rows]
        total = rz[0, rows].astype(F32)
        for i in range(1, self.Z):
            total = total + rz[i, rows].astype(F32)
        if s == l and self.r_route(l, k) == OWN:
            self.result(k, total)
        else:
            g[z, x, c, rows] = total.astype(g.dtype)
            if s != l:
                self.r_copy(SHARD, s, l, k).start()

    def r4(self, s, l, k):
        g, rows, r1, rx, rz, rf = self.r_bufs(l, k)
        self.r_copy(SHARD, s, l, k).wait_recv()
        total = rf[rows].astype(F32)
        if self.r_route(l, k) == BOTH:
            total = g[self.z, self.x, self.c, rows].astype(F32) + total
        self.result(k, total)

    def result(self, k, v):
        o, rp = self.o, self.rp
        if self.r_small(k):
            o.d_small[...] = v
            return
        p0, n = REDUCE[k]
        w = v.shape[1]
        for i in range(n):
            p, t = p0 + i, v[i * rp : (i + 1) * rp]
            if p < 3:
                o.d_wq[0, :, p * w : (p + 1) * w] = t
            elif p == 3:
                o.d_wo[0] = t
            elif p < 8:
                o.d_wi[0, :, (p - 4) * w : (p - 3) * w] = t
            else:
                o.wft[(p - 8) * rp : (p - 7) * rp, :] = t

    def turn(self):
        for m in range(self.o.wft.shape[1] // 128):
            ms = slice(m * 128, m * 128 + 128)
            self.o.d_wf[0, :, ms] = self.o.wft[:, ms].T

    def re(self, s, l):
        for k in range(len(REDUCE) + 1):
            route, works = self.r_route(l, k), self.r_works(s, l, k)
            self.r_copy(TO_CORE, s, l, k).wait_send()
            if works:
                self.r_copy(ALONG_X, s, l, k).wait_send()
                for j in range(self.Z - 1):
                    self.r_copy(ALONG_Z, s, l, k, j).wait_send()
                if s != l:
                    self.r_copy(SHARD, s, l, k).wait_send()
            else:
                self.r_copy(PLANE, s, l, k).wait_send()


def kernel(names, grid, *refs):
    o = types.SimpleNamespace(**dict(zip(names, refs)))
    fused = grid is not None
    W = o.h_s.shape[2]
    FF = o.f_s.shape[1]
    Z, X, C, total = o.wall.shape[1:5]
    rp = total // PARTS
    flag, hb, wall, g1 = o.flag, o.hb, o.wall, o.g1
    q_s, k_s, v_s, p_s, c_s, cl_s, xh1, rst, n1 = o.q_s, o.k_s, o.v_s, o.p_s, o.c_s, o.cl_s, o.xh1, o.rst, o.n1
    f_s, gp, xh2, y_s, h_s, oc = o.f_s, o.gp, o.xh2, o.y_s, o.h_s, o.oc
    gin1, mask_s, g_s, go, gh_s, ds_s, gqkv, xt, cols = o.gin1, o.mask_s, o.g_s, o.go, o.gh_s, o.ds_s, o.gqkv, o.xt, o.cols
    vec, bff, dvec, dbff, sems = o.vec, o.bff, o.dvec, o.dbff, o.sems

    R = h_s.shape[1]
    s = lax.axis_index("section")
    mine = pl.ds(tiled(s * R, R), R)
    tc = o.tc_in[mine].reshape(1, R)
    mask = o.mask_in[mine].reshape(1, R).astype(F32)
    hw = o.hw_in[...].reshape(1, W)
    long = flag[s] == 1
    if fused:
        ex = Exchange(o, grid, rp)
        z, x, c = ex.z, ex.x, ex.c
        cin = [pltpu.make_async_copy(o.x_in.at[mine], h_s.at[0], sems.at[0]),
               pltpu.make_async_copy(o.oc_in.at[mine], oc, sems.at[1])]
        for t in cin:
            t.start()
        for i in range(3):
            o.own[i * rp : (i + 1) * rp, :] = o.wq_in[0, :, i * W : (i + 1) * W]
        o.own[3 * rp : 4 * rp, :] = o.wo_in[0]
        for i in range(4):
            o.own[(4 + i) * rp : (5 + i) * rp, :] = o.wi_in[0, :, i * W : (i + 1) * W]
        o.own[8 * rp :, :] = o.wf_in[0]
        wall[s, z, x, c] = o.own[...]
        nv, nb = o.vec_in.shape[2], o.bff_in.shape[1]
        o.own_small[...] = jnp.zeros(o.own_small.shape, F32)
        o.own_small[0:8, 0:nv] = o.vec_in[0].astype(F32)
        o.own_small[8:9, 0:nb] = o.bff_in[...].astype(F32)
        o.wsm[s, z, x, c] = o.own_small[...]
        ex.barrier()
    else:
        cin = [pltpu.make_async_copy(o.x_in.at[mine], h_s.at[0], sems.at[0]),
               pltpu.make_async_copy(o.oc_in.at[mine], oc, sems.at[1]),
               pltpu.make_async_copy(o.w_in, wall, sems.at[2])]
        for t in cin:
            t.start()
        vec[...] = o.vec_in[...]
        bff[...] = o.bff_in[...]

    for t in cin:
        t.wait()

    lane = lax.broadcasted_iota(jnp.int32, (W, 128), 1)
    row_run = lax.broadcasted_iota(jnp.int32, (W, 128), 0) // RUN
    flagged = lambda cond: cond.astype(F32).astype(BF16)
    sides = (flagged(lane < 64), flagged(lane >= 64))
    spare = (lane - 64, lane)
    run_lane = tuple(flagged(t == row_run) for t in spare)
    two_lanes = tuple(flagged((t == 0) | (t == 1)) for t in spare)

    valid = mask > 0.0
    key_run = lax.broadcasted_iota(jnp.int32, (8, W), 1) // RUN
    query_run = lax.broadcasted_iota(jnp.int32, (8, W), 0)
    open_key = valid & ((key_run == query_run) | long)
    blocked = jnp.where(open_key, 0.0, -1e9).T
    for t in range(2):
        wide = jnp.zeros((W, 128), F32)
        for r in range(R // RUN):
            wide = jnp.where(spare[t] == r, blocked[:, r : r + 1], wide)
        mask_s[t] = wide.astype(BF16)

    def small_weights(l):
        for i in range(Z * X * C):
            b = o.wsm.at[l, i // (X * C), (i // C) % X, i % C]
            vec[l, :, i * nv : (i + 1) * nv] = b[0:8, 0:nv]
            bff[l, 0:1, i * nb : (i + 1) * nb] = b[8:9, 0:nb]

    def part(l, p, cs=slice(None)):
        a = wall[l, :, :, :, pl.ds(tiled(p * rp, rp), rp), cs]
        return a.reshape(W, a.shape[-1])

    def part_rows(l, p, r0, n):
        if C == 1:
            return wall[l, 0, 0, 0, pl.ds(tiled(p * rp + r0, n), n), :]
        k = n // (X * C * rp)
        return wall[l, pl.ds(r0 // (X * C * rp), k), :, :, pl.ds(tiled(p * rp, rp), rp), :].reshape(n, W)

    def back_w(l, cs):
        a = wall[l, :, :, :, 8 * rp :, cs]
        return a.reshape(FF, a.shape[-1])

    def back_rows(l, j, n):
        if C == 1:
            return wall[l, 0, 0, 0, pl.ds(tiled(8 * rp + j * n, n), n), :]
        return wall[l, j // X, lax.rem(j, X), :, 8 * rp :, :].reshape(n, W)

    def g_ref(l):
        return g1 if l == 1 else wall.at[1]

    def put_part(l, p, cs, val):
        rows = pl.ds(tiled(p * rp, rp), rp)
        g_ref(l)[:, :, :, rows, cs] = val.reshape(Z, X, C, rp, -1).astype(BF16)

    def put_back(l, j, val):
        val = val.astype(BF16)
        for i in range(val.shape[1] // 128):
            for m in range(W // 128):
                block = val[m * 128 : m * 128 + 128, i * 128 : i * 128 + 128]
                ms = slice(m * 128, m * 128 + 128)
                if C == 1:
                    g_ref(l)[0, 0, 0, pl.ds(tiled(8 * rp + (4 * j + i) * 128, 128), 128), ms] = block
                else:
                    g_ref(l)[j, i // C, i % C, 8 * rp :, ms] = block

    def vrow(l, i):
        return vec[l, i : i + 1, :]

    def keep(src, dst, i):
        return pltpu.make_async_copy(src, dst, sems.at[i])

    def qkv(l):
        h = h_s.at[l]

        def step(j, _):
            cs = pl.ds(tiled(j * 256, 256), 256)
            hv = h[...]
            rq = dot(hv, part(l, 0, cs)) + vec[l, 0:1, cs]
            q_s[l, :, cs] = (rq.astype(BF16).astype(F32) * 0.125).astype(BF16)
            k_s[l, :, cs] = dot(hv, part(l, 1, cs)).astype(BF16)
            v_s[l, :, cs] = (dot(hv, part(l, 2, cs)) + vec[l, 1:2, cs]).astype(BF16)
            return 0

        loop(0, 2, step)

    def attend(l, p0, p1):
        def pair(p, _):
            cs = pl.ds(tiled(p * 128, 128), 128)
            k2 = k_s[l, :, cs]
            v2 = v_s[l, :, cs]
            for r in range(0, R, ATTEND_ROWS):
                rs = slice(r, r + ATTEND_ROWS)
                q2 = q_s[l, rs, cs]
                c = []
                for t in range(2):
                    raw = dot_nt(q2 * sides[t][rs] + run_lane[t][rs], k2 * sides[t] + mask_s[t])
                    for b in range(0, ATTEND_ROWS, SOFTMAX_ROWS):
                        a = raw[b : b + SOFTMAX_ROWS]
                        e = jnp.exp(a - jnp.max(a, -1, keepdims=True))
                        e = e * (1.0 / jnp.sum(e, -1, keepdims=True))
                        p_s[2 * p + t, r + b : r + b + SOFTMAX_ROWS, :] = e.astype(BF16)
                    c.append(dot(p_s[2 * p + t, rs, :], v2 * sides[t]))
                c = c[0] + c[1]
                c_s[l, rs, cs] = c.astype(BF16)
                cl_s[l, rs, cs] = (c - c.astype(BF16).astype(F32)).astype(BF16)
            return 0

        lax.fori_loop(p0, p1, pair, 0)
        if l == 0 and p1 == 4:
            keep(p_s, o.keep_p, 3).start()

    def project(l):
        def step(j, _):
            rs = pl.ds(tiled(j * 256, 256), 256)
            y = h_s[l, rs, :].astype(F32) + dot(c_s[l, rs, :], part(l, 3)) + vrow(l, 2)
            xh, r = layer_norm_rows(y)
            xh1[l, rs, :] = xh
            rst[l, rs, 0:1] = r
            n1[l, rs, :] = (xh * vrow(l, 3) + vrow(l, 4)).astype(BF16)
            return 0

        loop(0, 2, step)

    def ff_in(l, j0, j1):
        def step(j, _):
            cs = pl.ds(tiled(j * 256, 256), 256)
            sub = pl.ds(tiled((j % 2) * 256, 256), 256)
            u = dot(n1[l], part(l, 4 + j // 2, sub))
            b = bff[l, 0:1, cs]
            for r in range(0, W, GELU_ROWS):
                f, d = gelu_both(u[r : r + GELU_ROWS] + b)
                f_s[r : r + GELU_ROWS, cs] = f.astype(BF16)
                gp[r : r + GELU_ROWS, cs] = d.astype(BF16)
            return 0

        loop(j0, j1, step)

    def ff_out(l):
        def step(j, _):
            cs = pl.ds(tiled(j * 256, 256), 256)
            y_s[:, cs] = dot(f_s[...], back_w(l, cs))
            return 0

        loop(0, 2, step)
        if l == 0:
            keep(f_s, o.keep_f, 4).start()
            keep(gp, o.keep_g, 5).start()

        def top(j, _):
            rs = pl.ds(tiled(j * RUN, RUN), RUN)
            y = xh1[l, rs, :] * vrow(l, 3) + vrow(l, 4) + y_s[rs, :] + vrow(l, 5)
            xh, r = layer_norm_rows(y)
            xh2[l, rs, :] = xh
            rst[l, rs, 1:2] = r
            h_s[l + 1, rs, :] = (xh * vrow(l, 6) + vrow(l, 7)).astype(BF16)
            return 0

        loop(0, 4, top)

    spilled = ((p_s, o.keep_p, 3), (f_s, o.keep_f, 4), (gp, o.keep_g, 5))

    def restore(i):
        src, dst, at = spilled[i]
        keep(src, dst, at).wait()

    def reload(i):
        src, dst, at = spilled[i]
        keep(dst, src, at).wait()

    act1 = h_s.at[2]

    def head():
        hw16 = jnp.broadcast_to(hw, (16, W))
        zr = dot_nt(hw16, act1[...])[0:1] + hb[0]
        ez = jnp.exp(-jnp.abs(zr))
        terms = jnp.log1p(ez) + jnp.maximum(zr, 0.0)
        sig = jnp.where(zr >= 0.0, 1.0, ez) / (1.0 + ez)
        gz = tc * mask * sig
        o.dhb[...] = jnp.sum(gz, -1, keepdims=True)
        sub8 = lax.broadcasted_iota(jnp.int32, (8, W), 0)
        cols[...] = jnp.where(sub8 == 0, gz, jnp.where(sub8 == 1, mask, 0.0)).T
        if fused:
            o.term[s] = terms
        else:
            o.term[...] = terms

    if fused:
        own_rows = mine
        across = ex.dev(s=1 - s)
        send_act = ex.copy(h_s.at[2 - s], o.act_out.at[own_rows], o.os.at[0], o.orr.at[0], across)
        send_term = ex.copy(o.term.at[s], o.term.at[s], o.os.at[1], o.orr.at[1], across)
        own_act = pltpu.make_async_copy(h_s.at[1 + s], o.act_out.at[own_rows], sems.at[0])
        send_g = [ex.copy(g, o.gin_out.at[own_rows], o.os.at[2], o.orr.at[2], across) for g in (oc, gin1)]
        own_g = [pltpu.make_async_copy(g, o.gin_out.at[own_rows], sems.at[1]) for g in (oc, gin1)]

    def send_acts():
        send_act.start()
        send_term.start()
        own_act.start()

    def send_grad(i):
        pl.when(s != i)(send_g[i].start)
        pl.when(s == i)(own_g[i].start)

    def top_back(l):
        zero = jnp.zeros((8, W), F32)

        def step(j, carry):
            sg, ss, sb, sh = carry
            rs = pl.ds(tiled(j * RUN, RUN), RUN)
            if l == 1:
                gzc = cols[rs, 0:1]
                g = oc[rs, :].astype(F32) * cols[rs, 1:2] + gzc * hw.astype(F32)
                sh = sh + rows8(gzc * act1[rs, :].astype(F32))
            else:
                g = gin1[rs, :].astype(F32)
            xh = xh2[l, rs, :]
            sg = sg + rows8(g * xh)
            ss = ss + rows8(g)
            gy = layer_norm_back(g, vrow(l, 6), xh, rst[l, rs, 1:2])
            g_s[rs, :] = gy
            gl = gy.astype(BF16)
            go[rs, :] = gl
            sb = sb + rows8(gl.astype(F32))
            return sg, ss, sb, sh

        sg, ss, sb, sh = lax.fori_loop(0, 4, step, (zero,) * 4)
        dvec[l, 6:7, :] = jnp.sum(sg, 0, keepdims=True)
        dvec[l, 7:8, :] = jnp.sum(ss, 0, keepdims=True)
        dvec[l, 5:6, :] = jnp.sum(sb, 0, keepdims=True)
        if l == 1:
            o.dhw[...] = jnp.sum(sh, 0, keepdims=True)

    def ff_out_grad(l):
        xt[...] = go[...].T

        def step(j, _):
            cs = pl.ds(tiled(j * 512, 512), 512)
            put_back(l, j, dot(xt[...], f_s[:, cs]))
            return 0

        loop(0, FF // 512, step)

    def ff_back(l, j0, j1):
        if j0 == 0:
            xt[...] = n1[l].T

        def step(j, _):
            cs = pl.ds(tiled(j * 256, 256), 256)
            gf = dot_nt(go[...], back_rows(l, j, 256))
            total = jnp.zeros((8, 256), F32)
            for r in range(0, W, GELU_ROWS):
                gul = (gf[r : r + GELU_ROWS] * gp[r : r + GELU_ROWS, cs].astype(F32)).astype(BF16)
                f_s[r : r + GELU_ROWS, cs] = gul
                total = total + rows8(gul.astype(F32))
            dbff[l, 0:1, cs] = jnp.sum(total, 0, keepdims=True)
            return 0

        loop(j0, j1, step)

        def grad(j, _):
            cs = pl.ds(tiled(j * 512, 512), 512)
            put_part(l, 4 + j, slice(None), dot(xt[...], f_s[:, cs]))
            return 0

        loop(j0 // 2, j1 // 2, grad)

    def mid(l):
        def step(j, _):
            cs = pl.ds(tiled(j * 256, 256), 256)
            acc = None
            for p in range(4):
                d = dot_nt(f_s[:, p * W : (p + 1) * W], part_rows(l, 4 + p, j * 256, 256))
                acc = d if acc is None else acc + d
            y_s[:, cs] = acc
            return 0

        loop(0, 2, step)
        if l == 1:
            keep(o.keep_f, f_s, 4).start()
            keep(o.keep_g, gp, 5).start()

        zero = jnp.zeros((8, W), F32)

        def back(j, carry):
            sg, ss, sb = carry
            rs = pl.ds(tiled(j * RUN, RUN), RUN)
            g = g_s[rs, :] + y_s[rs, :]
            xh = xh1[l, rs, :]
            sg = sg + rows8(g * xh)
            ss = ss + rows8(g)
            gy = layer_norm_back(g, vrow(l, 3), xh, rst[l, rs, 0:1])
            g_s[rs, :] = gy
            gl = gy.astype(BF16)
            go[rs, :] = gl
            sb = sb + rows8(gl.astype(F32))
            return sg, ss, sb

        sg, ss, sb = lax.fori_loop(0, 4, back, (zero,) * 3)
        dvec[l, 3:4, :] = jnp.sum(sg, 0, keepdims=True)
        dvec[l, 4:5, :] = jnp.sum(ss, 0, keepdims=True)
        dvec[l, 2:3, :] = jnp.sum(sb, 0, keepdims=True)

    def project_back(l):
        put_part(l, 3, slice(None), dot_tn(c_s[l], go[...]))
        gc = dot_nt(go[...], part(l, 3))
        for i in range(0, W, 128):
            gl = gc[:, i : i + 128].astype(BF16)
            go[:, i : i + 128] = gl
            w = gl.astype(F32) * (c_s[l, :, i : i + 128].astype(F32) + cl_s[l, :, i : i + 128].astype(F32))
            low = lane < 64
            offs = (jnp.sum(jnp.where(low, w, 0.0), -1, keepdims=True), jnp.sum(jnp.where(low, 0.0, w), -1, keepdims=True))
            for t in range(2):
                hi = offs[t].astype(BF16).astype(F32)
                off = jnp.where(spare[t] == 0, -hi, jnp.where(spare[t] == 1, hi - offs[t], 0.0))
                gh_s[t, :, i : i + 128] = gl * sides[t] + off.astype(BF16)
        xt[...] = go[...].T

    def attend_back(l, p0, p1):
        def pair(p, _):
            c0 = tiled(p * 128, 128)
            cs = pl.ds(c0, 128)
            k2 = k_s[l, :, cs]
            v2 = v_s[l, :, cs]
            qt = q_s[l, :, cs].T
            gct = xt[cs, :]
            dq = [None] * (R // ATTEND_ROWS)
            dvt, dkt = [], []
            for t in range(2):
                for i in range(len(dq)):
                    r = i * ATTEND_ROWS
                    rs = slice(r, r + ATTEND_ROWS)
                    w = dot_nt(gh_s[t, rs, cs], v2 * sides[t] + two_lanes[t])
                    for b in range(0, ATTEND_ROWS, SOFTMAX_ROWS):
                        bs = slice(r + b, r + b + SOFTMAX_ROWS)
                        ds_s[t, bs, :] = (p_s[2 * p + t, bs, :].astype(F32) * w[b : b + SOFTMAX_ROWS]).astype(BF16)
                    dd = dot(ds_s[t, rs, :], k2 * sides[t])
                    dq[i] = dd if dq[i] is None else dq[i] + dd
                hs = slice(64 * t, 64 * t + 64)
                dvt.append(dot(gct[hs], p_s[2 * p + t]))
                dkt.append(dot(qt[hs], ds_s[t]))
            dql = (jnp.concatenate(dq, 0) * 0.125).astype(BF16)
            dvl = jnp.concatenate(dvt, 0).T.astype(BF16)
            dkl = jnp.concatenate(dkt, 0).T.astype(BF16)
            gqkv[:, cs] = dql
            gqkv[:, pl.ds(tiled(c0 + W, 128), 128)] = dkl
            gqkv[:, pl.ds(tiled(c0 + 2 * W, 128), 128)] = dvl
            dvec[l, 0:1, cs] = jnp.sum(rows8(dql.astype(F32)), 0, keepdims=True)
            dvec[l, 1:2, cs] = jnp.sum(rows8(dvl.astype(F32)), 0, keepdims=True)
            return 0

        lax.fori_loop(p0, p1, pair, 0)
        if p1 == 4:
            if l == 1:
                keep(o.keep_p, p_s, 3).start()
            xt[...] = h_s[l].T

    def qkv_grad(l):
        for p in range(3):
            put_part(l, p, slice(None), dot(xt[...], gqkv[:, p * W : (p + 1) * W]))

    def qkv_back(l):
        gdst = gin1 if l == 1 else oc

        def step(j, _):
            cs = pl.ds(tiled(j * 256, 256), 256)
            acc = g_s[:, cs]
            for p in range(3):
                acc = acc + dot_nt(gqkv[:, p * W : (p + 1) * W], part_rows(l, p, j * 256, 256))
            gdst[:, cs] = acc.astype(BF16)
            return 0

        loop(0, 2, step)

    def small_grads(l):
        for i in range(Z * X * C):
            b = o.gsm.at[l, i // (X * C), (i // C) % X, i % C]
            b[...] = jnp.zeros(b.shape, F32)
            b[0:8, 0:nv] = dvec[l, :, i * nv : (i + 1) * nv]
            b[8:9, 0:nb] = dbff[l, 0:1, i * nb : (i + 1) * nb]
            for t in range(W // 128):
                b[9 + t : 10 + t, :] = o.dhw[0:1, t * 128 : (t + 1) * 128]
            b[9 + W // 128 : 10 + W // 128, 0:1] = o.dhb[...]

    steps = {
        QKV: qkv, ATTEND: attend, PROJECT: project, FF_IN: ff_in, FF_OUT: ff_out, RESTORE: restore, HEAD: head,
        TOP_BACK: top_back, FF_OUT_GRAD: ff_out_grad, FF_BACK: ff_back, MID: mid, PROJECT_BACK: project_back,
        ATTEND_BACK: attend_back, QKV_GRAD: qkv_grad, QKV_BACK: qkv_back, RELOAD: reload,
    }
    def exchange(*lists):
        for sec, todo in enumerate(lists):
            if todo:
                @pl.when(s == sec)
                def _():
                    for what, *which in todo:
                        calls[what](sec, *which)

    if fused:
        calls = {GY: ex.gy, GZ: ex.gz, GX: ex.gx, GC: ex.gc, GD: ex.gd, GE: ex.ge,
                 RC: ex.rc, R1: ex.r1, RY: ex.ry, R2: ex.r2, R3: ex.r3, R4: ex.r4, RE: ex.re}
        steps |= {EXCHANGE: exchange, SMALL_WEIGHTS: small_weights, SMALL_GRADS: small_grads, SEND_ACTS: send_acts,
                  SEND_GRAD: send_grad}
    for name, *args in FUSED_STEPS if fused else PLAIN_STEPS:
        steps[name](*args)

    if fused:
        ex.turn()
        send_act.wait()
        send_term.wait()
        own_act.wait()
        send_g[0].wait()
        own_g[0].wait()
    else:
        outs = [pltpu.make_async_copy(g1, o.g_out.at[1], sems.at[0]),
                pltpu.make_async_copy(wall.at[1], o.g_out.at[0], sems.at[1]),
                pltpu.make_async_copy(h_s.at[pl.ds(1, 2)], o.act_out, sems.at[2]),
                pltpu.make_async_copy(oc, o.gin_out.at[0], sems.at[3]),
                pltpu.make_async_copy(gin1, o.gin_out.at[1], sems.at[4])]
        for t in outs:
            t.start()
        for t in outs:
            t.wait()


def make_call(rows, width, inner, n_vec, n_bias, grid, gather=None):
    f32 = lambda *t: jax.ShapeDtypeStruct(t, F32)
    b16 = lambda *t: jax.ShapeDtypeStruct(t, BF16)
    v = lambda dt, *t: pltpu.VMEM(t, dt)
    Z, X, C = grid or (1, 1, 1)
    rp = width // (Z * X * C)
    total = PARTS * rp
    vm = pl.BlockSpec(memory_space=pltpu.VMEM)
    sm = pl.BlockSpec(memory_space=pltpu.SMEM)
    hbm = pl.BlockSpec(memory_space=pl.ANY)
    ins = dict(flag=sm, hb=sm, x_in=hbm, oc_in=hbm, tc_in=vm, mask_in=vm, hw_in=vm)
    if grid:
        ins |= dict(wq_in=vm, wo_in=vm, wi_in=vm, wf_in=vm, vec_in=vm, bff_in=vm)
        outs = dict(
            act_out=(b16(2 * rows, width), hbm), gin_out=(b16(2 * rows, width), hbm),
            term=(f32(2, 1, rows), vm),
            d_wq=(f32(1, rp, 3 * width), vm), d_wo=(f32(1, rp, width), vm), d_wi=(f32(1, rp, inner), vm),
            d_wf=(f32(1, 4 * rp, width), vm), d_small=(f32(16, 128), vm),
        )
    else:
        ins |= dict(w_in=hbm, vec_in=vm, bff_in=vm)
        outs = dict(
            act_out=(b16(2, rows, width), hbm), gin_out=(b16(2, rows, width), hbm), term=(f32(1, rows), vm),
            g_out=(b16(2, 1, 1, 1, total, width), hbm), dvec=(f32(2, 8, width), vm),
            dbff=(f32(2, 1, inner), vm), dhw=(f32(1, width), vm), dhb=(f32(1, 1), vm),
        )
    outs |= dict(keep_p=(b16(HEADS, rows, rows), hbm), keep_f=(b16(rows, inner), hbm),
             keep_g=(b16(rows, inner), hbm))
    scratch = dict(
        wall=v(BF16, 2, Z, X, C, total, width), g1=v(BF16, Z, X, C, total, width),
        q_s=v(BF16, 2, rows, width), k_s=v(BF16, 2, rows, width), v_s=v(BF16, 2, rows, width),
        p_s=v(BF16, HEADS, rows, rows), c_s=v(BF16, 2, rows, width), cl_s=v(BF16, 2, rows, width),
        xh1=v(F32, 2, rows, width), rst=v(F32, 2, rows, 2), n1=v(BF16, 2, rows, width),
        f_s=v(BF16, rows, inner), gp=v(BF16, rows, inner),
        xh2=v(F32, 2, rows, width), y_s=v(F32, rows, width),
        h_s=v(BF16, 3, rows, width), oc=v(BF16, rows, width), gin1=v(BF16, rows, width),
        mask_s=v(BF16, 2, rows, 128), g_s=v(F32, rows, width), go=v(BF16, rows, width),
        gh_s=v(BF16, 2, rows, width), ds_s=v(BF16, 2, rows, rows), gqkv=v(BF16, rows, 3 * width), xt=v(BF16, width, rows),
        cols=v(F32, rows, 8), vec=v(F32, 2, 8, width), bff=v(F32, 2, 1, inner),
        sems=pltpu.SemaphoreType.DMA((6,)),
    )
    if grid:
        late = late_parts() * rp
        kg, kr = len(GATHER) + 1, len(REDUCE) + 1
        dma = pltpu.SemaphoreType.DMA
        scratch |= dict(
            dvec=v(F32, 2, 8, width), dbff=v(F32, 2, 1, inner), dhw=v(F32, 1, width), dhb=v(F32, 1, 1),
            wsm=v(F32, 2, Z, X, C, 16, 128), gsm=v(F32, 2, Z, X, C, 16, 128),
            r1s=v(F32, 2, Z, X, 16, 128), rxs=v(F32, 2, Z, 16, 128), rzs=v(F32, 2, Z, 16, 128),
            rys=v(F32, 16, 128),
            r1=v(BF16, Z, X, total, width), ry=v(BF16, Z, X, late, width),
            rx=v(BF16, 2, Z, total, width), rz=v(BF16, 2, Z, total, width), rf=v(BF16, total, width),
            wft=v(F32, 4 * rp, width), own=v(BF16, total, width), own_small=v(F32, 16, 128),
            gs=dma((2, kg, 6)), gr=dma((2, kg, 6)), ss=dma((2, kr, 6)), sr=dma((2, kr, 6)),
            os=dma((3,)), orr=dma((3,)), credit=pltpu.SemaphoreType.REGULAR((kr,)),
        )
    names = list(ins) + list(outs) + list(scratch)
    params = dict(vmem_limit_bytes=VMEM_BYTES)
    if grid:
        params |= dict(collective_id=0, has_side_effects=True)
    call = pl.pallas_call(
        functools.partial(kernel, names, grid),
        out_shape=tuple(t[0] for t in outs.values()),
        in_specs=list(ins.values()),
        out_specs=tuple(t[1] for t in outs.values()),
        scratch_shapes=list(scratch.values()),
        compiler_params=pltpu.CompilerParams(**params),
    )
    return call, list(outs)


def hand_over(act, gin, term, wq, wo, wi, wf, small, act_o, gin_o, term_o, wq_o, wo_o, wi_o, wf_o, vec_o, bff_o, hw_o,
              hb_o, sems):
    moves = [pltpu.make_async_copy(a, b, sems.at[i]) for i, (a, b) in enumerate(
        ((act, act_o.at[0]), (gin, gin_o.at[0]), (wq, wq_o), (wo, wo_o), (wi, wi_o), (wf, wf_o)))]
    for m in moves:
        m.start()
    rows, heads = term.shape[2], hw_o.shape[0] // 128
    for i in range(term.shape[0]):
        term_o[i * rows : (i + 1) * rows] = term[i, 0].astype(BF16)
    vec_o[0] = small[0:8, 0 : vec_o.shape[2]]
    bff_o[...] = small[8:9, 0 : bff_o.shape[1]]
    for i in range(heads):
        hw_o[i * 128 : (i + 1) * 128] = small[9 + i, :]
    hb_o[...] = small[9 + heads, 0:1]
    for m in moves:
        m.wait()


def fused_local(grid, tokens_in, out_cot, term_cot, long_flag, token_mask, w_qkv, w_out, w_ff_in, w_ff_out, vectors,
                ff_bias, head_weight, head_bias):
    section = lax.axis_index("section")
    width = tokens_in.shape[1]
    micro = long_flag.shape[0]
    rows = tokens_in.shape[0] // micro
    call, names = make_call(rows, width, w_ff_in.shape[2], vectors.shape[2], ff_bias.shape[1], grid)
    res = types.SimpleNamespace(**dict(zip(names, call(long_flag, head_bias, tokens_in, out_cot, term_cot, token_mask,
                                                      head_weight, w_qkv, w_out, w_ff_in, w_ff_out, vectors, ff_bias))))
    vm, hbm = pl.BlockSpec(memory_space=pltpu.VMEM), pl.BlockSpec(memory_space=pl.ANY)
    f32 = lambda *t: jax.ShapeDtypeStruct(t, F32)
    b16 = lambda *t: jax.ShapeDtypeStruct(t, BF16)
    both = b16(1, micro * rows, width)
    acts, gins, *rest = pl.pallas_call(
        hand_over,
        out_shape=(both, both, b16(micro * rows), f32(*w_qkv.shape), f32(*w_out.shape), f32(*w_ff_in.shape),
                   f32(*w_ff_out.shape), f32(*vectors.shape), f32(*ff_bias.shape), f32(width), f32(1)),
        in_specs=[hbm, hbm, vm, hbm, hbm, hbm, hbm, vm],
        out_specs=(vm,) * 11,
        scratch_shapes=[pltpu.SemaphoreType.DMA((6,))],
    )(res.act_out, res.gin_out, res.term, res.d_wq, res.d_wo, res.d_wi, res.d_wf, res.d_small)
    return (acts, rest[0], gins, *rest[1:])


def plain_local(tokens_in, out_cot, term_cot, long_flag, token_mask, w_qkv, w_out, w_ff_in, w_ff_out, vectors, ff_bias,
                head_weight, head_bias):
    section = lax.axis_index("section")
    width = tokens_in.shape[1]
    micro = long_flag.shape[0]
    rows = tokens_in.shape[0] // micro
    inner = w_ff_in.shape[2]
    everyone = lambda a, ax: lax.all_gather(lax.all_gather(a, "dp", axis=ax, tiled=True), "section", axis=0, tiled=True)
    wq, wo, wi, wf = (everyone(a, 1) for a in (w_qkv, w_out, w_ff_in, w_ff_out))
    vec = everyone(vectors, 2).astype(F32)
    bff = everyone(ff_bias, 1).astype(F32)[:, None]
    cut = lambda a: a.reshape(2, width, -1, width).transpose(0, 2, 1, 3).reshape(2, -1, width)
    wall = jnp.concatenate([cut(wq), wo, cut(wi), wf], 1)[:, None, None, None]
    call, names = make_call(rows, width, inner, width, inner, None)
    res = types.SimpleNamespace(**dict(zip(names, call(long_flag, head_bias, tokens_in, out_cot, term_cot, token_mask,
                                                      head_weight, wall, vec, bff))))
    swap = lambda a: lax.all_gather(a, "section", axis=1, tiled=True)[section][None]
    terms = lax.all_gather(res.term[0], "section", axis=0, tiled=True).astype(BF16)

    def scatter(a, ax):
        a = lax.psum_scatter(a.astype(F32), "section", scatter_dimension=0, tiled=True)
        return lax.psum_scatter(a, "dp", scatter_dimension=ax, tiled=True)

    g = res.g_out[:, 0, 0, 0]
    glue = lambda a, n: a.reshape(2, n, width, width).transpose(0, 2, 1, 3).reshape(2, width, n * width)
    turned = lambda a: a.reshape(2, -1, 128, width // 128, 128).transpose(0, 1, 4, 3, 2).reshape(2, -1, width)
    dhw, dhb = lax.psum((res.dhw[0], res.dhb[0]), ("section", "dp"))
    return (
        swap(res.act_out), terms, swap(res.gin_out),
        scatter(glue(g[:, : 3 * width], 3), 1), scatter(g[:, 3 * width : 4 * width], 1),
        scatter(glue(g[:, 4 * width : 8 * width], 4), 1), scatter(turned(g[:, 8 * width :]), 1),
        scatter(res.dvec, 2), scatter(res.dbff[:, 0], 1), dhw, dhb,
    )


def solution(mesh):
    dp = mesh.shape["dp"]
    if dp == 16:
        local = functools.partial(fused_local, (4, 2, 2))
    else:
        local = plain_local
    shard = P("section", "dp", None)
    in_specs = (P("dp", None), P("dp", None), P("dp"), P("dp"), P("dp"), shard, shard, shard, shard,
                P("section", None, "dp"), P("section", "dp"), P(), P())
    out_specs = (shard, P("dp"), shard, shard, shard, shard, shard, P("section", None, "dp"), P("section", "dp"),
                 P(), P())
    return jax.shard_map(local, mesh=mesh, in_specs=in_specs, out_specs=out_specs, check_vma=False)
```

```python
import functools
import types

import jax
import jax.numpy as jnp
from jax import lax
from jax.experimental import pallas as pl
from jax.experimental.pallas import tpu as pltpu
from jax.sharding import PartitionSpec as P

RUN = 128
HEADS = 8
EPS = 1e-12
F32, BF16 = jnp.float32, jnp.bfloat16
VMEM_BYTES = 64 * 2**20
GELU_ROWS = 64
ATTEND_ROWS = 256
SOFTMAX_ROWS = 64


def dot(a, b):
    return lax.dot_general(a, b, (((1,), (0,)), ((), ())), preferred_element_type=F32)


def dot_nt(a, b):
    return lax.dot_general(a, b, (((1,), (1,)), ((), ())), preferred_element_type=F32)


def dot_tn(a, b):
    return lax.dot_general(a, b, (((0,), (0,)), ((), ())), preferred_element_type=F32)


def rows8(v):
    return jnp.sum(v.reshape(-1, 8, v.shape[1]), axis=0)


def tiled(i, n):
    return i if isinstance(i, int) else pl.multiple_of(i, n)


def loop(start, stop, step):
    for j in range(start, stop):
        step(j, 0)


def gelu_both(u):
    w = jnp.abs(u)
    e = jnp.exp2(u * u * -0.7213475204444817)
    d = w * (0.3275911 * 0.7071067811865476) + 1.0
    t = pl.reciprocal(d, approx=True)
    t = t * (2.0 - d * t)
    q = t * 0.5307027145 - 0.7265760135
    q = q * t + 0.7107068705
    q = q * t - 0.142248368
    q = q * t + 0.127414796
    q = q * t * e
    n = q - w * (e * 0.3989422804014327)
    return jnp.maximum(u, 0.0) - w * q, jnp.where(u >= 0.0, 1.0 - n, n)


def layer_norm_rows(y):
    c = y - jnp.mean(y, -1, keepdims=True)
    r = lax.rsqrt(jnp.mean(c * c, -1, keepdims=True) + EPS)
    return c * r, r


def layer_norm_back(g, gain, xh, r):
    gx = g * gain
    a = jnp.mean(gx, -1, keepdims=True)
    b = jnp.mean(gx * xh, -1, keepdims=True)
    return (gx - a - xh * b) * r


MESH = pl.DeviceIdType.MESH
(QKV, ATTEND, PROJECT, FF_IN, FF_OUT, RESTORE, HEAD, TOP_BACK, FF_OUT_GRAD, FF_BACK, MID, PROJECT_BACK, ATTEND_BACK,
 QKV_GRAD, QKV_BACK, RELOAD, EXCHANGE, SMALL_WEIGHTS, SMALL_GRADS, SEND_ACT, SEND_GRAD) = range(21)
GY, GZ, GF, GX, GC, GD, GE, RC, R1, RY, R2, RP, R3, R4, RE = range(15)
BOTH, OWN, OTHER, X_OWN, X_OTHER = range(5)
ALONG_Z, ALONG_X, SHARD, PLANE, COLUMN, PASS_ON, TO_CORE = range(7)
PARTS = 12
GATHER = ((0, 1), (1, 1), (2, 1), (3, 1), (4, 1), (5, 1), (6, 1), (7, 1), (8, 1), (9, 1), (10, 1), (11, 1))
GATHER_ROUTE = ((OWN, OWN, X_OTHER, BOTH, X_OTHER, BOTH, X_OWN, X_OTHER, OWN, X_OTHER, X_OWN, OTHER), (OWN, X_OTHER, BOTH, X_OTHER, X_OWN, OWN, OTHER, BOTH, OTHER, BOTH, OWN, BOTH))
REDUCE = ((0, 1), (1, 1), (2, 1), (3, 1), (4, 2), (6, 2), (8, 2), (10, 2))
REDUCE_ROUTE = ((OWN, X_OTHER, X_OTHER, BOTH, X_OWN, X_OWN, X_OTHER, BOTH), (X_OTHER, OTHER, X_OWN, BOTH, BOTH, X_OTHER, X_OWN, BOTH))


def late_place(l, k):
    takes = lambda a, b: a if REDUCE_ROUTE[a][b] in (OWN, X_OWN) else 1 - a
    kind = (OWN, OTHER) if REDUCE_ROUTE[l][k] in (OWN, OTHER) else (X_OWN, X_OTHER)
    at = 0
    for a in range(2):
        for b, (_, n) in enumerate(REDUCE):
            if (a, b) == (l, k):
                return at, n
            if REDUCE_ROUTE[a][b] in kind and takes(a, b) == takes(l, k):
                at += n
    return at, 0


def late_parts(kind):
    ends = [sum(late_place(l, k)) for l in range(2) for k in range(len(REDUCE)) if REDUCE_ROUTE[l][k] in kind]
    return max(ends, default=1)


def layer_steps(l):
    return (
        ((RESTORE, 0),) if l else ()) + (
        (QKV, l), (ATTEND, l, 0, 4), (PROJECT, l)) + (
        ((RESTORE, 1), (RESTORE, 2)) if l else ()) + (
        (FF_IN, l, 0, 8), (FF_OUT, l))


def layer_back_steps(l):
    return (
        () if l else ((RELOAD, 0), (RELOAD, 1), (RELOAD, 2))) + (
        (TOP_BACK, l), (FF_OUT_GRAD, l), (FF_BACK, l, 0, 8), (MID, l), (PROJECT_BACK, l),
        (ATTEND_BACK, l, 0, 4), (QKV_BACK, l), (QKV_GRAD, l))


PLAIN_STEPS = layer_steps(0) + layer_steps(1) + ((HEAD,),) + layer_back_steps(1) + layer_back_steps(0)


FUSED_STEPS = (
    (EXCHANGE, (
        (GY, 0, 12), (GY, 0, 2), (GY, 0, 10), (GY, 0, 3), (GZ, 0, 12), (GY, 0, 6), (GZ, 0, 0), (GY, 0, 11),
        (GZ, 0, 1), (GY, 0, 5), (GY, 0, 4), (GY, 0, 7), (GZ, 1, 12), (GF, 0, 12), (GZ, 0, 2), (GY, 0, 9), (GF, 0, 0),
        (GZ, 0, 10), (GX, 0, 12), (GF, 0, 1), (GZ, 0, 3), (GF, 1, 12), (GX, 0, 0), (GC, 0, 12), (GZ, 0, 6),
        (GF, 0, 2), (GD, 0, 12),
    ), (
        (GY, 1, 12), (GY, 1, 4), (GY, 1, 6), (GY, 1, 2), (GZ, 1, 12), (GY, 1, 11), (GZ, 1, 4), (GY, 1, 8),
        (GZ, 1, 0), (GY, 1, 1), (GY, 1, 7), (GY, 1, 9), (GZ, 0, 12), (GF, 1, 12), (GZ, 0, 2), (GY, 1, 3), (GF, 1, 4),
        (GZ, 0, 6), (GX, 1, 12), (GF, 1, 0), (GZ, 0, 4), (GF, 0, 12), (GX, 1, 4), (GC, 1, 12), (GZ, 0, 7),
        (GF, 0, 2), (GD, 1, 12), (GX, 1, 0), (GX, 0, 12), (GZ, 0, 11), (GF, 0, 6), (GX, 0, 2), (GZ, 0, 9),
        (GC, 1, 4), (GF, 0, 4), (GX, 0, 6), (GD, 1, 4), (GZ, 0, 5), (GF, 0, 7), (GC, 1, 0), (GC, 0, 12), (GX, 0, 4),
        (GZ, 0, 3), (GD, 1, 0), (GF, 0, 11), (GD, 0, 12),
    )),
    (SMALL_WEIGHTS, 0),
    (EXCHANGE, (
        (GX, 0, 1), (GX, 1, 12), (GZ, 1, 1), (GF, 0, 10), (GX, 0, 2), (GZ, 0, 8), (GC, 0, 0), (GF, 0, 3),
        (GX, 0, 10), (GD, 0, 0), (GZ, 1, 3), (GF, 0, 6), (GC, 0, 1), (GC, 1, 12), (GX, 0, 3), (GZ, 0, 5), (GD, 0, 1),
        (GF, 1, 1), (GD, 1, 12), (GX, 0, 6), (GZ, 0, 4), (GF, 0, 8), (GC, 0, 10), (GX, 1, 1), (GZ, 1, 6),
        (GD, 0, 10), (GF, 1, 3), (GC, 0, 3), (GX, 0, 8), (GZ, 1, 2), (GF, 0, 5), (GC, 1, 0), (GD, 0, 3), (GX, 1, 3),
        (GZ, 1, 8), (GC, 0, 6), (GD, 1, 0), (GF, 0, 4), (GC, 0, 2), (GD, 0, 6), (GX, 0, 5), (GZ, 0, 7), (GF, 1, 6),
        (GC, 1, 1), (GD, 0, 2),
    ), (
        (GX, 0, 7), (GZ, 1, 5), (GC, 0, 2), (GF, 0, 9), (GX, 0, 11), (GD, 0, 2), (GC, 0, 0), (GZ, 1, 2), (GF, 0, 5),
        (GC, 0, 4), (GD, 0, 0), (GX, 0, 9), (GZ, 1, 10), (GD, 0, 4), (GF, 0, 3), (GC, 0, 7), (GX, 0, 5), (GZ, 1, 11),
        (GF, 1, 5), (GD, 0, 7), (GC, 0, 1), (GX, 0, 3), (GZ, 0, 10), (GC, 0, 11), (GF, 1, 2), (GD, 0, 1),
    )),
    (QKV, 0),
    (EXCHANGE, (
        (GX, 0, 4),
    ), (
    )),
    (ATTEND, 0, 0, 1),
    (EXCHANGE, (
        (GF, 1, 2), (GC, 0, 4), (GZ, 0, 9), (GD, 1, 1),
    ), (
        (GX, 1, 5), (GF, 1, 10), (GC, 0, 9), (GZ, 1, 1), (GD, 0, 11),
    )),
    (ATTEND, 0, 1, 2),
    (EXCHANGE, (
        (GX, 1, 6), (GF, 1, 8), (GC, 0, 8), (GZ, 1, 7), (GD, 0, 4),
    ), (
        (GX, 1, 2), (GF, 1, 11), (GC, 0, 6), (GZ, 1, 7), (GD, 0, 9),
    )),
    (ATTEND, 0, 2, 3),
    (EXCHANGE, (
        (GX, 1, 2), (GC, 1, 3), (GF, 0, 7), (GZ, 1, 11), (GD, 0, 8),
    ), (
        (GX, 1, 10), (GC, 0, 5), (GZ, 1, 9), (GF, 0, 10), (GD, 0, 6),
    )),
    (ATTEND, 0, 3, 4),
    (EXCHANGE, (
        (GX, 1, 8), (GZ, 1, 9), (GD, 1, 3),
    ), (
        (GX, 1, 11), (GD, 0, 5), (GZ, 1, 3), (GC, 0, 3), (GF, 1, 1), (GD, 0, 3),
    )),
    (PROJECT, 0),
    (EXCHANGE, (
        (GF, 0, 9), (GC, 0, 5),
    ), (
        (GX, 0, 10), (GC, 0, 10), (GF, 1, 7),
    )),
    (FF_IN, 0, 0, 2),
    (EXCHANGE, (
        (GX, 0, 7), (GC, 0, 11), (GC, 0, 7), (GZ, 1, 4), (GD, 0, 5), (GF, 1, 7),
    ), (
        (GC, 1, 5),
    )),
    (FF_IN, 0, 2, 4),
    (EXCHANGE, (
        (GC, 1, 6), (GD, 0, 11),
    ), (
        (GX, 1, 1), (GF, 1, 9), (GC, 0, 8), (GC, 1, 1), (GD, 0, 10),
    )),
    (FF_IN, 0, 4, 6),
    (EXCHANGE, (
        (GX, 0, 9), (GF, 1, 11), (GC, 0, 9), (GD, 0, 7),
    ), (
        (GX, 1, 7), (GC, 1, 2), (GD, 1, 5),
    )),
    (FF_IN, 0, 6, 8),
    (EXCHANGE, (
        (GX, 1, 7), (GD, 1, 6), (GC, 1, 2), (GD, 0, 9),
    ), (
        (GF, 1, 3), (GD, 0, 8), (GD, 1, 1),
    )),
    (FF_OUT, 0),
    (EXCHANGE, (
        (GF, 1, 9), (GD, 1, 2),
    ), (
        (GX, 1, 9), (GC, 1, 10), (GD, 1, 2),
    )),
    (SEND_ACT, 0),
    (EXCHANGE, (
        (GX, 1, 11),
    ), (
    )),
    (SMALL_WEIGHTS, 1),
    (RESTORE, 0),
    (QKV, 1),
    (EXCHANGE, (
        (GF, 1, 4), (GC, 1, 8),
    ), (
    )),
    (ATTEND, 1, 0, 1),
    (EXCHANGE, (
    ), (
        (GX, 1, 3), (GC, 1, 11), (GC, 1, 3), (GD, 1, 10),
    )),
    (ATTEND, 1, 1, 2),
    (EXCHANGE, (
        (GX, 1, 9), (GC, 1, 7), (GC, 1, 5), (GD, 1, 8),
    ), (
        (GC, 1, 6), (GD, 1, 11),
    )),
    (ATTEND, 1, 2, 3),
    (EXCHANGE, (
        (GX, 1, 4), (GC, 1, 4), (GD, 1, 7),
    ), (
        (GC, 1, 7), (GD, 1, 3), (GD, 1, 6),
    )),
    (ATTEND, 1, 3, 4),
    (EXCHANGE, (
        (GC, 1, 11), (GD, 1, 5), (GD, 1, 4),
    ), (
    )),
    (PROJECT, 1),
    (EXCHANGE, (
    ), (
        (GD, 1, 7),
    )),
    (RESTORE, 1),
    (RESTORE, 2),
    (FF_IN, 1, 0, 2),
    (EXCHANGE, (
        (GD, 1, 11),
    ), (
        (GC, 1, 9),
    )),
    (FF_IN, 1, 2, 4),
    (EXCHANGE, (
        (GC, 1, 10), (GC, 1, 9),
    ), (
        (GC, 1, 8),
    )),
    (FF_IN, 1, 4, 6),
    (EXCHANGE, (
    ), (
        (GD, 1, 9),
    )),
    (FF_IN, 1, 6, 8),
    (EXCHANGE, (
        (GD, 1, 10), (GD, 1, 9),
    ), (
        (GD, 1, 8),
    )),
    (FF_OUT, 1),
    (HEAD,),
    (SEND_ACT, 1),
    (TOP_BACK, 1),
    (FF_OUT_GRAD, 1),
    (EXCHANGE, (
        (RC, 1, 7), (RC, 1, 6),
    ), (
        (RC, 1, 7), (RC, 1, 6),
    )),
    (FF_BACK, 1, 0, 2),
    (FF_BACK, 1, 2, 4),
    (EXCHANGE, (
        (RC, 1, 4),
    ), (
        (RC, 1, 4),
    )),
    (FF_BACK, 1, 4, 6),
    (EXCHANGE, (
        (R1, 1, 7),
    ), (
        (R1, 1, 7),
    )),
    (FF_BACK, 1, 6, 8),
    (EXCHANGE, (
        (R1, 1, 6), (RC, 1, 5), (R1, 1, 4),
    ), (
        (R1, 1, 6), (RC, 1, 5), (R1, 1, 4),
    )),
    (MID, 1),
    (EXCHANGE, (
        (R1, 1, 5),
    ), (
        (R1, 1, 5),
    )),
    (PROJECT_BACK, 1),
    (EXCHANGE, (
        (RC, 1, 3),
    ), (
        (RC, 1, 3),
    )),
    (ATTEND_BACK, 1, 0, 1),
    (ATTEND_BACK, 1, 1, 2),
    (EXCHANGE, (
        (RP, 1, 6), (R1, 1, 3),
    ), (
        (R1, 1, 3),
    )),
    (ATTEND_BACK, 1, 2, 3),
    (EXCHANGE, (
        (R2, 1, 7),
    ), (
        (R2, 1, 7),
    )),
    (ATTEND_BACK, 1, 3, 4),
    (EXCHANGE, (
    ), (
        (RP, 1, 5),
    )),
    (QKV_GRAD, 1),
    (EXCHANGE, (
        (RC, 1, 2), (RC, 1, 0), (RC, 1, 1),
    ), (
        (RC, 1, 2), (RC, 1, 0), (RC, 1, 1),
    )),
    (QKV_BACK, 1),
    (EXCHANGE, (
        (R3, 1, 6),
    ), (
    )),
    (SEND_GRAD, 1),
    (SMALL_GRADS, 1),
    (EXCHANGE, (
        (R1, 1, 2), (RY, 1, 5), (R1, 1, 0), (R1, 1, 1), (RC, 1, 8),
    ), (
        (RC, 1, 8),
    )),
    (RELOAD, 1),
    (EXCHANGE, (
    ), (
        (R1, 1, 2),
    )),
    (RELOAD, 2),
    (EXCHANGE, (
    ), (
        (R1, 1, 0),
    )),
    (EXCHANGE, (
        (GE, 0), (GE, 1),
    ), (
        (GE, 0), (GE, 1),
    )),
    (TOP_BACK, 0),
    (EXCHANGE, (
        (RP, 1, 7), (R2, 1, 4), (R1, 1, 8),
    ), (
        (R1, 1, 1), (R2, 1, 4), (R3, 1, 5), (RP, 1, 7), (RY, 1, 6), (R1, 1, 8),
    )),
    (FF_OUT_GRAD, 0),
    (EXCHANGE, (
        (RC, 0, 7), (RC, 0, 6),
    ), (
        (RC, 0, 7), (RC, 0, 6),
    )),
    (FF_BACK, 0, 0, 2),
    (EXCHANGE, (
        (R2, 1, 3), (RP, 1, 2),
    ), (
        (R2, 1, 3), (RP, 1, 0),
    )),
    (FF_BACK, 0, 2, 4),
    (EXCHANGE, (
        (RC, 0, 4),
    ), (
        (RC, 0, 4),
    )),
    (FF_BACK, 0, 4, 6),
    (EXCHANGE, (
        (R1, 0, 7), (R1, 0, 6), (R3, 1, 7), (RY, 1, 0), (R1, 0, 4),
    ), (
        (R1, 0, 7), (R3, 1, 7), (R1, 0, 6),
    )),
    (FF_BACK, 0, 6, 8),
    (EXCHANGE, (
        (R3, 1, 2), (RP, 1, 4), (RC, 0, 5),
    ), (
        (R1, 0, 4), (RC, 0, 5), (RP, 1, 4), (R3, 1, 0),
    )),
    (MID, 0),
    (EXCHANGE, (
        (R2, 1, 5), (R1, 0, 5), (R2, 1, 8), (RP, 1, 3),
    ), (
        (R1, 0, 5),
    )),
    (PROJECT_BACK, 0),
    (EXCHANGE, (
        (RY, 1, 1), (RC, 0, 3),
    ), (
        (RP, 1, 3), (R2, 1, 6), (R2, 1, 8), (RC, 0, 3),
    )),
    (RELOAD, 0),
    (ATTEND_BACK, 0, 0, 1),
    (EXCHANGE, (
        (R3, 1, 4), (R1, 0, 3),
    ), (
        (R3, 1, 4), (R1, 0, 3),
    )),
    (ATTEND_BACK, 0, 1, 2),
    (EXCHANGE, (
        (R3, 1, 3), (RP, 0, 6),
    ), (
        (RP, 0, 4), (R3, 1, 3),
    )),
    (ATTEND_BACK, 0, 2, 3),
    (EXCHANGE, (
        (R2, 0, 7),
    ), (
        (RY, 1, 2),
    )),
    (ATTEND_BACK, 0, 3, 4),
    (EXCHANGE, (
        (RY, 0, 4), (RP, 1, 5),
    ), (
        (R2, 0, 7),
    )),
    (QKV_GRAD, 0),
    (EXCHANGE, (
        (R2, 1, 0), (RC, 0, 0), (RC, 0, 2), (RC, 0, 1), (R3, 0, 6),
    ), (
        (RP, 0, 5), (RC, 0, 0), (RC, 0, 2), (RC, 0, 1),
    )),
    (QKV_BACK, 0),
    (EXCHANGE, (
    ), (
        (R3, 0, 4), (R2, 0, 3), (R1, 0, 0),
    )),
    (SEND_GRAD, 0),
    (EXCHANGE, (
        (R3, 1, 8), (R1, 0, 0),
    ), (
        (R1, 0, 2),
    )),
    (SMALL_GRADS, 0),
    (EXCHANGE, (
        (R1, 0, 2), (R2, 1, 1), (R1, 0, 1), (RC, 0, 8), (R3, 1, 5), (RY, 0, 5), (RP, 0, 7), (R1, 0, 8), (R2, 0, 3),
        (RP, 1, 0), (R3, 0, 7), (RP, 0, 2), (R3, 1, 0), (R2, 0, 4), (RY, 0, 0), (RP, 1, 1), (R3, 0, 2), (RP, 0, 1),
        (R3, 1, 1), (RP, 0, 3), (R2, 0, 5), (R3, 0, 1), (R2, 0, 8), (RP, 0, 4), (R3, 0, 3), (R2, 0, 0), (RP, 0, 5),
        (R3, 0, 4), (R4, 0, 4), (R4, 0, 7), (R4, 0, 3), (R3, 0, 8), (R4, 0, 8), (RP, 0, 0), (R4, 0, 6), (R3, 0, 5),
        (R4, 0, 5), (R4, 0, 2), (R3, 0, 0), (R4, 0, 1),
    ), (
        (R1, 0, 1), (RC, 0, 8), (RY, 0, 6), (R2, 1, 2), (RP, 1, 6), (R1, 0, 8), (R3, 0, 5), (R4, 1, 7), (R3, 1, 8),
        (R4, 1, 4), (R4, 1, 3), (R4, 1, 8), (R3, 1, 6), (R4, 1, 6), (RP, 0, 7), (RY, 0, 2), (R2, 0, 6), (RP, 0, 3),
        (R2, 0, 8), (RY, 0, 1), (R3, 0, 7), (RP, 1, 2), (R4, 1, 5), (R4, 1, 0), (R3, 0, 3), (R2, 0, 2), (R3, 1, 2),
        (R4, 1, 2), (RP, 0, 6), (R4, 1, 1), (R2, 0, 1), (R3, 0, 8), (RP, 0, 2), (R3, 0, 6), (RP, 0, 1), (R3, 0, 2),
        (R3, 0, 1),
    )),
    (EXCHANGE, (
        (RE, 1), (RE, 0),
    ), (
        (RE, 1), (RE, 0),
    )),
)


class Exchange:
    def __init__(self, o, grid, rp):
        self.o, self.rp = o, rp
        self.Z, self.X, self.C = grid
        self.s = lax.axis_index("section")
        d = lax.axis_index("dp")
        self.c = lax.rem(d, 2)
        self.x = lax.rem(d // 2, 2)
        self.z = d // 4

    def dev(self, s=None, z=None, x=None, c=None):
        s = self.s if s is None else s
        z = self.z if z is None else z
        x = self.x if x is None else x
        c = self.c if c is None else c
        return (s, (z * 2 + x) * 2 + c)

    def along_z(self, j):
        return lax.rem(self.z + j + 1, self.Z)

    def peers(self):
        out = [self.dev(z=self.along_z(j)) for j in range(self.Z - 1)]
        return out + [self.dev(x=1 - self.x), self.dev(c=1 - self.c), self.dev(s=1 - self.s)]

    def greet(self):
        for p in self.peers():
            pl.semaphore_signal(pltpu.get_barrier_semaphore(), inc=1, device_id=p, device_id_type=MESH)

    def met(self):
        pl.semaphore_wait(pltpu.get_barrier_semaphore(), len(self.peers()))

    def copy(self, src, dst, send, recv, dev):
        return pltpu.make_async_remote_copy(
            src_ref=src, dst_ref=dst, send_sem=send, recv_sem=recv, device_id=dev, device_id_type=MESH)

    def g_route(self, l, k):
        return BOTH if k == len(GATHER) else GATHER_ROUTE[l][k]

    def works(self, route, s, l):
        own, other = (OWN, X_OWN) if s == l else (OTHER, X_OTHER), (X_OTHER if s == l else X_OWN,)
        return route == BOTH or route in own, route == BOTH or route in own + other

    def g_copy(self, kind, s, l, k, j=0):
        o = self.o
        z, x, c = self.z, self.x, self.c
        if k == len(GATHER):
            w, mine, rows = o.wsm.at[l], o.own_small, slice(None)
        else:
            p, n = GATHER[k]
            w, mine, rows = o.wall.at[l], o.own, slice(p * self.rp, (p + n) * self.rp)
        ss, rr = o.gs.at[l, k], o.gr.at[l, k]
        if kind == ALONG_Z:
            a = w.at[z, x, c, rows]
            return self.copy(a, a, ss.at[j], rr.at[j], self.dev(z=self.along_z(j)))
        if kind == ALONG_X:
            a = w.at[:, x, c, rows]
            return self.copy(a, a, ss.at[3], rr.at[3], self.dev(x=1 - x))
        if kind == SHARD:
            return self.copy(mine.at[rows], w.at[z, x, c, rows], ss.at[4], rr.at[4], self.dev(s=1 - s))
        a = w.at[:, :, c, rows]
        if kind == PLANE:
            return self.copy(a, a, ss.at[4], rr.at[4], self.dev(s=1 - s))
        if kind == COLUMN:
            a = w.at[:, 1 - x, c, rows]
            return self.copy(a, a, ss.at[6], rr.at[6], self.dev(s=1 - s))
        if kind == PASS_ON:
            to = self.z // 2 * 3
            a = w.at[3 - to, x, c, rows]
            return self.copy(a, a, ss.at[7], rr.at[self.z // 2 * 2], self.dev(z=to))
        return self.copy(a, a, ss.at[5], rr.at[5], self.dev(c=1 - c))

    def gy(self, s, l, k):
        self.g_copy(SHARD, s, l, k).start()

    def unless_end(self, j, f):
        if j == 1:
            f()
        else:
            pl.when(self.z != (0 if j == 2 else self.Z - 1))(f)

    def on_middle(self, f):
        pl.when((self.z > 0) & (self.z < self.Z - 1))(f)

    def on_ends(self, f):
        pl.when((self.z == 0) | (self.z == self.Z - 1))(f)

    def gz(self, s, l, k):
        if s != l:
            self.g_copy(SHARD, s, l, k).wait_recv()
        for j in range(self.Z - 1):
            self.unless_end(j, self.g_copy(ALONG_Z, s, l, k, j).start)

    def gf(self, s, l, k):
        @self.on_middle
        def _():
            self.g_copy(ALONG_Z, s, l, k, 1).wait_recv()
            self.g_copy(PASS_ON, s, l, k).start()

    def gx(self, s, l, k):
        self.g_copy(ALONG_Z, s, l, k, 0).wait_recv()
        self.on_ends(self.g_copy(ALONG_Z, s, l, k, 1).wait_recv)
        self.g_copy(ALONG_Z, s, l, k, 2).wait_recv()
        if self.works(self.g_route(l, k), s, l)[0]:
            self.g_copy(ALONG_X, s, l, k).start()

    def gc(self, s, l, k):
        route = self.g_route(l, k)
        on_x, on_z = self.works(route, s, l)
        beyond = PLANE if route in (OWN, OTHER) else COLUMN
        if on_x:
            self.g_copy(ALONG_X, s, l, k).wait_recv()
            if route != BOTH:
                self.g_copy(beyond, s, l, k).start()
        else:
            self.g_copy(beyond, s, l, k).wait_recv()
        self.g_copy(TO_CORE, s, l, k).start()

    def gd(self, s, l, k):
        self.g_copy(TO_CORE, s, l, k).wait_recv()

    def ge(self, s, l):
        for k in range(len(GATHER) + 1):
            route = self.g_route(l, k)
            on_x, on_z = self.works(route, s, l)
            if s == l and route != OWN:
                self.g_copy(SHARD, s, l, k).wait_send()
            if on_z:
                for j in range(self.Z - 1):
                    self.unless_end(j, self.g_copy(ALONG_Z, s, l, k, j).wait_send)
                self.on_middle(self.g_copy(PASS_ON, s, l, k).wait_send)
            if on_x:
                self.g_copy(ALONG_X, s, l, k).wait_send()
                if route != BOTH:
                    self.g_copy(PLANE if route in (OWN, OTHER) else COLUMN, s, l, k).wait_send()
            self.g_copy(TO_CORE, s, l, k).wait_send()

    def r_small(self, k):
        return k == len(REDUCE)

    def r_route(self, l, k):
        return BOTH if self.r_small(k) else REDUCE_ROUTE[l][k]

    def r_bufs(self, l, k):
        o = self.o
        if self.r_small(k):
            return o.gsm.at[l], slice(None), o.r1s.at[l], o.rxs.at[l], o.rzs.at[l], o.rys
        p, n = REDUCE[k]
        g = o.g1 if l == 1 else o.wall.at[1]
        return g, slice(p * self.rp, (p + n) * self.rp), o.r1, o.rx.at[l], o.rz.at[l], o.rf

    def r_late(self, l, k):
        at, n = late_place(l, k)
        return slice(at * self.rp, (at + n) * self.rp)

    def r_copy(self, kind, s, l, k, j=0):
        o = self.o
        g, rows, r1, rx, rz, rf = self.r_bufs(l, k)
        z, x, c = self.z, self.x, self.c
        ss, rr = o.ss.at[l, k], o.sr.at[l, k]
        if kind == TO_CORE:
            return self.copy(g.at[:, :, 1 - c, rows], r1.at[:, :, rows], ss.at[0], rr.at[0], self.dev(c=1 - c))
        if kind == ALONG_X:
            return self.copy(g.at[:, 1 - x, c, rows], rx.at[:, rows], ss.at[1], rr.at[1], self.dev(x=1 - x))
        if kind == ALONG_Z:
            to = self.along_z(j)
            return self.copy(g.at[to, x, c, rows], rz.at[z, rows], ss.at[2 + j], rr.at[2 + j], self.dev(z=to))
        if kind == PASS_ON:
            to = z // 2 + 1
            return self.copy(g.at[self.Z - 1 - z, x, c, rows], rz.at[to, rows], ss.at[7], rr.at[7], self.dev(z=to))
        if kind == COLUMN:
            return self.copy(g.at[:, 1 - x, c, rows], o.rcol.at[:, self.r_late(l, k)], ss.at[6], rr.at[6],
                             self.dev(s=1 - s))
        if kind == PLANE:
            return self.copy(g.at[:, :, c, rows], o.ry.at[:, :, self.r_late(l, k)], ss.at[5], rr.at[5],
                             self.dev(s=1 - s))
        return self.copy(g.at[z, x, c, rows], rf.at[rows], ss.at[5], rr.at[5], self.dev(s=1 - s))

    def add(self, n, dst, src):
        def one(i, _):
            d = dst(i)
            d[...] = d[...] + src(i)[...]
            return 0

        lax.fori_loop(0, n, one, 0)

    def rc(self, s, l, k):
        if l == 0 and not self.r_small(k):
            pl.semaphore_wait(self.o.credit.at[k], 1)
        self.r_copy(TO_CORE, s, l, k).start()

    def r1(self, s, l, k):
        g, rows, r1, rx, rz, rf = self.r_bufs(l, k)
        c, X = self.c, self.X
        self.r_copy(TO_CORE, s, l, k).wait_recv()
        self.add(self.Z * X, lambda i: g.at[i // X, lax.rem(i, X), c, rows], lambda i: r1.at[i // X, lax.rem(i, X), rows])
        if l == 1 and not self.r_small(k):
            pl.semaphore_signal(self.o.credit.at[k], inc=1, device_id=self.dev(c=1 - c), device_id_type=MESH)
        route = self.r_route(l, k)
        on_x, on_z = self.works(route, s, l)
        if route == BOTH:
            self.r_copy(ALONG_X, s, l, k).start()
        elif not on_x:
            self.r_copy(PLANE if route in (OWN, OTHER) else COLUMN, s, l, k).start()
            if on_z:
                self.z_sends(s, l, k)

    def z_sends(self, s, l, k):
        if self.r_small(k):
            for j in range(self.Z - 1):
                self.r_copy(ALONG_Z, s, l, k, j).start()
        else:
            self.on_ends(self.r_copy(PASS_ON, s, l, k).start)
            for j in (0, 2):
                self.unless_end(j, self.r_copy(ALONG_Z, s, l, k, j).start)
            self.on_ends(self.r_copy(ALONG_Z, s, l, k, 1).start)

    def ry(self, s, l, k):
        g, rows, r1, rx, rz, rf = self.r_bufs(l, k)
        c, X, late = self.c, self.X, self.r_late(l, k)
        if self.r_route(l, k) in (OWN, OTHER):
            self.r_copy(PLANE, s, l, k).wait_recv()
            self.add(self.Z * X, lambda i: g.at[i // X, lax.rem(i, X), c, rows],
                     lambda i: self.o.ry.at[i // X, lax.rem(i, X), late])
        else:
            self.r_copy(COLUMN, s, l, k).wait_recv()
            self.add(self.Z, lambda i: g.at[i, 1 - self.x, c, rows], lambda i: self.o.rcol.at[i, late])
        self.r_copy(ALONG_X, s, l, k).start()

    def r2(self, s, l, k):
        g, rows, r1, rx, rz, rf = self.r_bufs(l, k)
        x, c = self.x, self.c
        self.r_copy(ALONG_X, s, l, k).wait_recv()
        self.add(self.Z, lambda i: g.at[i, x, c, rows], lambda i: rx.at[i, rows])
        self.z_sends(s, l, k)

    def r_pass(self, s, l, k):
        g, rows, r1, rx, rz, rf = self.r_bufs(l, k)
        z, x, c = self.z, self.x, self.c

        @self.on_middle
        def _():
            far = (2 - z) * 3
            self.r_copy(PASS_ON, s, l, k).wait_recv()
            g[far, x, c, rows] = g[far, x, c, rows] + rz[z, rows]
            self.r_copy(ALONG_Z, s, l, k, 1).start()

    def r3(self, s, l, k):
        g, rows, r1, rx, rz, rf = self.r_bufs(l, k)
        z, x, c = self.z, self.x, self.c
        if self.r_small(k):
            for j in range(self.Z - 1):
                self.r_copy(ALONG_Z, s, l, k, j).wait_recv()
            rz[z, rows] = g[z, x, c, rows]
            total = rz[0, rows].astype(F32)
            for i in range(1, self.Z):
                total = total + rz[i, rows].astype(F32)
            g[z, x, c, rows] = total
            if s != l:
                self.r_copy(SHARD, s, l, k).start()
            return
        for j in range(self.Z - 1):
            (self.unless_end if j != 1 else self.always)(2 - j, self.r_copy(ALONG_Z, s, l, k, j).wait_recv)
        total = g[z, x, c, rows].astype(F32) + rz[lax.rem(z + 2, self.Z), rows].astype(F32)
        total = total + rz[z + 1 - 2 * lax.rem(z, 2), rows].astype(F32)
        acc = self.o.sum_s.at[0 : total.shape[0]]
        acc[...] = total

        @self.on_middle
        def _():
            acc[...] = acc[...] + rz[self.Z - 1 - z, rows].astype(F32)

        if s == l and self.r_route(l, k) == OWN:
            self.result(k, acc[...])
        else:
            g[z, x, c, rows] = acc[...].astype(g.dtype)
            if s != l:
                self.r_copy(SHARD, s, l, k).start()

    def always(self, j, f):
        f()

    def r4(self, s, l, k):
        g, rows, r1, rx, rz, rf = self.r_bufs(l, k)
        self.r_copy(SHARD, s, l, k).wait_recv()
        total = rf[rows].astype(F32)
        if self.r_route(l, k) in (BOTH, X_OWN, X_OTHER):
            total = g[self.z, self.x, self.c, rows].astype(F32) + total
        self.result(k, total)

    def result(self, k, v):
        o, rp = self.o, self.rp
        if self.r_small(k):
            o.d_small[...] = v
            return
        p0, n = REDUCE[k]
        w = v.shape[1]
        for i in range(n):
            p, t = p0 + i, v[i * rp : (i + 1) * rp]
            if p < 3:
                o.d_wq[0, :, p * w : (p + 1) * w] = t
            elif p == 3:
                o.d_wo[0] = t
            elif p < 8:
                o.d_wi[0, :, (p - 4) * w : (p - 3) * w] = t
            else:
                o.wft[(p - 8) * rp : (p - 7) * rp, :] = t

    def turn(self):
        for m in range(self.o.wft.shape[1] // 128):
            ms = slice(m * 128, m * 128 + 128)
            self.o.d_wf[0, :, ms] = self.o.wft[:, ms].T

    def re(self, s, l):
        for k in range(len(REDUCE) + 1):
            route = self.r_route(l, k)
            on_x, on_z = self.works(route, s, l)
            self.r_copy(TO_CORE, s, l, k).wait_send()
            if on_x:
                self.r_copy(ALONG_X, s, l, k).wait_send()
            else:
                self.r_copy(PLANE if route in (OWN, OTHER) else COLUMN, s, l, k).wait_send()
            if on_z:
                if self.r_small(k):
                    for j in range(self.Z - 1):
                        self.r_copy(ALONG_Z, s, l, k, j).wait_send()
                else:
                    for j in range(self.Z - 1):
                        self.unless_end(j, self.r_copy(ALONG_Z, s, l, k, j).wait_send)
                    self.on_ends(self.r_copy(PASS_ON, s, l, k).wait_send)
                if s != l:
                    self.r_copy(SHARD, s, l, k).wait_send()


def kernel(names, grid, *refs):
    o = types.SimpleNamespace(**dict(zip(names, refs)))
    fused = grid is not None
    W = o.h_s.shape[2]
    FF = o.f_s.shape[1]
    Z, X, C, total = o.wall.shape[1:5]
    rp = total // PARTS
    flag, hb, wall, g1 = o.flag, o.hb, o.wall, o.g1
    q_s, k_s, v_s, p_s, c_s, cl_s, xh1, rst, n1 = o.q_s, o.k_s, o.v_s, o.p_s, o.c_s, o.cl_s, o.xh1, o.rst, o.n1
    f_s, gp, xh2, y_s, h_s, oc = o.f_s, o.gp, o.xh2, o.y_s, o.h_s, o.oc
    gin1, mask_s, g_s, go, gh_s, ds_s, gqkv, xt, cols = o.gin1, o.mask_s, o.g_s, o.go, o.gh_s, o.ds_s, o.gqkv, o.xt, o.cols
    vec, bff, dvec, dbff, sems = o.vec, o.bff, o.dvec, o.dbff, o.sems

    R = h_s.shape[1]
    s = lax.axis_index("section")
    mine = pl.ds(tiled(s * R, R), R)
    tc = o.tc_in[mine].reshape(1, R)
    mask = o.mask_in[mine].reshape(1, R).astype(F32)
    hw = o.hw_in[...].reshape(1, W)
    long = flag[s] == 1
    if fused:
        ex = Exchange(o, grid, rp)
        z, x, c = ex.z, ex.x, ex.c
        ex.greet()
        own, ins = o.own, o.own_sems
        loads = [(o.wq_in.at[0, :, i * W : (i + 1) * W], i * rp, rp) for i in range(3)]
        loads += [(o.wo_in.at[0], 3 * rp, rp)]
        loads += [(o.wi_in.at[0, :, i * W : (i + 1) * W], (4 + i) * rp, rp) for i in range(4)]
        loads += [(o.wf_in.at[0], 8 * rp, 4 * rp)]
        loads = [pltpu.make_async_copy(a, own.at[at : at + n], ins.at[i]) for i, (a, at, n) in enumerate(loads)]
        cin = [pltpu.make_async_copy(o.x_in.at[mine], h_s.at[0], sems.at[0]),
               pltpu.make_async_copy(o.oc_in.at[mine], oc, sems.at[1])]
        for t in loads + cin:
            t.start()
        nv, nb = o.vec_in.shape[2], o.bff_in.shape[1]
        o.own_small[...] = jnp.zeros(o.own_small.shape, F32)
        o.own_small[0:8, 0:nv] = o.vec_in[0].astype(F32)
        o.own_small[8:9, 0:nb] = o.bff_in[...].astype(F32)
        o.wsm[s, z, x, c] = o.own_small[...]
        for t in loads:
            t.wait()
        wall[s, z, x, c] = own[...]
        ex.met()
    else:
        cin = [pltpu.make_async_copy(o.x_in.at[mine], h_s.at[0], sems.at[0]),
               pltpu.make_async_copy(o.oc_in.at[mine], oc, sems.at[1]),
               pltpu.make_async_copy(o.w_in, wall, sems.at[2])]
        for t in cin:
            t.start()
        vec[...] = o.vec_in[...]
        bff[...] = o.bff_in[...]

    if not fused:
        for t in cin:
            t.wait()

    lane = lax.broadcasted_iota(jnp.int32, (W, 128), 1)
    row_run = lax.broadcasted_iota(jnp.int32, (W, 128), 0) // RUN
    flagged = lambda cond: cond.astype(F32).astype(BF16)
    sides = (flagged(lane < 64), flagged(lane >= 64))
    spare = (lane - 64, lane)
    run_lane = tuple(flagged(t == row_run) for t in spare)
    two_lanes = tuple(flagged((t == 0) | (t == 1)) for t in spare)

    valid = mask > 0.0
    key_run = lax.broadcasted_iota(jnp.int32, (8, W), 1) // RUN
    query_run = lax.broadcasted_iota(jnp.int32, (8, W), 0)
    open_key = valid & ((key_run == query_run) | long)
    blocked = jnp.where(open_key, 0.0, -1e9).T
    for t in range(2):
        wide = jnp.zeros((W, 128), F32)
        for r in range(R // RUN):
            wide = jnp.where(spare[t] == r, blocked[:, r : r + 1], wide)
        mask_s[t] = wide.astype(BF16)

    def small_weights(l):
        for i in range(Z * X * C):
            b = o.wsm.at[l, i // (X * C), (i // C) % X, i % C]
            vec[l, :, i * nv : (i + 1) * nv] = b[0:8, 0:nv]
            bff[l, 0:1, i * nb : (i + 1) * nb] = b[8:9, 0:nb]

    def part(l, p, cs=slice(None)):
        a = wall[l, :, :, :, pl.ds(tiled(p * rp, rp), rp), cs]
        return a.reshape(W, a.shape[-1])

    def part_rows(l, p, r0, n):
        if C == 1:
            return wall[l, 0, 0, 0, pl.ds(tiled(p * rp + r0, n), n), :]
        k = n // (X * C * rp)
        return wall[l, pl.ds(r0 // (X * C * rp), k), :, :, pl.ds(tiled(p * rp, rp), rp), :].reshape(n, W)

    def back_w(l, cs):
        a = wall[l, :, :, :, 8 * rp :, cs]
        return a.reshape(FF, a.shape[-1])

    def back_rows(l, j, n):
        if C == 1:
            return wall[l, 0, 0, 0, pl.ds(tiled(8 * rp + j * n, n), n), :]
        return wall[l, j // X, lax.rem(j, X), :, 8 * rp :, :].reshape(n, W)

    def g_ref(l):
        return g1 if l == 1 else wall.at[1]

    def put_part(l, p, cs, val):
        rows = pl.ds(tiled(p * rp, rp), rp)
        g_ref(l)[:, :, :, rows, cs] = val.reshape(Z, X, C, rp, -1).astype(BF16)

    def put_back(l, j, val):
        val = val.astype(BF16)
        for i in range(val.shape[1] // 128):
            for m in range(W // 128):
                block = val[m * 128 : m * 128 + 128, i * 128 : i * 128 + 128]
                ms = slice(m * 128, m * 128 + 128)
                if C == 1:
                    g_ref(l)[0, 0, 0, pl.ds(tiled(8 * rp + (4 * j + i) * 128, 128), 128), ms] = block
                else:
                    g_ref(l)[j, i // C, i % C, 8 * rp :, ms] = block

    def vrow(l, i):
        return vec[l, i : i + 1, :]

    def keep(src, dst, i):
        return pltpu.make_async_copy(src, dst, sems.at[i])

    def qkv(l):
        h = h_s.at[l]
        if fused and l == 0:
            cin[0].wait()

        def step(j, _):
            cs = pl.ds(tiled(j * 256, 256), 256)
            hv = h[...]
            rq = dot(hv, part(l, 0, cs)) + vec[l, 0:1, cs]
            q_s[l, :, cs] = (rq.astype(BF16).astype(F32) * 0.125).astype(BF16)
            k_s[l, :, cs] = dot(hv, part(l, 1, cs)).astype(BF16)
            v_s[l, :, cs] = (dot(hv, part(l, 2, cs)) + vec[l, 1:2, cs]).astype(BF16)
            return 0

        loop(0, 2, step)

    def attend(l, p0, p1):
        def pair(p, _):
            cs = pl.ds(tiled(p * 128, 128), 128)
            k2 = k_s[l, :, cs]
            v2 = v_s[l, :, cs]
            for r in range(0, R, ATTEND_ROWS):
                rs = slice(r, r + ATTEND_ROWS)
                q2 = q_s[l, rs, cs]
                c = []
                for t in range(2):
                    raw = dot_nt(q2 * sides[t][rs] + run_lane[t][rs], k2 * sides[t] + mask_s[t])
                    for b in range(0, ATTEND_ROWS, SOFTMAX_ROWS):
                        a = raw[b : b + SOFTMAX_ROWS]
                        e = jnp.exp(a - jnp.max(a, -1, keepdims=True))
                        e = e * (1.0 / jnp.sum(e, -1, keepdims=True))
                        p_s[2 * p + t, r + b : r + b + SOFTMAX_ROWS, :] = e.astype(BF16)
                    c.append(dot(p_s[2 * p + t, rs, :], v2 * sides[t]))
                c = c[0] + c[1]
                c_s[l, rs, cs] = c.astype(BF16)
                cl_s[l, rs, cs] = (c - c.astype(BF16).astype(F32)).astype(BF16)
            return 0

        lax.fori_loop(p0, p1, pair, 0)
        if l == 0 and p1 == 4:
            keep(p_s, o.keep_p, 3).start()

    def project(l):
        def step(j, _):
            rs = pl.ds(tiled(j * 256, 256), 256)
            y = h_s[l, rs, :].astype(F32) + dot(c_s[l, rs, :], part(l, 3)) + vrow(l, 2)
            xh, r = layer_norm_rows(y)
            xh1[l, rs, :] = xh
            rst[l, rs, 0:1] = r
            n1[l, rs, :] = (xh * vrow(l, 3) + vrow(l, 4)).astype(BF16)
            return 0

        loop(0, 2, step)

    def ff_in(l, j0, j1):
        def step(j, _):
            cs = pl.ds(tiled(j * 256, 256), 256)
            sub = pl.ds(tiled((j % 2) * 256, 256), 256)
            u = dot(n1[l], part(l, 4 + j // 2, sub))
            b = bff[l, 0:1, cs]
            for r in range(0, W, GELU_ROWS):
                f, d = gelu_both(u[r : r + GELU_ROWS] + b)
                f_s[r : r + GELU_ROWS, cs] = f.astype(BF16)
                gp[r : r + GELU_ROWS, cs] = d.astype(BF16)
            return 0

        loop(j0, j1, step)

    def ff_out(l):
        def step(j, _):
            cs = pl.ds(tiled(j * 256, 256), 256)
            y_s[:, cs] = dot(f_s[...], back_w(l, cs))
            return 0

        loop(0, 2, step)
        if l == 0:
            keep(f_s, o.keep_f, 4).start()
            keep(gp, o.keep_g, 5).start()

        def top(j, _):
            rs = pl.ds(tiled(j * RUN, RUN), RUN)
            y = xh1[l, rs, :] * vrow(l, 3) + vrow(l, 4) + y_s[rs, :] + vrow(l, 5)
            xh, r = layer_norm_rows(y)
            xh2[l, rs, :] = xh
            rst[l, rs, 1:2] = r
            h_s[l + 1, rs, :] = (xh * vrow(l, 6) + vrow(l, 7)).astype(BF16)
            return 0

        loop(0, 4, top)

    spilled = ((p_s, o.keep_p, 3), (f_s, o.keep_f, 4), (gp, o.keep_g, 5))

    def restore(i):
        src, dst, at = spilled[i]
        keep(src, dst, at).wait()

    def reload(i):
        src, dst, at = spilled[i]
        keep(dst, src, at).wait()

    act1 = h_s.at[2]

    def head():
        hw16 = jnp.broadcast_to(hw, (16, W))
        zr = dot_nt(hw16, act1[...])[0:1] + hb[0]
        ez = jnp.exp(-jnp.abs(zr))
        terms = jnp.log1p(ez) + jnp.maximum(zr, 0.0)
        sig = jnp.where(zr >= 0.0, 1.0, ez) / (1.0 + ez)
        gz = tc * mask * sig
        o.dhb[...] = jnp.sum(gz, -1, keepdims=True)
        sub8 = lax.broadcasted_iota(jnp.int32, (8, W), 0)
        cols[...] = jnp.where(sub8 == 0, gz, jnp.where(sub8 == 1, mask, 0.0)).T
        if fused:
            o.term[s] = terms
            send_term.start()
        else:
            o.term[...] = terms

    if fused:
        own_rows = mine
        across = ex.dev(s=1 - s)
        put_act = ex.copy(h_s.at[2 - s], o.act_out.at[own_rows], o.os.at[0], o.orr.at[0], across)
        send_term = ex.copy(o.term.at[s], o.term.at[s], o.os.at[1], o.orr.at[1], across)
        own_act = pltpu.make_async_copy(h_s.at[1 + s], o.act_out.at[own_rows], sems.at[0])
        send_g = [ex.copy(g, o.gin_out.at[own_rows], o.os.at[2], o.orr.at[2], across) for g in (oc, gin1)]
        own_g = [pltpu.make_async_copy(g, o.gin_out.at[own_rows], sems.at[1]) for g in (oc, gin1)]

    def send_act(i):
        pl.when(s != i)(put_act.start)
        pl.when(s == i)(own_act.start)

    def send_grad(i):
        pl.when(s != i)(send_g[i].start)
        pl.when(s == i)(own_g[i].start)

    def top_back(l):
        if fused and l == 1:
            cin[1].wait()
        zero = jnp.zeros((8, W), F32)

        def step(j, carry):
            sg, ss, sb, sh = carry
            rs = pl.ds(tiled(j * RUN, RUN), RUN)
            if l == 1:
                gzc = cols[rs, 0:1]
                g = oc[rs, :].astype(F32) * cols[rs, 1:2] + gzc * hw.astype(F32)
                sh = sh + rows8(gzc * act1[rs, :].astype(F32))
            else:
                g = gin1[rs, :].astype(F32)
            xh = xh2[l, rs, :]
            sg = sg + rows8(g * xh)
            ss = ss + rows8(g)
            gy = layer_norm_back(g, vrow(l, 6), xh, rst[l, rs, 1:2])
            g_s[rs, :] = gy
            gl = gy.astype(BF16)
            go[rs, :] = gl
            sb = sb + rows8(gl.astype(F32))
            return sg, ss, sb, sh

        sg, ss, sb, sh = lax.fori_loop(0, 4, step, (zero,) * 4)
        dvec[l, 6:7, :] = jnp.sum(sg, 0, keepdims=True)
        dvec[l, 7:8, :] = jnp.sum(ss, 0, keepdims=True)
        dvec[l, 5:6, :] = jnp.sum(sb, 0, keepdims=True)
        if l == 1:
            o.dhw[...] = jnp.sum(sh, 0, keepdims=True)

    def ff_out_grad(l):
        xt[...] = go[...].T

        def step(j, _):
            cs = pl.ds(tiled(j * 512, 512), 512)
            put_back(l, j, dot(xt[...], f_s[:, cs]))
            return 0

        loop(0, FF // 512, step)

    def ff_back(l, j0, j1):
        if j0 == 0:
            xt[...] = n1[l].T

        def step(j, _):
            cs = pl.ds(tiled(j * 256, 256), 256)
            gf = dot_nt(go[...], back_rows(l, j, 256))
            total = jnp.zeros((8, 256), F32)
            for r in range(0, W, GELU_ROWS):
                gul = (gf[r : r + GELU_ROWS] * gp[r : r + GELU_ROWS, cs].astype(F32)).astype(BF16)
                f_s[r : r + GELU_ROWS, cs] = gul
                total = total + rows8(gul.astype(F32))
            dbff[l, 0:1, cs] = jnp.sum(total, 0, keepdims=True)
            return 0

        loop(j0, j1, step)

        def grad(j, _):
            cs = pl.ds(tiled(j * 512, 512), 512)
            put_part(l, 4 + j, slice(None), dot(xt[...], f_s[:, cs]))
            return 0

        loop(j0 // 2, j1 // 2, grad)

    def mid(l):
        def step(j, _):
            cs = pl.ds(tiled(j * 256, 256), 256)
            acc = None
            for p in range(4):
                d = dot_nt(f_s[:, p * W : (p + 1) * W], part_rows(l, 4 + p, j * 256, 256))
                acc = d if acc is None else acc + d
            y_s[:, cs] = acc
            return 0

        loop(0, 2, step)
        if l == 1:
            keep(o.keep_f, f_s, 4).start()
            keep(o.keep_g, gp, 5).start()

        zero = jnp.zeros((8, W), F32)

        def back(j, carry):
            sg, ss, sb = carry
            rs = pl.ds(tiled(j * RUN, RUN), RUN)
            g = g_s[rs, :] + y_s[rs, :]
            xh = xh1[l, rs, :]
            sg = sg + rows8(g * xh)
            ss = ss + rows8(g)
            gy = layer_norm_back(g, vrow(l, 3), xh, rst[l, rs, 0:1])
            g_s[rs, :] = gy
            gl = gy.astype(BF16)
            go[rs, :] = gl
            sb = sb + rows8(gl.astype(F32))
            return sg, ss, sb

        sg, ss, sb = lax.fori_loop(0, 4, back, (zero,) * 3)
        dvec[l, 3:4, :] = jnp.sum(sg, 0, keepdims=True)
        dvec[l, 4:5, :] = jnp.sum(ss, 0, keepdims=True)
        dvec[l, 2:3, :] = jnp.sum(sb, 0, keepdims=True)

    def project_back(l):
        put_part(l, 3, slice(None), dot_tn(c_s[l], go[...]))
        gc = dot_nt(go[...], part(l, 3))
        for i in range(0, W, 128):
            gl = gc[:, i : i + 128].astype(BF16)
            go[:, i : i + 128] = gl
            w = gl.astype(F32) * (c_s[l, :, i : i + 128].astype(F32) + cl_s[l, :, i : i + 128].astype(F32))
            low = lane < 64
            offs = (jnp.sum(jnp.where(low, w, 0.0), -1, keepdims=True), jnp.sum(jnp.where(low, 0.0, w), -1, keepdims=True))
            for t in range(2):
                hi = offs[t].astype(BF16).astype(F32)
                off = jnp.where(spare[t] == 0, -hi, jnp.where(spare[t] == 1, hi - offs[t], 0.0))
                gh_s[t, :, i : i + 128] = gl * sides[t] + off.astype(BF16)
        xt[...] = go[...].T

    def attend_back(l, p0, p1):
        def pair(p, _):
            c0 = tiled(p * 128, 128)
            cs = pl.ds(c0, 128)
            k2 = k_s[l, :, cs]
            v2 = v_s[l, :, cs]
            qt = q_s[l, :, cs].T
            gct = xt[cs, :]
            dq = [None] * (R // ATTEND_ROWS)
            dvt, dkt = [], []
            for t in range(2):
                for i in range(len(dq)):
                    r = i * ATTEND_ROWS
                    rs = slice(r, r + ATTEND_ROWS)
                    w = dot_nt(gh_s[t, rs, cs], v2 * sides[t] + two_lanes[t])
                    for b in range(0, ATTEND_ROWS, SOFTMAX_ROWS):
                        bs = slice(r + b, r + b + SOFTMAX_ROWS)
                        ds_s[t, bs, :] = (p_s[2 * p + t, bs, :].astype(F32) * w[b : b + SOFTMAX_ROWS]).astype(BF16)
                    dd = dot(ds_s[t, rs, :], k2 * sides[t])
                    dq[i] = dd if dq[i] is None else dq[i] + dd
                hs = slice(64 * t, 64 * t + 64)
                dvt.append(dot(gct[hs], p_s[2 * p + t]))
                dkt.append(dot(qt[hs], ds_s[t]))
            dql = (jnp.concatenate(dq, 0) * 0.125).astype(BF16)
            dvl = jnp.concatenate(dvt, 0).T.astype(BF16)
            dkl = jnp.concatenate(dkt, 0).T.astype(BF16)
            gqkv[:, cs] = dql
            gqkv[:, pl.ds(tiled(c0 + W, 128), 128)] = dkl
            gqkv[:, pl.ds(tiled(c0 + 2 * W, 128), 128)] = dvl
            dvec[l, 0:1, cs] = jnp.sum(rows8(dql.astype(F32)), 0, keepdims=True)
            dvec[l, 1:2, cs] = jnp.sum(rows8(dvl.astype(F32)), 0, keepdims=True)
            return 0

        lax.fori_loop(p0, p1, pair, 0)
        if p1 == 4:
            if l == 1:
                keep(o.keep_p, p_s, 3).start()
            xt[...] = h_s[l].T

    def qkv_grad(l):
        for p in range(3):
            put_part(l, p, slice(None), dot(xt[...], gqkv[:, p * W : (p + 1) * W]))

    def qkv_back(l):
        gdst = gin1 if l == 1 else oc

        def step(j, _):
            cs = pl.ds(tiled(j * 256, 256), 256)
            acc = g_s[:, cs]
            for p in range(3):
                acc = acc + dot_nt(gqkv[:, p * W : (p + 1) * W], part_rows(l, p, j * 256, 256))
            gdst[:, cs] = acc.astype(BF16)
            return 0

        loop(0, 2, step)

    def small_grads(l):
        for i in range(Z * X * C):
            b = o.gsm.at[l, i // (X * C), (i // C) % X, i % C]
            b[...] = jnp.zeros(b.shape, F32)
            b[0:8, 0:nv] = dvec[l, :, i * nv : (i + 1) * nv]
            b[8:9, 0:nb] = dbff[l, 0:1, i * nb : (i + 1) * nb]
            for t in range(W // 128):
                b[9 + t : 10 + t, :] = o.dhw[0:1, t * 128 : (t + 1) * 128]
            b[9 + W // 128 : 10 + W // 128, 0:1] = o.dhb[...]

    steps = {
        QKV: qkv, ATTEND: attend, PROJECT: project, FF_IN: ff_in, FF_OUT: ff_out, RESTORE: restore, HEAD: head,
        TOP_BACK: top_back, FF_OUT_GRAD: ff_out_grad, FF_BACK: ff_back, MID: mid, PROJECT_BACK: project_back,
        ATTEND_BACK: attend_back, QKV_GRAD: qkv_grad, QKV_BACK: qkv_back, RELOAD: reload,
    }
    def exchange(*lists):
        for sec, todo in enumerate(lists):
            if todo:
                @pl.when(s == sec)
                def _():
                    for what, *which in todo:
                        calls[what](sec, *which)

    if fused:
        calls = {GY: ex.gy, GZ: ex.gz, GX: ex.gx, GC: ex.gc, GD: ex.gd, GE: ex.ge, GF: ex.gf, RP: ex.r_pass,
                 RC: ex.rc, R1: ex.r1, RY: ex.ry, R2: ex.r2, R3: ex.r3, R4: ex.r4, RE: ex.re}
        steps |= {EXCHANGE: exchange, SMALL_WEIGHTS: small_weights, SMALL_GRADS: small_grads, SEND_ACT: send_act,
                  SEND_GRAD: send_grad}
    for name, *args in FUSED_STEPS if fused else PLAIN_STEPS:
        steps[name](*args)

    if fused:
        ex.turn()
        put_act.wait()
        send_term.wait()
        own_act.wait()
        send_g[0].wait()
        own_g[0].wait()
    else:
        outs = [pltpu.make_async_copy(g1, o.g_out.at[1], sems.at[0]),
                pltpu.make_async_copy(wall.at[1], o.g_out.at[0], sems.at[1]),
                pltpu.make_async_copy(h_s.at[pl.ds(1, 2)], o.act_out, sems.at[2]),
                pltpu.make_async_copy(oc, o.gin_out.at[0], sems.at[3]),
                pltpu.make_async_copy(gin1, o.gin_out.at[1], sems.at[4])]
        for t in outs:
            t.start()
        for t in outs:
            t.wait()


def make_call(rows, width, inner, n_vec, n_bias, grid, gather=None):
    f32 = lambda *t: jax.ShapeDtypeStruct(t, F32)
    b16 = lambda *t: jax.ShapeDtypeStruct(t, BF16)
    v = lambda dt, *t: pltpu.VMEM(t, dt)
    Z, X, C = grid or (1, 1, 1)
    rp = width // (Z * X * C)
    total = PARTS * rp
    vm = pl.BlockSpec(memory_space=pltpu.VMEM)
    sm = pl.BlockSpec(memory_space=pltpu.SMEM)
    hbm = pl.BlockSpec(memory_space=pl.ANY)
    ins = dict(flag=sm, hb=sm, x_in=hbm, oc_in=hbm, tc_in=vm, mask_in=vm, hw_in=vm)
    if grid:
        ins |= dict(wq_in=hbm, wo_in=hbm, wi_in=hbm, wf_in=hbm, vec_in=vm, bff_in=vm)
        outs = dict(
            act_out=(b16(2 * rows, width), hbm), gin_out=(b16(2 * rows, width), hbm),
            term=(f32(2, 1, rows), vm),
            d_wq=(f32(1, rp, 3 * width), vm), d_wo=(f32(1, rp, width), vm), d_wi=(f32(1, rp, inner), vm),
            d_wf=(f32(1, 4 * rp, width), vm), d_small=(f32(16, 128), vm),
        )
    else:
        ins |= dict(w_in=hbm, vec_in=vm, bff_in=vm)
        outs = dict(
            act_out=(b16(2, rows, width), hbm), gin_out=(b16(2, rows, width), hbm), term=(f32(1, rows), vm),
            g_out=(b16(2, 1, 1, 1, total, width), hbm), dvec=(f32(2, 8, width), vm),
            dbff=(f32(2, 1, inner), vm), dhw=(f32(1, width), vm), dhb=(f32(1, 1), vm),
        )
    outs |= dict(keep_p=(b16(HEADS, rows, rows), hbm), keep_f=(b16(rows, inner), hbm),
             keep_g=(b16(rows, inner), hbm))
    scratch = dict(
        wall=v(BF16, 2, Z, X, C, total, width), g1=v(BF16, Z, X, C, total, width),
        q_s=v(BF16, 2, rows, width), k_s=v(BF16, 2, rows, width), v_s=v(BF16, 2, rows, width),
        p_s=v(BF16, HEADS, rows, rows), c_s=v(BF16, 2, rows, width), cl_s=v(BF16, 2, rows, width),
        xh1=v(F32, 2, rows, width), rst=v(F32, 2, rows, 2), n1=v(BF16, 2, rows, width),
        f_s=v(BF16, rows, inner), gp=v(BF16, rows, inner),
        xh2=v(F32, 2, rows, width), y_s=v(F32, rows, width),
        h_s=v(BF16, 3, rows, width), oc=v(BF16, rows, width), gin1=v(BF16, rows, width),
        mask_s=v(BF16, 2, rows, 128), g_s=v(F32, rows, width), go=v(BF16, rows, width),
        gh_s=v(BF16, 2, rows, width), ds_s=v(BF16, 2, rows, rows), gqkv=v(BF16, rows, 3 * width), xt=v(BF16, width, rows),
        cols=v(F32, rows, 8), vec=v(F32, 2, 8, width), bff=v(F32, 2, 1, inner),
        sems=pltpu.SemaphoreType.DMA((6,)),
    )
    if grid:
        late, columns = (late_parts(kind) * rp for kind in ((OWN, OTHER), (X_OWN, X_OTHER)))
        kg, kr = len(GATHER) + 1, len(REDUCE) + 1
        dma = pltpu.SemaphoreType.DMA
        scratch |= dict(
            dvec=v(F32, 2, 8, width), dbff=v(F32, 2, 1, inner), dhw=v(F32, 1, width), dhb=v(F32, 1, 1),
            wsm=v(F32, 2, Z, X, C, 16, 128), gsm=v(F32, 2, Z, X, C, 16, 128),
            r1s=v(F32, 2, Z, X, 16, 128), rxs=v(F32, 2, Z, 16, 128), rzs=v(F32, 2, Z, 16, 128),
            rys=v(F32, 16, 128),
            r1=v(BF16, Z, X, total, width), ry=v(BF16, Z, X, late, width), rcol=v(BF16, Z, columns, width),
            rx=v(BF16, 2, Z, total, width), rz=v(BF16, 2, Z, total, width), rf=v(BF16, total, width),
            wft=v(F32, 4 * rp, width), own_sems=pltpu.SemaphoreType.DMA((9,)), own=v(BF16, total, width), own_small=v(F32, 16, 128),
            gs=dma((2, kg, 8)), gr=dma((2, kg, 8)), ss=dma((2, kr, 8)), sr=dma((2, kr, 8)), sum_s=v(F32, max(n for _, n in REDUCE) * rp, width),
            os=dma((3,)), orr=dma((3,)), credit=pltpu.SemaphoreType.REGULAR((kr,)),
        )
    names = list(ins) + list(outs) + list(scratch)
    params = dict(vmem_limit_bytes=VMEM_BYTES)
    if grid:
        params |= dict(collective_id=0, has_side_effects=True)
    call = pl.pallas_call(
        functools.partial(kernel, names, grid),
        out_shape=tuple(t[0] for t in outs.values()),
        in_specs=list(ins.values()),
        out_specs=tuple(t[1] for t in outs.values()),
        scratch_shapes=list(scratch.values()),
        compiler_params=pltpu.CompilerParams(**params),
    )
    return call, list(outs)


def hand_over(act, gin, term, wq, wo, wi, wf, small, act_o, gin_o, term_o, wq_o, wo_o, wi_o, wf_o, vec_o, bff_o, hw_o,
              hb_o, sems):
    moves = [pltpu.make_async_copy(a, b, sems.at[i]) for i, (a, b) in enumerate(
        ((act, act_o.at[0]), (gin, gin_o.at[0]), (wq, wq_o), (wo, wo_o), (wi, wi_o), (wf, wf_o)))]
    for m in moves:
        m.start()
    rows, heads = term.shape[2], hw_o.shape[0] // 128
    for i in range(term.shape[0]):
        term_o[i * rows : (i + 1) * rows] = term[i, 0].astype(BF16)
    vec_o[0] = small[0:8, 0 : vec_o.shape[2]]
    bff_o[...] = small[8:9, 0 : bff_o.shape[1]]
    for i in range(heads):
        hw_o[i * 128 : (i + 1) * 128] = small[9 + i, :]
    hb_o[...] = small[9 + heads, 0:1]
    for m in moves:
        m.wait()


def fused_local(grid, tokens_in, out_cot, term_cot, long_flag, token_mask, w_qkv, w_out, w_ff_in, w_ff_out, vectors,
                ff_bias, head_weight, head_bias):
    section = lax.axis_index("section")
    width = tokens_in.shape[1]
    micro = long_flag.shape[0]
    rows = tokens_in.shape[0] // micro
    call, names = make_call(rows, width, w_ff_in.shape[2], vectors.shape[2], ff_bias.shape[1], grid)
    res = types.SimpleNamespace(**dict(zip(names, call(long_flag, head_bias, tokens_in, out_cot, term_cot, token_mask,
                                                      head_weight, w_qkv, w_out, w_ff_in, w_ff_out, vectors, ff_bias))))
    vm, hbm = pl.BlockSpec(memory_space=pltpu.VMEM), pl.BlockSpec(memory_space=pl.ANY)
    f32 = lambda *t: jax.ShapeDtypeStruct(t, F32)
    b16 = lambda *t: jax.ShapeDtypeStruct(t, BF16)
    both = b16(1, micro * rows, width)
    acts, gins, *rest = pl.pallas_call(
        hand_over,
        out_shape=(both, both, b16(micro * rows), f32(*w_qkv.shape), f32(*w_out.shape), f32(*w_ff_in.shape),
                   f32(*w_ff_out.shape), f32(*vectors.shape), f32(*ff_bias.shape), f32(width), f32(1)),
        in_specs=[hbm, hbm, vm, hbm, hbm, hbm, hbm, vm],
        out_specs=(vm,) * 11,
        scratch_shapes=[pltpu.SemaphoreType.DMA((6,))],
    )(res.act_out, res.gin_out, res.term, res.d_wq, res.d_wo, res.d_wi, res.d_wf, res.d_small)
    return (acts, rest[0], gins, *rest[1:])


def plain_local(tokens_in, out_cot, term_cot, long_flag, token_mask, w_qkv, w_out, w_ff_in, w_ff_out, vectors, ff_bias,
                head_weight, head_bias):
    section = lax.axis_index("section")
    width = tokens_in.shape[1]
    micro = long_flag.shape[0]
    rows = tokens_in.shape[0] // micro
    inner = w_ff_in.shape[2]
    everyone = lambda a, ax: lax.all_gather(lax.all_gather(a, "dp", axis=ax, tiled=True), "section", axis=0, tiled=True)
    wq, wo, wi, wf = (everyone(a, 1) for a in (w_qkv, w_out, w_ff_in, w_ff_out))
    vec = everyone(vectors, 2).astype(F32)
    bff = everyone(ff_bias, 1).astype(F32)[:, None]
    cut = lambda a: a.reshape(2, width, -1, width).transpose(0, 2, 1, 3).reshape(2, -1, width)
    wall = jnp.concatenate([cut(wq), wo, cut(wi), wf], 1)[:, None, None, None]
    call, names = make_call(rows, width, inner, width, inner, None)
    res = types.SimpleNamespace(**dict(zip(names, call(long_flag, head_bias, tokens_in, out_cot, term_cot, token_mask,
                                                      head_weight, wall, vec, bff))))
    swap = lambda a: lax.all_gather(a, "section", axis=1, tiled=True)[section][None]
    terms = lax.all_gather(res.term[0], "section", axis=0, tiled=True).astype(BF16)

    def scatter(a, ax):
        a = lax.psum_scatter(a.astype(F32), "section", scatter_dimension=0, tiled=True)
        return lax.psum_scatter(a, "dp", scatter_dimension=ax, tiled=True)

    g = res.g_out[:, 0, 0, 0]
    glue = lambda a, n: a.reshape(2, n, width, width).transpose(0, 2, 1, 3).reshape(2, width, n * width)
    turned = lambda a: a.reshape(2, -1, 128, width // 128, 128).transpose(0, 1, 4, 3, 2).reshape(2, -1, width)
    dhw, dhb = lax.psum((res.dhw[0], res.dhb[0]), ("section", "dp"))
    return (
        swap(res.act_out), terms, swap(res.gin_out),
        scatter(glue(g[:, : 3 * width], 3), 1), scatter(g[:, 3 * width : 4 * width], 1),
        scatter(glue(g[:, 4 * width : 8 * width], 4), 1), scatter(turned(g[:, 8 * width :]), 1),
        scatter(res.dvec, 2), scatter(res.dbff[:, 0], 1), dhw, dhb,
    )


def solution(mesh):
    dp = mesh.shape["dp"]
    if dp == 16:
        local = functools.partial(fused_local, (4, 2, 2))
    else:
        local = plain_local
    shard = P("section", "dp", None)
    in_specs = (P("dp", None), P("dp", None), P("dp"), P("dp"), P("dp"), shard, shard, shard, shard,
                P("section", None, "dp"), P("section", "dp"), P(), P())
    out_specs = (shard, P("dp"), shard, shard, shard, shard, shard, P("section", None, "dp"), P("section", "dp"),
                 P(), P())
    return jax.shard_map(local, mesh=mesh, in_specs=in_specs, out_specs=out_specs, check_vma=False)
```

```python
import functools
import types

import jax
import jax.numpy as jnp
from jax import lax
from jax.experimental import pallas as pl
from jax.experimental.pallas import tpu as pltpu
from jax.sharding import PartitionSpec as P

RUN = 128
HEADS = 8
EPS = 1e-12
F32, BF16 = jnp.float32, jnp.bfloat16
VMEM_BYTES = 64 * 2**20
GELU_ROWS = 64
ATTEND_ROWS = 256
SOFTMAX_ROWS = 64


def dot(a, b):
    return lax.dot_general(a, b, (((1,), (0,)), ((), ())), preferred_element_type=F32)


def dot_nt(a, b):
    return lax.dot_general(a, b, (((1,), (1,)), ((), ())), preferred_element_type=F32)


def dot_tn(a, b):
    return lax.dot_general(a, b, (((0,), (0,)), ((), ())), preferred_element_type=F32)


def rows8(v):
    return jnp.sum(v.reshape(-1, 8, v.shape[1]), axis=0)


def tiled(i, n):
    return i if isinstance(i, int) else pl.multiple_of(i, n)


def loop(start, stop, step):
    for j in range(start, stop):
        step(j, 0)


def gelu_both(u):
    w = jnp.abs(u)
    e = jnp.exp2(u * u * -0.7213475204444817)
    d = w * (0.3275911 * 0.7071067811865476) + 1.0
    t = pl.reciprocal(d, approx=True)
    t = t * (2.0 - d * t)
    q = t * 0.5307027145 - 0.7265760135
    q = q * t + 0.7107068705
    q = q * t - 0.142248368
    q = q * t + 0.127414796
    q = q * t * e
    n = q - w * (e * 0.3989422804014327)
    return jnp.maximum(u, 0.0) - w * q, jnp.where(u >= 0.0, 1.0 - n, n)


def layer_norm_rows(y):
    c = y - jnp.mean(y, -1, keepdims=True)
    r = lax.rsqrt(jnp.mean(c * c, -1, keepdims=True) + EPS)
    return c * r, r


def layer_norm_back(g, gain, xh, r):
    gx = g * gain
    a = jnp.mean(gx, -1, keepdims=True)
    b = jnp.mean(gx * xh, -1, keepdims=True)
    return (gx - a - xh * b) * r


MESH = pl.DeviceIdType.MESH
(QKV, ATTEND, PROJECT, FF_IN, FF_OUT, RESTORE, HEAD, TOP_BACK, FF_OUT_GRAD, FF_BACK, MID, PROJECT_BACK, ATTEND_BACK,
 QKV_GRAD, QKV_BACK, RELOAD, EXCHANGE, SMALL_WEIGHTS, SMALL_GRADS, SEND_ACT, SEND_GRAD) = range(21)
GY, GZ, GF, GX, GC, GD, GE, RC, R1, RY, R2, RP, R3, R4, RE = range(15)
BOTH, OWN, OTHER, X_OWN, X_OTHER = range(5)
ALONG_Z, ALONG_X, SHARD, PLANE, COLUMN, PASS_ON, TO_CORE = range(7)
PARTS = 12
GATHER = ((0, 1), (1, 1), (2, 1), (3, 1), (4, 1), (5, 1), (6, 1), (7, 1), (8, 1), (9, 1), (10, 1), (11, 1))
GATHER_ROUTE = ((OWN, OWN, X_OTHER, BOTH, X_OTHER, BOTH, X_OWN, X_OTHER, OWN, X_OTHER, X_OWN, OTHER), (OWN, X_OTHER, BOTH, X_OTHER, X_OWN, OWN, OTHER, BOTH, OTHER, BOTH, OWN, BOTH))
REDUCE = ((0, 1), (1, 1), (2, 1), (3, 1), (4, 2), (6, 2), (8, 2), (10, 2))
REDUCE_ROUTE = ((OWN, X_OTHER, X_OTHER, BOTH, X_OWN, X_OWN, X_OTHER, BOTH), (X_OTHER, OTHER, X_OWN, BOTH, BOTH, X_OTHER, X_OWN, BOTH))


def late_place(l, k):
    takes = lambda a, b: a if REDUCE_ROUTE[a][b] in (OWN, X_OWN) else 1 - a
    kind = (OWN, OTHER) if REDUCE_ROUTE[l][k] in (OWN, OTHER) else (X_OWN, X_OTHER)
    at = 0
    for a in range(2):
        for b, (_, n) in enumerate(REDUCE):
            if (a, b) == (l, k):
                return at, n
            if REDUCE_ROUTE[a][b] in kind and takes(a, b) == takes(l, k):
                at += n
    return at, 0


def late_parts(kind):
    ends = [sum(late_place(l, k)) for l in range(2) for k in range(len(REDUCE)) if REDUCE_ROUTE[l][k] in kind]
    return max(ends, default=1)


def layer_steps(l):
    return (
        ((RESTORE, 0),) if l else ()) + (
        (QKV, l), (ATTEND, l, 0, 4), (PROJECT, l)) + (
        ((RESTORE, 1), (RESTORE, 2)) if l else ()) + (
        (FF_IN, l, 0, 8), (FF_OUT, l))


def layer_back_steps(l):
    return (
        () if l else ((RELOAD, 0), (RELOAD, 1), (RELOAD, 2))) + (
        (TOP_BACK, l), (FF_OUT_GRAD, l), (FF_BACK, l, 0, 8), (MID, l), (PROJECT_BACK, l),
        (ATTEND_BACK, l, 0, 4), (QKV_BACK, l), (QKV_GRAD, l))


PLAIN_STEPS = layer_steps(0) + layer_steps(1) + ((HEAD,),) + layer_back_steps(1) + layer_back_steps(0)


FUSED_STEPS = (
    (EXCHANGE, (
        (GY, 0, 12), (GY, 0, 2), (GY, 0, 10), (GY, 0, 3), (GZ, 0, 12), (GY, 0, 6), (GZ, 0, 0), (GY, 0, 11),
        (GZ, 0, 1), (GY, 0, 5), (GY, 0, 4), (GY, 0, 7), (GZ, 1, 12), (GZ, 0, 2), (GY, 0, 9), (GF, 0, 12),
        (GZ, 0, 10), (GF, 0, 0), (GX, 0, 12), (GZ, 0, 3), (GF, 0, 1), (GF, 1, 12), (GX, 0, 0), (GZ, 0, 6),
        (GC, 0, 12), (GF, 0, 2), (GX, 0, 1), (GX, 1, 12), (GZ, 1, 1), (GD, 0, 12),
    ), (
        (GY, 1, 12), (GY, 1, 4), (GY, 1, 6), (GY, 1, 2), (GZ, 1, 12), (GY, 1, 11), (GZ, 1, 4), (GY, 1, 8),
        (GZ, 1, 0), (GY, 1, 1), (GY, 1, 7), (GY, 1, 9), (GZ, 0, 12), (GZ, 0, 2), (GY, 1, 3), (GF, 1, 12), (GZ, 0, 6),
        (GF, 1, 4), (GX, 1, 12), (GZ, 0, 4), (GF, 1, 0), (GF, 0, 12), (GX, 1, 4), (GZ, 0, 7), (GC, 1, 12),
        (GF, 0, 2), (GX, 1, 0), (GX, 0, 12), (GZ, 0, 11), (GD, 1, 12), (GF, 0, 6), (GZ, 0, 9), (GX, 0, 2),
        (GF, 0, 4), (GC, 1, 4), (GZ, 0, 5), (GX, 0, 6), (GF, 0, 7), (GD, 1, 4), (GZ, 0, 3), (GC, 1, 0), (GX, 0, 4),
        (GC, 0, 12), (GF, 0, 11), (GD, 1, 0), (GZ, 1, 5), (GD, 0, 12),
    )),
    (SMALL_WEIGHTS, 0),
    (EXCHANGE, (
        (GF, 0, 10), (GZ, 0, 8), (GX, 0, 2), (GF, 0, 3), (GC, 0, 0), (GZ, 1, 3), (GX, 0, 10), (GF, 0, 6), (GD, 0, 0),
        (GZ, 0, 5), (GC, 0, 1), (GX, 0, 3), (GC, 1, 12), (GF, 1, 1), (GD, 0, 1), (GZ, 0, 4), (GD, 1, 12), (GX, 0, 6),
        (GF, 0, 8), (GC, 0, 10), (GZ, 1, 6), (GX, 1, 1), (GF, 1, 3), (GD, 0, 10), (GZ, 1, 2), (GX, 0, 8), (GC, 0, 3),
        (GF, 0, 5), (GZ, 1, 8), (GD, 0, 3), (GC, 1, 0), (GX, 1, 3), (GF, 0, 4), (GC, 0, 6), (GD, 1, 0), (GZ, 0, 7),
        (GX, 0, 5), (GD, 0, 6), (GC, 0, 2), (GF, 1, 6), (GC, 1, 1), (GZ, 0, 9), (GX, 0, 4), (GD, 0, 2),
    ), (
        (GX, 0, 7), (GF, 0, 9), (GC, 0, 2), (GZ, 1, 2), (GX, 0, 11), (GF, 0, 5), (GD, 0, 2), (GC, 0, 0), (GZ, 1, 10),
        (GC, 0, 4), (GX, 0, 9), (GF, 0, 3), (GD, 0, 0), (GD, 0, 4), (GZ, 1, 11), (GX, 0, 5), (GC, 0, 7), (GF, 1, 5),
        (GZ, 0, 10), (GD, 0, 7), (GX, 0, 3), (GC, 0, 1), (GF, 1, 2), (GC, 0, 11), (GZ, 1, 1), (GD, 0, 1),
    )),
    (QKV, 0),
    (EXCHANGE, (
        (GF, 1, 2), (GD, 1, 1), (GC, 0, 4),
    ), (
        (GX, 1, 5), (GF, 1, 10), (GD, 0, 11),
    )),
    (ATTEND, 0, 0, 1),
    (EXCHANGE, (
        (GX, 1, 6), (GF, 1, 8), (GC, 0, 8), (GZ, 1, 7), (GD, 0, 4),
    ), (
        (GX, 1, 2), (GC, 0, 9), (GF, 1, 11), (GZ, 1, 7),
    )),
    (ATTEND, 0, 1, 2),
    (EXCHANGE, (
        (GZ, 1, 11), (GD, 0, 8),
    ), (
        (GC, 0, 6), (GZ, 1, 9), (GC, 0, 5), (GD, 0, 9),
    )),
    (ATTEND, 0, 2, 3),
    (EXCHANGE, (
        (GX, 1, 2), (GF, 0, 7), (GC, 1, 3), (GZ, 1, 9), (GX, 1, 8),
    ), (
        (GX, 1, 10), (GF, 0, 10), (GZ, 1, 3), (GD, 0, 6), (GX, 1, 11), (GD, 0, 5),
    )),
    (ATTEND, 0, 3, 4),
    (EXCHANGE, (
        (GF, 0, 9), (GC, 0, 5), (GZ, 1, 4), (GD, 1, 3),
    ), (
        (GF, 1, 1), (GC, 0, 3), (GF, 1, 7), (GD, 0, 3),
    )),
    (PROJECT, 0),
    (EXCHANGE, (
    ), (
        (GX, 0, 10), (GC, 1, 5), (GC, 0, 10),
    )),
    (FF_IN, 0, 0, 2),
    (EXCHANGE, (
        (GX, 0, 7), (GF, 1, 7), (GC, 0, 11), (GC, 0, 7), (GD, 0, 5),
    ), (
        (GX, 1, 1), (GF, 1, 9), (GC, 1, 1),
    )),
    (FF_IN, 0, 2, 4),
    (EXCHANGE, (
        (GF, 1, 11), (GC, 1, 6), (GX, 0, 9),
    ), (
        (GX, 1, 7), (GC, 1, 2), (GC, 0, 8), (GF, 1, 3), (GD, 1, 5), (GD, 0, 10),
    )),
    (FF_IN, 0, 4, 6),
    (EXCHANGE, (
        (GC, 0, 9), (GD, 0, 11), (GD, 0, 7),
    ), (
        (GD, 1, 1),
    )),
    (FF_IN, 0, 6, 8),
    (EXCHANGE, (
        (GX, 1, 7), (GF, 1, 9), (GC, 1, 2), (GD, 1, 6), (GD, 0, 9),
    ), (
        (GX, 1, 9), (GD, 1, 2), (GD, 0, 8),
    )),
    (FF_OUT, 0),
    (EXCHANGE, (
        (GX, 1, 11), (GF, 1, 4), (GD, 1, 2),
    ), (
        (GX, 1, 3), (GC, 1, 10), (GC, 1, 3),
    )),
    (SEND_ACT, 0),
    (EXCHANGE, (
        (GC, 1, 8),
    ), (
    )),
    (SMALL_WEIGHTS, 1),
    (RESTORE, 0),
    (QKV, 1),
    (EXCHANGE, (
    ), (
        (GC, 1, 11),
    )),
    (ATTEND, 1, 0, 1),
    (EXCHANGE, (
        (GX, 1, 9), (GC, 1, 5), (GD, 1, 8),
    ), (
        (GD, 1, 10), (GD, 1, 3),
    )),
    (ATTEND, 1, 1, 2),
    (EXCHANGE, (
        (GX, 1, 4), (GC, 1, 7), (GC, 1, 4),
    ), (
        (GC, 1, 6), (GC, 1, 7), (GD, 1, 11),
    )),
    (ATTEND, 1, 2, 3),
    (EXCHANGE, (
        (GD, 1, 5),
    ), (
    )),
    (ATTEND, 1, 3, 4),
    (EXCHANGE, (
        (GC, 1, 11), (GD, 1, 7), (GD, 1, 4),
    ), (
        (GC, 1, 9), (GD, 1, 6), (GD, 1, 7),
    )),
    (PROJECT, 1),
    (RESTORE, 1),
    (RESTORE, 2),
    (FF_IN, 1, 0, 2),
    (EXCHANGE, (
        (GD, 1, 11),
    ), (
        (GD, 1, 9),
    )),
    (FF_IN, 1, 2, 4),
    (EXCHANGE, (
        (GC, 1, 10), (GC, 1, 9),
    ), (
        (GC, 1, 8),
    )),
    (FF_IN, 1, 4, 6),
    (FF_IN, 1, 6, 8),
    (EXCHANGE, (
        (GD, 1, 10), (GD, 1, 9),
    ), (
        (GD, 1, 8),
    )),
    (FF_OUT, 1),
    (HEAD,),
    (SEND_ACT, 1),
    (TOP_BACK, 1),
    (FF_OUT_GRAD, 1),
    (EXCHANGE, (
        (RC, 1, 7), (RC, 1, 6),
    ), (
        (RC, 1, 7), (RC, 1, 6),
    )),
    (FF_BACK, 1, 0, 2),
    (FF_BACK, 1, 2, 4),
    (EXCHANGE, (
        (RC, 1, 4),
    ), (
        (RC, 1, 4),
    )),
    (FF_BACK, 1, 4, 6),
    (FF_BACK, 1, 6, 8),
    (EXCHANGE, (
        (R1, 1, 7), (R1, 1, 6), (RC, 1, 5),
    ), (
        (R1, 1, 7), (R1, 1, 6), (RC, 1, 5),
    )),
    (MID, 1),
    (EXCHANGE, (
        (R1, 1, 4),
    ), (
        (R1, 1, 4),
    )),
    (PROJECT_BACK, 1),
    (EXCHANGE, (
        (R1, 1, 5), (RC, 1, 3),
    ), (
        (R1, 1, 5), (RC, 1, 3),
    )),
    (ATTEND_BACK, 1, 0, 1),
    (ATTEND_BACK, 1, 1, 2),
    (EXCHANGE, (
        (RP, 1, 6), (R1, 1, 3),
    ), (
        (R1, 1, 3),
    )),
    (ATTEND_BACK, 1, 2, 3),
    (ATTEND_BACK, 1, 3, 4),
    (EXCHANGE, (
        (R2, 1, 7),
    ), (
        (R2, 1, 7),
    )),
    (QKV_GRAD, 1),
    (EXCHANGE, (
        (RC, 1, 2), (RC, 1, 0), (RC, 1, 1),
    ), (
        (RP, 1, 5), (RC, 1, 2), (RC, 1, 0), (RC, 1, 1),
    )),
    (QKV_BACK, 1),
    (EXCHANGE, (
        (R3, 1, 6),
    ), (
    )),
    (SEND_GRAD, 1),
    (SMALL_GRADS, 1),
    (EXCHANGE, (
        (RC, 1, 8), (R1, 1, 2),
    ), (
        (RC, 1, 8),
    )),
    (RELOAD, 1),
    (RELOAD, 2),
    (EXCHANGE, (
        (R1, 1, 0),
    ), (
    )),
    (EXCHANGE, (
        (GE, 0), (GE, 1),
    ), (
        (GE, 0), (GE, 1),
    )),
    (TOP_BACK, 0),
    (EXCHANGE, (
        (RY, 1, 5), (R1, 1, 1), (R2, 1, 4), (R1, 1, 8),
    ), (
        (R1, 1, 2), (R1, 1, 0), (R1, 1, 1), (RY, 1, 6), (R1, 1, 8), (R2, 1, 4),
    )),
    (FF_OUT_GRAD, 0),
    (EXCHANGE, (
        (RP, 1, 7), (RC, 0, 7), (RC, 0, 6),
    ), (
        (R3, 1, 5), (RP, 1, 7), (RC, 0, 7), (RC, 0, 6),
    )),
    (FF_BACK, 0, 0, 2),
    (FF_BACK, 0, 2, 4),
    (EXCHANGE, (
        (R2, 1, 3), (RC, 0, 4),
    ), (
        (R2, 1, 3), (RC, 0, 4),
    )),
    (FF_BACK, 0, 4, 6),
    (EXCHANGE, (
        (R1, 0, 7), (RP, 1, 2),
    ), (
        (RP, 1, 0), (R1, 0, 7),
    )),
    (FF_BACK, 0, 6, 8),
    (EXCHANGE, (
        (R1, 0, 6), (R1, 0, 4), (RY, 1, 0), (RC, 0, 5),
    ), (
        (R1, 0, 6), (R1, 0, 4), (RC, 0, 5),
    )),
    (MID, 0),
    (EXCHANGE, (
        (R3, 1, 7), (RP, 1, 4),
    ), (
        (R3, 1, 7), (RP, 1, 4),
    )),
    (PROJECT_BACK, 0),
    (EXCHANGE, (
        (R3, 1, 2), (R2, 1, 5), (R2, 1, 8), (R1, 0, 5), (RP, 1, 3), (RC, 0, 3),
    ), (
        (R3, 1, 0), (R2, 1, 6), (R2, 1, 8), (R1, 0, 5), (RC, 0, 3),
    )),
    (RELOAD, 0),
    (EXCHANGE, (
    ), (
        (RP, 1, 3),
    )),
    (ATTEND_BACK, 0, 0, 1),
    (EXCHANGE, (
        (RY, 1, 1),
    ), (
    )),
    (ATTEND_BACK, 0, 1, 2),
    (EXCHANGE, (
        (R3, 1, 4), (R1, 0, 3),
    ), (
        (R3, 1, 4), (R1, 0, 3),
    )),
    (ATTEND_BACK, 0, 2, 3),
    (EXCHANGE, (
        (R3, 1, 3), (RP, 0, 6), (R2, 0, 7),
    ), (
        (R3, 1, 3), (RP, 0, 4), (RY, 1, 2), (R2, 0, 7),
    )),
    (ATTEND_BACK, 0, 3, 4),
    (QKV_GRAD, 0),
    (EXCHANGE, (
        (RY, 0, 4), (R2, 1, 0), (RC, 0, 0), (RP, 1, 5), (RC, 0, 2), (RC, 0, 1),
    ), (
        (RC, 0, 0), (RC, 0, 2), (RC, 0, 1),
    )),
    (QKV_BACK, 0),
    (EXCHANGE, (
    ), (
        (RP, 1, 6),
    )),
    (SEND_GRAD, 0),
    (SMALL_GRADS, 0),
    (EXCHANGE, (
        (RC, 0, 8), (R1, 0, 0), (R3, 0, 6), (R1, 0, 2), (R2, 1, 1), (R3, 1, 8), (R1, 0, 1), (R1, 0, 8), (RY, 0, 5),
        (R3, 1, 5), (RP, 0, 7), (R2, 0, 3), (RP, 1, 0), (RP, 0, 2), (R3, 0, 7), (R2, 0, 4), (R2, 0, 8), (R3, 1, 0),
        (RP, 1, 1), (R3, 0, 2), (RP, 0, 1), (R3, 1, 1), (RP, 0, 3), (R2, 0, 5), (R3, 0, 1), (RP, 0, 4), (R3, 0, 3),
        (RY, 0, 0), (R3, 0, 8), (R3, 0, 4), (R4, 0, 4), (RP, 0, 5), (R4, 0, 7), (R4, 0, 3), (R4, 0, 8), (R2, 0, 0),
        (R4, 0, 6), (R3, 0, 5), (R4, 0, 5), (R4, 0, 2), (RP, 0, 0), (R4, 0, 1), (R3, 0, 0),
    ), (
        (RC, 0, 8), (R1, 0, 0), (R2, 0, 3), (R3, 0, 4), (R1, 0, 2), (R1, 0, 1), (R1, 0, 8), (RY, 0, 6), (R3, 1, 8),
        (R4, 1, 7), (R2, 1, 2), (R3, 1, 6), (R4, 1, 6), (RP, 0, 5), (R4, 1, 4), (R2, 0, 8), (R4, 1, 3), (RP, 0, 7),
        (RY, 0, 2), (R4, 1, 8), (R3, 0, 5), (R2, 0, 6), (RP, 0, 3), (RY, 0, 1), (R4, 1, 5), (R3, 0, 7), (RP, 1, 2),
        (R4, 1, 0), (R2, 0, 2), (R3, 0, 3), (R3, 0, 8), (R3, 1, 2), (R4, 1, 2), (RP, 0, 6), (R2, 0, 1), (R4, 1, 1),
        (RP, 0, 2), (R3, 0, 6), (RP, 0, 1), (R3, 0, 2), (R3, 0, 1),
    )),
    (EXCHANGE, (
        (RE, 1), (RE, 0),
    ), (
        (RE, 1), (RE, 0),
    )),
)


class Exchange:
    def __init__(self, o, grid, rp):
        self.o, self.rp = o, rp
        self.Z, self.X, self.C = grid
        self.s = lax.axis_index("section")
        d = lax.axis_index("dp")
        self.c = lax.rem(d, 2)
        self.x = lax.rem(d // 2, 2)
        self.z = d // 4

    def dev(self, s=None, z=None, x=None, c=None):
        s = self.s if s is None else s
        z = self.z if z is None else z
        x = self.x if x is None else x
        c = self.c if c is None else c
        return (s, (z * 2 + x) * 2 + c)

    def along_z(self, j):
        return lax.rem(self.z + j + 1, self.Z)

    def peers(self):
        out = [self.dev(z=self.along_z(j)) for j in range(self.Z - 1)]
        return out + [self.dev(x=1 - self.x), self.dev(c=1 - self.c), self.dev(s=1 - self.s)]

    def greet(self):
        for p in self.peers():
            pl.semaphore_signal(pltpu.get_barrier_semaphore(), inc=1, device_id=p, device_id_type=MESH)

    def met(self):
        pl.semaphore_wait(pltpu.get_barrier_semaphore(), len(self.peers()))

    def copy(self, src, dst, send, recv, dev):
        return pltpu.make_async_remote_copy(
            src_ref=src, dst_ref=dst, send_sem=send, recv_sem=recv, device_id=dev, device_id_type=MESH)

    def g_route(self, l, k):
        return BOTH if k == len(GATHER) else GATHER_ROUTE[l][k]

    def works(self, route, s, l):
        own, other = (OWN, X_OWN) if s == l else (OTHER, X_OTHER), (X_OTHER if s == l else X_OWN,)
        return route == BOTH or route in own, route == BOTH or route in own + other

    def g_copy(self, kind, s, l, k, j=0):
        o = self.o
        z, x, c = self.z, self.x, self.c
        if k == len(GATHER):
            w, mine, rows = o.wsm.at[l], o.own_small, slice(None)
        else:
            p, n = GATHER[k]
            w, mine, rows = o.wall.at[l], o.own, slice(p * self.rp, (p + n) * self.rp)
        ss, rr = o.gs.at[l, k], o.gr.at[l, k]
        if kind == ALONG_Z:
            a = w.at[z, x, c, rows]
            return self.copy(a, a, ss.at[j], rr.at[j], self.dev(z=self.along_z(j)))
        if kind == ALONG_X:
            a = w.at[:, x, c, rows]
            return self.copy(a, a, ss.at[3], rr.at[3], self.dev(x=1 - x))
        if kind == SHARD:
            return self.copy(mine.at[rows], w.at[z, x, c, rows], ss.at[4], rr.at[4], self.dev(s=1 - s))
        a = w.at[:, :, c, rows]
        if kind == PLANE:
            return self.copy(a, a, ss.at[4], rr.at[4], self.dev(s=1 - s))
        if kind == COLUMN:
            a = w.at[:, 1 - x, c, rows]
            return self.copy(a, a, ss.at[6], rr.at[6], self.dev(s=1 - s))
        if kind == PASS_ON:
            to = self.z // 2 * 3
            a = w.at[3 - to, x, c, rows]
            return self.copy(a, a, ss.at[7], rr.at[self.z // 2 * 2], self.dev(z=to))
        return self.copy(a, a, ss.at[5], rr.at[5], self.dev(c=1 - c))

    def gy(self, s, l, k):
        self.g_copy(SHARD, s, l, k).start()

    def unless_end(self, j, f):
        if j == 1:
            f()
        else:
            pl.when(self.z != (0 if j == 2 else self.Z - 1))(f)

    def on_middle(self, f):
        pl.when((self.z > 0) & (self.z < self.Z - 1))(f)

    def on_ends(self, f):
        pl.when((self.z == 0) | (self.z == self.Z - 1))(f)

    def gz(self, s, l, k):
        if s != l:
            self.g_copy(SHARD, s, l, k).wait_recv()
        for j in range(self.Z - 1):
            self.unless_end(j, self.g_copy(ALONG_Z, s, l, k, j).start)

    def gf(self, s, l, k):
        @self.on_middle
        def _():
            self.g_copy(ALONG_Z, s, l, k, 1).wait_recv()
            self.g_copy(PASS_ON, s, l, k).start()

    def gx(self, s, l, k):
        self.g_copy(ALONG_Z, s, l, k, 0).wait_recv()
        self.on_ends(self.g_copy(ALONG_Z, s, l, k, 1).wait_recv)
        self.g_copy(ALONG_Z, s, l, k, 2).wait_recv()
        if self.works(self.g_route(l, k), s, l)[0]:
            self.g_copy(ALONG_X, s, l, k).start()

    def gc(self, s, l, k):
        route = self.g_route(l, k)
        on_x, on_z = self.works(route, s, l)
        beyond = PLANE if route in (OWN, OTHER) else COLUMN
        if on_x:
            self.g_copy(ALONG_X, s, l, k).wait_recv()
            if route != BOTH:
                self.g_copy(beyond, s, l, k).start()
        else:
            self.g_copy(beyond, s, l, k).wait_recv()
        self.g_copy(TO_CORE, s, l, k).start()

    def gd(self, s, l, k):
        self.g_copy(TO_CORE, s, l, k).wait_recv()

    def ge(self, s, l):
        for k in range(len(GATHER) + 1):
            route = self.g_route(l, k)
            on_x, on_z = self.works(route, s, l)
            if s == l and route != OWN:
                self.g_copy(SHARD, s, l, k).wait_send()
            if on_z:
                for j in range(self.Z - 1):
                    self.unless_end(j, self.g_copy(ALONG_Z, s, l, k, j).wait_send)
                self.on_middle(self.g_copy(PASS_ON, s, l, k).wait_send)
            if on_x:
                self.g_copy(ALONG_X, s, l, k).wait_send()
                if route != BOTH:
                    self.g_copy(PLANE if route in (OWN, OTHER) else COLUMN, s, l, k).wait_send()
            self.g_copy(TO_CORE, s, l, k).wait_send()

    def r_small(self, k):
        return k == len(REDUCE)

    def r_route(self, l, k):
        return BOTH if self.r_small(k) else REDUCE_ROUTE[l][k]

    def r_bufs(self, l, k):
        o = self.o
        if self.r_small(k):
            return o.gsm.at[l], slice(None), o.r1s.at[l], o.rxs.at[l], o.rzs.at[l], o.rys
        p, n = REDUCE[k]
        g = o.g1 if l == 1 else o.wall.at[1]
        return g, slice(p * self.rp, (p + n) * self.rp), o.r1, o.rx.at[l], o.rz.at[l], o.rf

    def r_late(self, l, k):
        at, n = late_place(l, k)
        return slice(at * self.rp, (at + n) * self.rp)

    def r_copy(self, kind, s, l, k, j=0):
        o = self.o
        g, rows, r1, rx, rz, rf = self.r_bufs(l, k)
        z, x, c = self.z, self.x, self.c
        ss, rr = o.ss.at[l, k], o.sr.at[l, k]
        if kind == TO_CORE:
            return self.copy(g.at[:, :, 1 - c, rows], r1.at[:, :, rows], ss.at[0], rr.at[0], self.dev(c=1 - c))
        if kind == ALONG_X:
            return self.copy(g.at[:, 1 - x, c, rows], rx.at[:, rows], ss.at[1], rr.at[1], self.dev(x=1 - x))
        if kind == ALONG_Z:
            to = self.along_z(j)
            return self.copy(g.at[to, x, c, rows], rz.at[z, rows], ss.at[2 + j], rr.at[2 + j], self.dev(z=to))
        if kind == PASS_ON:
            to = z // 2 + 1
            return self.copy(g.at[self.Z - 1 - z, x, c, rows], rz.at[to, rows], ss.at[7], rr.at[7], self.dev(z=to))
        if kind == COLUMN:
            return self.copy(g.at[:, 1 - x, c, rows], o.rcol.at[:, self.r_late(l, k)], ss.at[6], rr.at[6],
                             self.dev(s=1 - s))
        if kind == PLANE:
            return self.copy(g.at[:, :, c, rows], o.ry.at[:, :, self.r_late(l, k)], ss.at[5], rr.at[5],
                             self.dev(s=1 - s))
        return self.copy(g.at[z, x, c, rows], rf.at[rows], ss.at[5], rr.at[5], self.dev(s=1 - s))

    def add(self, n, dst, src):
        def one(i, _):
            d = dst(i)
            d[...] = d[...] + src(i)[...]
            return 0

        lax.fori_loop(0, n, one, 0)

    def rc(self, s, l, k):
        if l == 0 and not self.r_small(k):
            pl.semaphore_wait(self.o.credit.at[k], 1)
        self.r_copy(TO_CORE, s, l, k).start()

    def r1(self, s, l, k):
        g, rows, r1, rx, rz, rf = self.r_bufs(l, k)
        c, X = self.c, self.X
        self.r_copy(TO_CORE, s, l, k).wait_recv()
        self.add(self.Z * X, lambda i: g.at[i // X, lax.rem(i, X), c, rows], lambda i: r1.at[i // X, lax.rem(i, X), rows])
        if l == 1 and not self.r_small(k):
            pl.semaphore_signal(self.o.credit.at[k], inc=1, device_id=self.dev(c=1 - c), device_id_type=MESH)
        route = self.r_route(l, k)
        on_x, on_z = self.works(route, s, l)
        if route == BOTH:
            self.r_copy(ALONG_X, s, l, k).start()
        elif not on_x:
            self.r_copy(PLANE if route in (OWN, OTHER) else COLUMN, s, l, k).start()
            if on_z:
                self.z_sends(s, l, k)

    def z_sends(self, s, l, k):
        if self.r_small(k):
            for j in range(self.Z - 1):
                self.r_copy(ALONG_Z, s, l, k, j).start()
        else:
            self.on_ends(self.r_copy(PASS_ON, s, l, k).start)
            for j in (0, 2):
                self.unless_end(j, self.r_copy(ALONG_Z, s, l, k, j).start)
            self.on_ends(self.r_copy(ALONG_Z, s, l, k, 1).start)

    def ry(self, s, l, k):
        g, rows, r1, rx, rz, rf = self.r_bufs(l, k)
        c, X, late = self.c, self.X, self.r_late(l, k)
        if self.r_route(l, k) in (OWN, OTHER):
            self.r_copy(PLANE, s, l, k).wait_recv()
            self.add(self.Z * X, lambda i: g.at[i // X, lax.rem(i, X), c, rows],
                     lambda i: self.o.ry.at[i // X, lax.rem(i, X), late])
        else:
            self.r_copy(COLUMN, s, l, k).wait_recv()
            self.add(self.Z, lambda i: g.at[i, 1 - self.x, c, rows], lambda i: self.o.rcol.at[i, late])
        self.r_copy(ALONG_X, s, l, k).start()

    def r2(self, s, l, k):
        g, rows, r1, rx, rz, rf = self.r_bufs(l, k)
        x, c = self.x, self.c
        self.r_copy(ALONG_X, s, l, k).wait_recv()
        self.add(self.Z, lambda i: g.at[i, x, c, rows], lambda i: rx.at[i, rows])
        self.z_sends(s, l, k)

    def r_pass(self, s, l, k):
        g, rows, r1, rx, rz, rf = self.r_bufs(l, k)
        z, x, c = self.z, self.x, self.c

        @self.on_middle
        def _():
            far = (2 - z) * 3
            self.r_copy(PASS_ON, s, l, k).wait_recv()
            g[far, x, c, rows] = g[far, x, c, rows] + rz[z, rows]
            self.r_copy(ALONG_Z, s, l, k, 1).start()

    def r3(self, s, l, k):
        g, rows, r1, rx, rz, rf = self.r_bufs(l, k)
        z, x, c = self.z, self.x, self.c
        if self.r_small(k):
            for j in range(self.Z - 1):
                self.r_copy(ALONG_Z, s, l, k, j).wait_recv()
            rz[z, rows] = g[z, x, c, rows]
            total = rz[0, rows].astype(F32)
            for i in range(1, self.Z):
                total = total + rz[i, rows].astype(F32)
            g[z, x, c, rows] = total
            if s != l:
                self.r_copy(SHARD, s, l, k).start()
            return
        for j in range(self.Z - 1):
            (self.unless_end if j != 1 else self.always)(2 - j, self.r_copy(ALONG_Z, s, l, k, j).wait_recv)
        total = g[z, x, c, rows].astype(F32) + rz[lax.rem(z + 2, self.Z), rows].astype(F32)
        total = total + rz[z + 1 - 2 * lax.rem(z, 2), rows].astype(F32)
        acc = self.o.sum_s.at[0 : total.shape[0]]
        acc[...] = total

        @self.on_middle
        def _():
            acc[...] = acc[...] + rz[self.Z - 1 - z, rows].astype(F32)

        if s == l and self.r_route(l, k) == OWN:
            self.result(k, acc[...])
        else:
            g[z, x, c, rows] = acc[...].astype(g.dtype)
            if s != l:
                self.r_copy(SHARD, s, l, k).start()

    def always(self, j, f):
        f()

    def r4(self, s, l, k):
        g, rows, r1, rx, rz, rf = self.r_bufs(l, k)
        self.r_copy(SHARD, s, l, k).wait_recv()
        total = rf[rows].astype(F32)
        if self.r_route(l, k) in (BOTH, X_OWN, X_OTHER):
            total = g[self.z, self.x, self.c, rows].astype(F32) + total
        self.result(k, total)

    def result(self, k, v):
        o, rp = self.o, self.rp
        if self.r_small(k):
            o.d_small[...] = v
            return
        p0, n = REDUCE[k]
        w = v.shape[1]
        for i in range(n):
            p, t = p0 + i, v[i * rp : (i + 1) * rp]
            if p < 3:
                o.d_wq[0, :, p * w : (p + 1) * w] = t
            elif p == 3:
                o.d_wo[0] = t
            elif p < 8:
                o.d_wi[0, :, (p - 4) * w : (p - 3) * w] = t
            else:
                o.wft[(p - 8) * rp : (p - 7) * rp, :] = t

    def turn(self):
        for m in range(self.o.wft.shape[1] // 128):
            ms = slice(m * 128, m * 128 + 128)
            self.o.d_wf[0, :, ms] = self.o.wft[:, ms].T

    def re(self, s, l):
        for k in range(len(REDUCE) + 1):
            route = self.r_route(l, k)
            on_x, on_z = self.works(route, s, l)
            self.r_copy(TO_CORE, s, l, k).wait_send()
            if on_x:
                self.r_copy(ALONG_X, s, l, k).wait_send()
            else:
                self.r_copy(PLANE if route in (OWN, OTHER) else COLUMN, s, l, k).wait_send()
            if on_z:
                if self.r_small(k):
                    for j in range(self.Z - 1):
                        self.r_copy(ALONG_Z, s, l, k, j).wait_send()
                else:
                    for j in range(self.Z - 1):
                        self.unless_end(j, self.r_copy(ALONG_Z, s, l, k, j).wait_send)
                    self.on_ends(self.r_copy(PASS_ON, s, l, k).wait_send)
                if s != l:
                    self.r_copy(SHARD, s, l, k).wait_send()


def kernel(names, grid, *refs):
    o = types.SimpleNamespace(**dict(zip(names, refs)))
    fused = grid is not None
    W = o.h_s.shape[2]
    FF = o.f_s.shape[1]
    Z, X, C, total = o.wall.shape[1:5]
    rp = total // PARTS
    flag, hb, wall, g1 = o.flag, o.hb, o.wall, o.g1
    q_s, k_s, v_s, p_s, c_s, cl_s, xh1, rst, n1 = o.q_s, o.k_s, o.v_s, o.p_s, o.c_s, o.cl_s, o.xh1, o.rst, o.n1
    f_s, gp, xh2, y_s, h_s, oc = o.f_s, o.gp, o.xh2, o.y_s, o.h_s, o.oc
    gin1, mask_s, g_s, go, gh_s, ds_s, gqkv, xt, cols = o.gin1, o.mask_s, o.g_s, o.go, o.gh_s, o.ds_s, o.gqkv, o.xt, o.cols
    vec, bff, dvec, dbff, sems = o.vec, o.bff, o.dvec, o.dbff, o.sems

    R = h_s.shape[1]
    s = lax.axis_index("section")
    mine = pl.ds(tiled(s * R, R), R)
    tc = o.tc_in[mine].reshape(1, R)
    mask = o.mask_in[mine].reshape(1, R).astype(F32)
    hw = o.hw_in[...].reshape(1, W)
    long = flag[s] == 1
    if fused:
        ex = Exchange(o, grid, rp)
        z, x, c = ex.z, ex.x, ex.c
        ex.greet()
        own, ins = o.own, o.own_sems
        loads = [(o.wq_in.at[0, :, i * W : (i + 1) * W], i * rp, rp) for i in range(3)]
        loads += [(o.wo_in.at[0], 3 * rp, rp)]
        loads += [(o.wi_in.at[0, :, i * W : (i + 1) * W], (4 + i) * rp, rp) for i in range(4)]
        loads += [(o.wf_in.at[0], 8 * rp, 4 * rp)]
        loads = [pltpu.make_async_copy(a, own.at[at : at + n], ins.at[i]) for i, (a, at, n) in enumerate(loads)]
        cin = [pltpu.make_async_copy(o.x_in.at[mine], h_s.at[0], sems.at[0]),
               pltpu.make_async_copy(o.oc_in.at[mine], oc, sems.at[1])]
        for t in loads + cin:
            t.start()
        nv, nb = o.vec_in.shape[2], o.bff_in.shape[1]
        o.own_small[...] = jnp.zeros(o.own_small.shape, F32)
        o.own_small[0:8, 0:nv] = o.vec_in[0].astype(F32)
        o.own_small[8:9, 0:nb] = o.bff_in[...].astype(F32)
        o.wsm[s, z, x, c] = o.own_small[...]
        for t in loads:
            t.wait()
        wall[s, z, x, c] = own[...]
        ex.met()
    else:
        cin = [pltpu.make_async_copy(o.x_in.at[mine], h_s.at[0], sems.at[0]),
               pltpu.make_async_copy(o.oc_in.at[mine], oc, sems.at[1]),
               pltpu.make_async_copy(o.w_in, wall, sems.at[2])]
        for t in cin:
            t.start()
        vec[...] = o.vec_in[...]
        bff[...] = o.bff_in[...]

    if not fused:
        for t in cin:
            t.wait()

    lane = lax.broadcasted_iota(jnp.int32, (W, 128), 1)
    row_run = lax.broadcasted_iota(jnp.int32, (W, 128), 0) // RUN
    flagged = lambda cond: cond.astype(F32).astype(BF16)
    sides = (flagged(lane < 64), flagged(lane >= 64))
    spare = (lane - 64, lane)
    run_lane = tuple(flagged(t == row_run) for t in spare)
    two_lanes = tuple(flagged((t == 0) | (t == 1)) for t in spare)

    valid = mask > 0.0
    key_run = lax.broadcasted_iota(jnp.int32, (8, W), 1) // RUN
    query_run = lax.broadcasted_iota(jnp.int32, (8, W), 0)
    open_key = valid & ((key_run == query_run) | long)
    blocked = jnp.where(open_key, 0.0, -1e9).T
    for t in range(2):
        wide = jnp.zeros((W, 128), F32)
        for r in range(R // RUN):
            wide = jnp.where(spare[t] == r, blocked[:, r : r + 1], wide)
        mask_s[t] = wide.astype(BF16)

    def small_weights(l):
        for i in range(Z * X * C):
            b = o.wsm.at[l, i // (X * C), (i // C) % X, i % C]
            vec[l, :, i * nv : (i + 1) * nv] = b[0:8, 0:nv]
            bff[l, 0:1, i * nb : (i + 1) * nb] = b[8:9, 0:nb]

    def part(l, p, cs=slice(None)):
        a = wall[l, :, :, :, pl.ds(tiled(p * rp, rp), rp), cs]
        return a.reshape(W, a.shape[-1])

    def part_rows(l, p, r0, n):
        if C == 1:
            return wall[l, 0, 0, 0, pl.ds(tiled(p * rp + r0, n), n), :]
        k = n // (X * C * rp)
        return wall[l, pl.ds(r0 // (X * C * rp), k), :, :, pl.ds(tiled(p * rp, rp), rp), :].reshape(n, W)

    def back_w(l, cs):
        a = wall[l, :, :, :, 8 * rp :, cs]
        return a.reshape(FF, a.shape[-1])

    def back_rows(l, j, n):
        if C == 1:
            return wall[l, 0, 0, 0, pl.ds(tiled(8 * rp + j * n, n), n), :]
        return wall[l, j // X, lax.rem(j, X), :, 8 * rp :, :].reshape(n, W)

    def g_ref(l):
        return g1 if l == 1 else wall.at[1]

    def put_part(l, p, cs, val):
        rows = pl.ds(tiled(p * rp, rp), rp)
        g_ref(l)[:, :, :, rows, cs] = val.reshape(Z, X, C, rp, -1).astype(BF16)

    def put_back(l, j, val):
        val = val.astype(BF16)
        for i in range(val.shape[1] // 128):
            for m in range(W // 128):
                block = val[m * 128 : m * 128 + 128, i * 128 : i * 128 + 128]
                ms = slice(m * 128, m * 128 + 128)
                if C == 1:
                    g_ref(l)[0, 0, 0, pl.ds(tiled(8 * rp + (4 * j + i) * 128, 128), 128), ms] = block
                else:
                    g_ref(l)[j, i // C, i % C, 8 * rp :, ms] = block

    def vrow(l, i):
        return vec[l, i : i + 1, :]

    def keep(src, dst, i):
        return pltpu.make_async_copy(src, dst, sems.at[i])

    def qkv(l):
        h = h_s.at[l]
        if fused and l == 0:
            cin[0].wait()

        def step(j, _):
            cs = pl.ds(tiled(j * 256, 256), 256)
            hv = h[...]
            rq = dot(hv, part(l, 0, cs)) + vec[l, 0:1, cs]
            q_s[l, :, cs] = (rq.astype(BF16).astype(F32) * 0.125).astype(BF16)
            k_s[l, :, cs] = dot(hv, part(l, 1, cs)).astype(BF16)
            v_s[l, :, cs] = (dot(hv, part(l, 2, cs)) + vec[l, 1:2, cs]).astype(BF16)
            return 0

        loop(0, 2, step)

    def attend(l, p0, p1):
        def pair(p, _):
            cs = pl.ds(tiled(p * 128, 128), 128)
            k2 = k_s[l, :, cs]
            v2 = v_s[l, :, cs]
            for r in range(0, R, ATTEND_ROWS):
                rs = slice(r, r + ATTEND_ROWS)
                q2 = q_s[l, rs, cs]
                c = []
                for t in range(2):
                    raw = dot_nt(q2 * sides[t][rs] + run_lane[t][rs], k2 * sides[t] + mask_s[t])
                    for b in range(0, ATTEND_ROWS, SOFTMAX_ROWS):
                        a = raw[b : b + SOFTMAX_ROWS]
                        e = jnp.exp(a - jnp.max(a, -1, keepdims=True))
                        e = e * (1.0 / jnp.sum(e, -1, keepdims=True))
                        p_s[2 * p + t, r + b : r + b + SOFTMAX_ROWS, :] = e.astype(BF16)
                    c.append(dot(p_s[2 * p + t, rs, :], v2 * sides[t]))
                c = c[0] + c[1]
                c_s[l, rs, cs] = c.astype(BF16)
                cl_s[l, rs, cs] = (c - c.astype(BF16).astype(F32)).astype(BF16)
            return 0

        lax.fori_loop(p0, p1, pair, 0)
        if l == 0 and p1 == 4:
            keep(p_s, o.keep_p, 3).start()

    def project(l):
        def step(j, _):
            rs = pl.ds(tiled(j * 256, 256), 256)
            y = h_s[l, rs, :].astype(F32) + dot(c_s[l, rs, :], part(l, 3)) + vrow(l, 2)
            xh, r = layer_norm_rows(y)
            xh1[l, rs, :] = xh
            rst[l, rs, 0:1] = r
            n1[l, rs, :] = (xh * vrow(l, 3) + vrow(l, 4)).astype(BF16)
            return 0

        loop(0, 2, step)

    def ff_in(l, j0, j1):
        def step(j, _):
            cs = pl.ds(tiled(j * 256, 256), 256)
            sub = pl.ds(tiled((j % 2) * 256, 256), 256)
            u = dot(n1[l], part(l, 4 + j // 2, sub))
            b = bff[l, 0:1, cs]
            for r in range(0, W, GELU_ROWS):
                f, d = gelu_both(u[r : r + GELU_ROWS] + b)
                f_s[r : r + GELU_ROWS, cs] = f.astype(BF16)
                gp[r : r + GELU_ROWS, cs] = d.astype(BF16)
            return 0

        loop(j0, j1, step)

    def ff_out(l):
        def step(j, _):
            cs = pl.ds(tiled(j * 256, 256), 256)
            y_s[:, cs] = dot(f_s[...], back_w(l, cs))
            return 0

        loop(0, 2, step)
        if l == 0:
            keep(f_s, o.keep_f, 4).start()
            keep(gp, o.keep_g, 5).start()

        def top(j, _):
            rs = pl.ds(tiled(j * RUN, RUN), RUN)
            y = xh1[l, rs, :] * vrow(l, 3) + vrow(l, 4) + y_s[rs, :] + vrow(l, 5)
            xh, r = layer_norm_rows(y)
            xh2[l, rs, :] = xh
            rst[l, rs, 1:2] = r
            h_s[l + 1, rs, :] = (xh * vrow(l, 6) + vrow(l, 7)).astype(BF16)
            return 0

        loop(0, 4, top)

    spilled = ((p_s, o.keep_p, 3), (f_s, o.keep_f, 4), (gp, o.keep_g, 5))

    def restore(i):
        src, dst, at = spilled[i]
        keep(src, dst, at).wait()

    def reload(i):
        src, dst, at = spilled[i]
        keep(dst, src, at).wait()

    act1 = h_s.at[2]

    def head():
        hw16 = jnp.broadcast_to(hw, (16, W))
        zr = dot_nt(hw16, act1[...])[0:1] + hb[0]
        ez = jnp.exp(-jnp.abs(zr))
        terms = jnp.log1p(ez) + jnp.maximum(zr, 0.0)
        sig = jnp.where(zr >= 0.0, 1.0, ez) / (1.0 + ez)
        gz = tc * mask * sig
        o.dhb[...] = jnp.sum(gz, -1, keepdims=True)
        sub8 = lax.broadcasted_iota(jnp.int32, (8, W), 0)
        cols[...] = jnp.where(sub8 == 0, gz, jnp.where(sub8 == 1, mask, 0.0)).T
        if fused:
            o.term[s] = terms
            send_term.start()
        else:
            o.term[...] = terms

    if fused:
        own_rows = mine
        across = ex.dev(s=1 - s)
        put_act = ex.copy(h_s.at[2 - s], o.act_out.at[own_rows], o.os.at[0], o.orr.at[0], across)
        send_term = ex.copy(o.term.at[s], o.term.at[s], o.os.at[1], o.orr.at[1], across)
        own_act = pltpu.make_async_copy(h_s.at[1 + s], o.act_out.at[own_rows], sems.at[0])
        send_g = [ex.copy(g, o.gin_out.at[own_rows], o.os.at[2], o.orr.at[2], across) for g in (oc, gin1)]
        own_g = [pltpu.make_async_copy(g, o.gin_out.at[own_rows], sems.at[1]) for g in (oc, gin1)]

    def send_act(i):
        pl.when(s != i)(put_act.start)
        pl.when(s == i)(own_act.start)

    def send_grad(i):
        pl.when(s != i)(send_g[i].start)
        pl.when(s == i)(own_g[i].start)

    def top_back(l):
        if fused and l == 1:
            cin[1].wait()
        zero = jnp.zeros((8, W), F32)

        def step(j, carry):
            sg, ss, sb, sh = carry
            rs = pl.ds(tiled(j * RUN, RUN), RUN)
            if l == 1:
                gzc = cols[rs, 0:1]
                g = oc[rs, :].astype(F32) * cols[rs, 1:2] + gzc * hw.astype(F32)
                sh = sh + rows8(gzc * act1[rs, :].astype(F32))
            else:
                g = gin1[rs, :].astype(F32)
            xh = xh2[l, rs, :]
            sg = sg + rows8(g * xh)
            ss = ss + rows8(g)
            gy = layer_norm_back(g, vrow(l, 6), xh, rst[l, rs, 1:2])
            g_s[rs, :] = gy
            gl = gy.astype(BF16)
            go[rs, :] = gl
            sb = sb + rows8(gl.astype(F32))
            return sg, ss, sb, sh

        sg, ss, sb, sh = lax.fori_loop(0, 4, step, (zero,) * 4)
        dvec[l, 6:7, :] = jnp.sum(sg, 0, keepdims=True)
        dvec[l, 7:8, :] = jnp.sum(ss, 0, keepdims=True)
        dvec[l, 5:6, :] = jnp.sum(sb, 0, keepdims=True)
        if l == 1:
            o.dhw[...] = jnp.sum(sh, 0, keepdims=True)

    def ff_out_grad(l):
        xt[...] = go[...].T

        def step(j, _):
            cs = pl.ds(tiled(j * 512, 512), 512)
            put_back(l, j, dot(xt[...], f_s[:, cs]))
            return 0

        loop(0, FF // 512, step)

    def ff_back(l, j0, j1):
        if j0 == 0:
            xt[...] = n1[l].T

        def step(j, _):
            cs = pl.ds(tiled(j * 256, 256), 256)
            gf = dot_nt(go[...], back_rows(l, j, 256))
            total = jnp.zeros((8, 256), F32)
            for r in range(0, W, GELU_ROWS):
                gul = (gf[r : r + GELU_ROWS] * gp[r : r + GELU_ROWS, cs].astype(F32)).astype(BF16)
                f_s[r : r + GELU_ROWS, cs] = gul
                total = total + rows8(gul.astype(F32))
            dbff[l, 0:1, cs] = jnp.sum(total, 0, keepdims=True)
            return 0

        loop(j0, j1, step)

        def grad(j, _):
            cs = pl.ds(tiled(j * 512, 512), 512)
            put_part(l, 4 + j, slice(None), dot(xt[...], f_s[:, cs]))
            return 0

        loop(j0 // 2, j1 // 2, grad)

    def mid(l):
        def step(j, _):
            cs = pl.ds(tiled(j * 256, 256), 256)
            acc = None
            for p in range(4):
                d = dot_nt(f_s[:, p * W : (p + 1) * W], part_rows(l, 4 + p, j * 256, 256))
                acc = d if acc is None else acc + d
            y_s[:, cs] = acc
            return 0

        loop(0, 2, step)
        if l == 1:
            keep(o.keep_f, f_s, 4).start()
            keep(o.keep_g, gp, 5).start()

        zero = jnp.zeros((8, W), F32)

        def back(j, carry):
            sg, ss, sb = carry
            rs = pl.ds(tiled(j * RUN, RUN), RUN)
            g = g_s[rs, :] + y_s[rs, :]
            xh = xh1[l, rs, :]
            sg = sg + rows8(g * xh)
            ss = ss + rows8(g)
            gy = layer_norm_back(g, vrow(l, 3), xh, rst[l, rs, 0:1])
            g_s[rs, :] = gy
            gl = gy.astype(BF16)
            go[rs, :] = gl
            sb = sb + rows8(gl.astype(F32))
            return sg, ss, sb

        sg, ss, sb = lax.fori_loop(0, 4, back, (zero,) * 3)
        dvec[l, 3:4, :] = jnp.sum(sg, 0, keepdims=True)
        dvec[l, 4:5, :] = jnp.sum(ss, 0, keepdims=True)
        dvec[l, 2:3, :] = jnp.sum(sb, 0, keepdims=True)

    def project_back(l):
        put_part(l, 3, slice(None), dot_tn(c_s[l], go[...]))
        gc = dot_nt(go[...], part(l, 3))
        for i in range(0, W, 128):
            gl = gc[:, i : i + 128].astype(BF16)
            go[:, i : i + 128] = gl
            w = gl.astype(F32) * (c_s[l, :, i : i + 128].astype(F32) + cl_s[l, :, i : i + 128].astype(F32))
            low = lane < 64
            offs = (jnp.sum(jnp.where(low, w, 0.0), -1, keepdims=True), jnp.sum(jnp.where(low, 0.0, w), -1, keepdims=True))
            for t in range(2):
                hi = offs[t].astype(BF16).astype(F32)
                off = jnp.where(spare[t] == 0, -hi, jnp.where(spare[t] == 1, hi - offs[t], 0.0))
                gh_s[t, :, i : i + 128] = gl * sides[t] + off.astype(BF16)
        xt[...] = go[...].T

    def attend_back(l, p0, p1):
        def pair(p, _):
            c0 = tiled(p * 128, 128)
            cs = pl.ds(c0, 128)
            k2 = k_s[l, :, cs]
            v2 = v_s[l, :, cs]
            qt = q_s[l, :, cs].T
            gct = xt[cs, :]
            dq = [None] * (R // ATTEND_ROWS)
            dvt, dkt = [], []
            for t in range(2):
                for i in range(len(dq)):
                    r = i * ATTEND_ROWS
                    rs = slice(r, r + ATTEND_ROWS)
                    w = dot_nt(gh_s[t, rs, cs], v2 * sides[t] + two_lanes[t])
                    for b in range(0, ATTEND_ROWS, SOFTMAX_ROWS):
                        bs = slice(r + b, r + b + SOFTMAX_ROWS)
                        ds_s[t, bs, :] = (p_s[2 * p + t, bs, :].astype(F32) * w[b : b + SOFTMAX_ROWS]).astype(BF16)
                    dd = dot(ds_s[t, rs, :], k2 * sides[t])
                    dq[i] = dd if dq[i] is None else dq[i] + dd
                hs = slice(64 * t, 64 * t + 64)
                dvt.append(dot(gct[hs], p_s[2 * p + t]))
                dkt.append(dot(qt[hs], ds_s[t]))
            dql = (jnp.concatenate(dq, 0) * 0.125).astype(BF16)
            dvl = jnp.concatenate(dvt, 0).T.astype(BF16)
            dkl = jnp.concatenate(dkt, 0).T.astype(BF16)
            gqkv[:, cs] = dql
            gqkv[:, pl.ds(tiled(c0 + W, 128), 128)] = dkl
            gqkv[:, pl.ds(tiled(c0 + 2 * W, 128), 128)] = dvl
            dvec[l, 0:1, cs] = jnp.sum(rows8(dql.astype(F32)), 0, keepdims=True)
            dvec[l, 1:2, cs] = jnp.sum(rows8(dvl.astype(F32)), 0, keepdims=True)
            return 0

        lax.fori_loop(p0, p1, pair, 0)
        if p1 == 4:
            if l == 1:
                keep(o.keep_p, p_s, 3).start()
            xt[...] = h_s[l].T

    def qkv_grad(l):
        for p in range(3):
            put_part(l, p, slice(None), dot(xt[...], gqkv[:, p * W : (p + 1) * W]))

    def qkv_back(l):
        gdst = gin1 if l == 1 else oc

        def step(j, _):
            cs = pl.ds(tiled(j * 256, 256), 256)
            acc = g_s[:, cs]
            for p in range(3):
                acc = acc + dot_nt(gqkv[:, p * W : (p + 1) * W], part_rows(l, p, j * 256, 256))
            gdst[:, cs] = acc.astype(BF16)
            return 0

        loop(0, 2, step)

    def small_grads(l):
        for i in range(Z * X * C):
            b = o.gsm.at[l, i // (X * C), (i // C) % X, i % C]
            b[...] = jnp.zeros(b.shape, F32)
            b[0:8, 0:nv] = dvec[l, :, i * nv : (i + 1) * nv]
            b[8:9, 0:nb] = dbff[l, 0:1, i * nb : (i + 1) * nb]
            for t in range(W // 128):
                b[9 + t : 10 + t, :] = o.dhw[0:1, t * 128 : (t + 1) * 128]
            b[9 + W // 128 : 10 + W // 128, 0:1] = o.dhb[...]

    steps = {
        QKV: qkv, ATTEND: attend, PROJECT: project, FF_IN: ff_in, FF_OUT: ff_out, RESTORE: restore, HEAD: head,
        TOP_BACK: top_back, FF_OUT_GRAD: ff_out_grad, FF_BACK: ff_back, MID: mid, PROJECT_BACK: project_back,
        ATTEND_BACK: attend_back, QKV_GRAD: qkv_grad, QKV_BACK: qkv_back, RELOAD: reload,
    }
    def exchange(*lists):
        for sec, todo in enumerate(lists):
            if todo:
                @pl.when(s == sec)
                def _():
                    for what, *which in todo:
                        calls[what](sec, *which)

    if fused:
        calls = {GY: ex.gy, GZ: ex.gz, GX: ex.gx, GC: ex.gc, GD: ex.gd, GE: ex.ge, GF: ex.gf, RP: ex.r_pass,
                 RC: ex.rc, R1: ex.r1, RY: ex.ry, R2: ex.r2, R3: ex.r3, R4: ex.r4, RE: ex.re}
        steps |= {EXCHANGE: exchange, SMALL_WEIGHTS: small_weights, SMALL_GRADS: small_grads, SEND_ACT: send_act,
                  SEND_GRAD: send_grad}
    for name, *args in FUSED_STEPS if fused else PLAIN_STEPS:
        steps[name](*args)

    if fused:
        ex.turn()
        put_act.wait()
        send_term.wait()
        own_act.wait()
        send_g[0].wait()
        own_g[0].wait()
    else:
        outs = [pltpu.make_async_copy(g1, o.g_out.at[1], sems.at[0]),
                pltpu.make_async_copy(wall.at[1], o.g_out.at[0], sems.at[1]),
                pltpu.make_async_copy(h_s.at[pl.ds(1, 2)], o.act_out, sems.at[2]),
                pltpu.make_async_copy(oc, o.gin_out.at[0], sems.at[3]),
                pltpu.make_async_copy(gin1, o.gin_out.at[1], sems.at[4])]
        for t in outs:
            t.start()
        for t in outs:
            t.wait()


def make_call(rows, width, inner, n_vec, n_bias, grid, gather=None):
    f32 = lambda *t: jax.ShapeDtypeStruct(t, F32)
    b16 = lambda *t: jax.ShapeDtypeStruct(t, BF16)
    v = lambda dt, *t: pltpu.VMEM(t, dt)
    Z, X, C = grid or (1, 1, 1)
    rp = width // (Z * X * C)
    total = PARTS * rp
    vm = pl.BlockSpec(memory_space=pltpu.VMEM)
    sm = pl.BlockSpec(memory_space=pltpu.SMEM)
    hbm = pl.BlockSpec(memory_space=pl.ANY)
    ins = dict(flag=sm, hb=sm, x_in=hbm, oc_in=hbm, tc_in=vm, mask_in=vm, hw_in=vm)
    if grid:
        ins |= dict(wq_in=hbm, wo_in=hbm, wi_in=hbm, wf_in=hbm, vec_in=vm, bff_in=vm)
        outs = dict(
            act_out=(b16(2 * rows, width), hbm), gin_out=(b16(2 * rows, width), hbm),
            term=(f32(2, 1, rows), vm),
            d_wq=(f32(1, rp, 3 * width), vm), d_wo=(f32(1, rp, width), vm), d_wi=(f32(1, rp, inner), vm),
            d_wf=(f32(1, 4 * rp, width), vm), d_small=(f32(16, 128), vm),
        )
    else:
        ins |= dict(w_in=hbm, vec_in=vm, bff_in=vm)
        outs = dict(
            act_out=(b16(2, rows, width), hbm), gin_out=(b16(2, rows, width), hbm), term=(f32(1, rows), vm),
            g_out=(b16(2, 1, 1, 1, total, width), hbm), dvec=(f32(2, 8, width), vm),
            dbff=(f32(2, 1, inner), vm), dhw=(f32(1, width), vm), dhb=(f32(1, 1), vm),
        )
    outs |= dict(keep_p=(b16(HEADS, rows, rows), hbm), keep_f=(b16(rows, inner), hbm),
             keep_g=(b16(rows, inner), hbm))
    scratch = dict(
        wall=v(BF16, 2, Z, X, C, total, width), g1=v(BF16, Z, X, C, total, width),
        q_s=v(BF16, 2, rows, width), k_s=v(BF16, 2, rows, width), v_s=v(BF16, 2, rows, width),
        p_s=v(BF16, HEADS, rows, rows), c_s=v(BF16, 2, rows, width), cl_s=v(BF16, 2, rows, width),
        xh1=v(F32, 2, rows, width), rst=v(F32, 2, rows, 2), n1=v(BF16, 2, rows, width),
        f_s=v(BF16, rows, inner), gp=v(BF16, rows, inner),
        xh2=v(F32, 2, rows, width), y_s=v(F32, rows, width),
        h_s=v(BF16, 3, rows, width), oc=v(BF16, rows, width), gin1=v(BF16, rows, width),
        mask_s=v(BF16, 2, rows, 128), g_s=v(F32, rows, width), go=v(BF16, rows, width),
        gh_s=v(BF16, 2, rows, width), ds_s=v(BF16, 2, rows, rows), gqkv=v(BF16, rows, 3 * width), xt=v(BF16, width, rows),
        cols=v(F32, rows, 8), vec=v(F32, 2, 8, width), bff=v(F32, 2, 1, inner),
        sems=pltpu.SemaphoreType.DMA((6,)),
    )
    if grid:
        late, columns = (late_parts(kind) * rp for kind in ((OWN, OTHER), (X_OWN, X_OTHER)))
        kg, kr = len(GATHER) + 1, len(REDUCE) + 1
        dma = pltpu.SemaphoreType.DMA
        scratch |= dict(
            dvec=v(F32, 2, 8, width), dbff=v(F32, 2, 1, inner), dhw=v(F32, 1, width), dhb=v(F32, 1, 1),
            wsm=v(F32, 2, Z, X, C, 16, 128), gsm=v(F32, 2, Z, X, C, 16, 128),
            r1s=v(F32, 2, Z, X, 16, 128), rxs=v(F32, 2, Z, 16, 128), rzs=v(F32, 2, Z, 16, 128),
            rys=v(F32, 16, 128),
            r1=v(BF16, Z, X, total, width), ry=v(BF16, Z, X, late, width), rcol=v(BF16, Z, columns, width),
            rx=v(BF16, 2, Z, total, width), rz=v(BF16, 2, Z, total, width), rf=v(BF16, total, width),
            wft=v(F32, 4 * rp, width), own_sems=pltpu.SemaphoreType.DMA((9,)), own=v(BF16, total, width), own_small=v(F32, 16, 128),
            gs=dma((2, kg, 8)), gr=dma((2, kg, 8)), ss=dma((2, kr, 8)), sr=dma((2, kr, 8)), sum_s=v(F32, max(n for _, n in REDUCE) * rp, width),
            os=dma((3,)), orr=dma((3,)), credit=pltpu.SemaphoreType.REGULAR((kr,)),
        )
    names = list(ins) + list(outs) + list(scratch)
    params = dict(vmem_limit_bytes=VMEM_BYTES)
    if grid:
        params |= dict(collective_id=0, has_side_effects=True)
    call = pl.pallas_call(
        functools.partial(kernel, names, grid),
        out_shape=tuple(t[0] for t in outs.values()),
        in_specs=list(ins.values()),
        out_specs=tuple(t[1] for t in outs.values()),
        scratch_shapes=list(scratch.values()),
        compiler_params=pltpu.CompilerParams(**params),
    )
    return call, list(outs)


def hand_over(act, gin, term, wq, wo, wi, wf, small, act_o, gin_o, term_o, wq_o, wo_o, wi_o, wf_o, vec_o, bff_o, hw_o,
              hb_o, sems):
    moves = [pltpu.make_async_copy(a, b, sems.at[i]) for i, (a, b) in enumerate(
        ((act, act_o.at[0]), (gin, gin_o.at[0]), (wq, wq_o), (wo, wo_o), (wi, wi_o), (wf, wf_o)))]
    for m in moves:
        m.start()
    rows, heads = term.shape[2], hw_o.shape[0] // 128
    for i in range(term.shape[0]):
        term_o[i * rows : (i + 1) * rows] = term[i, 0].astype(BF16)
    vec_o[0] = small[0:8, 0 : vec_o.shape[2]]
    bff_o[...] = small[8:9, 0 : bff_o.shape[1]]
    for i in range(heads):
        hw_o[i * 128 : (i + 1) * 128] = small[9 + i, :]
    hb_o[...] = small[9 + heads, 0:1]
    for m in moves:
        m.wait()


def fused_local(grid, tokens_in, out_cot, term_cot, long_flag, token_mask, w_qkv, w_out, w_ff_in, w_ff_out, vectors,
                ff_bias, head_weight, head_bias):
    section = lax.axis_index("section")
    width = tokens_in.shape[1]
    micro = long_flag.shape[0]
    rows = tokens_in.shape[0] // micro
    call, names = make_call(rows, width, w_ff_in.shape[2], vectors.shape[2], ff_bias.shape[1], grid)
    res = types.SimpleNamespace(**dict(zip(names, call(long_flag, head_bias, tokens_in, out_cot, term_cot, token_mask,
                                                      head_weight, w_qkv, w_out, w_ff_in, w_ff_out, vectors, ff_bias))))
    vm, hbm = pl.BlockSpec(memory_space=pltpu.VMEM), pl.BlockSpec(memory_space=pl.ANY)
    f32 = lambda *t: jax.ShapeDtypeStruct(t, F32)
    b16 = lambda *t: jax.ShapeDtypeStruct(t, BF16)
    both = b16(1, micro * rows, width)
    acts, gins, *rest = pl.pallas_call(
        hand_over,
        out_shape=(both, both, b16(micro * rows), f32(*w_qkv.shape), f32(*w_out.shape), f32(*w_ff_in.shape),
                   f32(*w_ff_out.shape), f32(*vectors.shape), f32(*ff_bias.shape), f32(width), f32(1)),
        in_specs=[hbm, hbm, vm, hbm, hbm, hbm, hbm, vm],
        out_specs=(vm,) * 11,
        scratch_shapes=[pltpu.SemaphoreType.DMA((6,))],
    )(res.act_out, res.gin_out, res.term, res.d_wq, res.d_wo, res.d_wi, res.d_wf, res.d_small)
    return (acts, rest[0], gins, *rest[1:])


def plain_local(tokens_in, out_cot, term_cot, long_flag, token_mask, w_qkv, w_out, w_ff_in, w_ff_out, vectors, ff_bias,
                head_weight, head_bias):
    section = lax.axis_index("section")
    width = tokens_in.shape[1]
    micro = long_flag.shape[0]
    rows = tokens_in.shape[0] // micro
    inner = w_ff_in.shape[2]
    everyone = lambda a, ax: lax.all_gather(lax.all_gather(a, "dp", axis=ax, tiled=True), "section", axis=0, tiled=True)
    wq, wo, wi, wf = (everyone(a, 1) for a in (w_qkv, w_out, w_ff_in, w_ff_out))
    vec = everyone(vectors, 2).astype(F32)
    bff = everyone(ff_bias, 1).astype(F32)[:, None]
    cut = lambda a: a.reshape(2, width, -1, width).transpose(0, 2, 1, 3).reshape(2, -1, width)
    wall = jnp.concatenate([cut(wq), wo, cut(wi), wf], 1)[:, None, None, None]
    call, names = make_call(rows, width, inner, width, inner, None)
    res = types.SimpleNamespace(**dict(zip(names, call(long_flag, head_bias, tokens_in, out_cot, term_cot, token_mask,
                                                      head_weight, wall, vec, bff))))
    swap = lambda a: lax.all_gather(a, "section", axis=1, tiled=True)[section][None]
    terms = lax.all_gather(res.term[0], "section", axis=0, tiled=True).astype(BF16)

    def scatter(a, ax):
        a = lax.psum_scatter(a.astype(F32), "section", scatter_dimension=0, tiled=True)
        return lax.psum_scatter(a, "dp", scatter_dimension=ax, tiled=True)

    g = res.g_out[:, 0, 0, 0]
    glue = lambda a, n: a.reshape(2, n, width, width).transpose(0, 2, 1, 3).reshape(2, width, n * width)
    turned = lambda a: a.reshape(2, -1, 128, width // 128, 128).transpose(0, 1, 4, 3, 2).reshape(2, -1, width)
    dhw, dhb = lax.psum((res.dhw[0], res.dhb[0]), ("section", "dp"))
    return (
        swap(res.act_out), terms, swap(res.gin_out),
        scatter(glue(g[:, : 3 * width], 3), 1), scatter(g[:, 3 * width : 4 * width], 1),
        scatter(glue(g[:, 4 * width : 8 * width], 4), 1), scatter(turned(g[:, 8 * width :]), 1),
        scatter(res.dvec, 2), scatter(res.dbff[:, 0], 1), dhw, dhb,
    )


def solution(mesh):
    dp = mesh.shape["dp"]
    if dp == 16:
        local = functools.partial(fused_local, (4, 2, 2))
    else:
        local = plain_local
    shard = P("section", "dp", None)
    in_specs = (P("dp", None), P("dp", None), P("dp"), P("dp"), P("dp"), shard, shard, shard, shard,
                P("section", None, "dp"), P("section", "dp"), P(), P())
    out_specs = (shard, P("dp"), shard, shard, shard, shard, shard, P("section", None, "dp"), P("section", "dp"),
                 P(), P())
    return jax.shard_map(local, mesh=mesh, in_specs=in_specs, out_specs=out_specs, check_vma=False)
```
